32 devices in a mesh: dp: 8 (over y, x, core), tensor: 4 (over z).
Axes of the slice: x: 2, y: 2, z: 4, core: 2. Of those that a mesh axis runs over, the one named last changes fastest.
Arguments:
- block_in: bfloat16 [2, 8, 1024, 1280], P(None, 'dp', 'tensor'), may hold values from -6 to 6
- out_grad: float32 [2, 8, 1024, 1280], P(None, 'dp', 'tensor'), may hold values from -6 to 6
- global_pos: int32 [2, 8, 64], P(None, 'dp'), may hold values from 0 to 1023, as said below
- w_query: bfloat16 [1280, 1280], P('dp', 'tensor'), may hold values from -0.15625 to 0.15625
- w_key: bfloat16 [1280, 1280], P('dp', 'tensor'), may hold values from -0.15625 to 0.15625
- w_value: bfloat16 [1280, 1280], P('dp', 'tensor'), may hold values from -0.15625 to 0.15625
- w_out: bfloat16 [1280, 1280], P('dp', 'tensor'), may hold values from -0.15625 to 0.15625
- w_up: bfloat16 [1280, 5120], P('dp', 'tensor'), may hold values from -0.15625 to 0.15625
- w_gate: bfloat16 [1280, 5120], P('dp', 'tensor'), may hold values from -0.15625 to 0.15625
- w_down: bfloat16 [1280, 5120], P('dp', 'tensor'), may hold values from -0.078125 to 0.078125
- qk_gain: float32 [1280], P('tensor'), may hold values from 0.8 to 1.6
- up_gain: float32 [5120], P('tensor'), may hold values from 0.5 to 1.5
- gate_gain: float32 [5120], P('tensor'), may hold values from 0.5 to 1.5
- att_rate: float32 [1280], replicated, may hold values from 0.2 to 0.8
- mlp_rate: float32 [1280], replicated, may hold values from 0.2 to 0.8
Outputs:
- block_out: float32 [2, 8, 1024, 1280], P(None, 'dp', 'tensor')
- in_grad: float32 [2, 8, 1024, 1280], P(None, 'dp', 'tensor')
- grad_query: float32 [1280, 1280], P('dp', 'tensor')
- grad_key: float32 [1280, 1280], P('dp', 'tensor')
- grad_value: float32 [1280, 1280], P('dp', 'tensor')
- grad_out: float32 [1280, 1280], P('dp', 'tensor')
- grad_up: float32 [1280, 5120], P('dp', 'tensor')
- grad_gate: float32 [1280, 5120], P('dp', 'tensor')
- grad_down: float32 [1280, 5120], P('dp', 'tensor')
- grad_qk_gain: float32 [1280], P('tensor')
- grad_up_gain: float32 [5120], P('tensor')
- grad_gate_gain: float32 [5120], P('tensor')
- grad_att_rate: float32 [1280], replicated
- grad_mlp_rate: float32 [1280], replicated
The draws below stay inside these ranges and needn't reach their ends.
Inputs may be any that keep to these rules, and one draw needn't show every extreme that they name: `global_pos`: each row holds 64 distinct positions of its sequence.
All inputs are finite; a program needn't handle non-finite values.
Results may differ from the reference program's by a relative error of at most 0.023.
Values may be sent and summed in bfloat16 or wider, within the bound.
No kernel may reach another device: no remote copies, remote signals or barrier semaphores. Data moves between devices by JAX's collectives and lax.ppermute only.
A program may use at most 256 MiB of HBM per device.

```python
import math
import jax
import jax.numpy as jnp
from jax import lax

D = 1280
HEADS = 20
HD = 64
FF = 5120
SEQ = 1024
WINDOW = 512
NGLOB = 64
MB = 2
BATCH = 8
N_TENSOR = 4


def draw_global_pos(key, part):
    key = jax.random.fold_in(key, 11)
    streams = jax.random.split(key, MB * BATCH)
    chosen = jax.vmap(lambda stream: jax.random.permutation(stream, SEQ)[:NGLOB])(streams)
    return chosen.reshape(MB, BATCH, NGLOB).astype(jnp.int32)


def steps_of(rng, shape, cuts, least, top_value):
    def one(position, blocks):
        draws = jax.random.uniform(jax.random.fold_in(jax.random.fold_in(rng, 6), position), (blocks,), jnp.float32, least / len(cuts), top_value / len(cuts))
        return jnp.repeat(jnp.exp(draws), shape[position] // blocks).reshape((-1,) + (1,) * (len(shape) - position - 1))

    level = one(*cuts[0])
    for cut in cuts[1:]:
        level = level * one(*cut)
    return level


def normal_values(rng, extent, deviation, limit, pieces=(), kind=jnp.bfloat16):
    drawn = deviation * jax.random.normal(rng, extent, jnp.float32)
    if pieces:
        drawn = drawn * steps_of(rng, extent, pieces, -0.22, 0.18)
    return jnp.clip(drawn, -limit, limit).astype(kind)


def setup_inputs(seed: int = 0) -> dict:
    keys = jax.random.split(jax.random.key(seed), 16)
    return {
        "block_in": normal_values(keys[0], (MB, BATCH, SEQ, D), 1.0, 6.0, ((1, 8), (2, 4))),
        "out_grad": normal_values(keys[1], (MB, BATCH, SEQ, D), 1.0, 6.0, ((1, 8), (2, 4)), jnp.float32),
        "global_pos": draw_global_pos(jax.random.fold_in(keys[15], 71), 0),
        "w_query": normal_values(keys[3], (D, D), D ** -0.5, 0.15625, ((0, 8), (1, 4))),
        "w_key": normal_values(keys[4], (D, D), D ** -0.5, 0.15625, ((0, 8), (1, 4))),
        "w_value": normal_values(keys[5], (D, D), D ** -0.5, 0.15625, ((0, 8), (1, 4))),
        "w_out": normal_values(keys[6], (D, D), D ** -0.5, 0.15625, ((0, 8), (1, 4))),
        "w_up": normal_values(keys[7], (D, FF), D ** -0.5, 0.15625, ((0, 8), (1, 4))),
        "w_gate": normal_values(keys[8], (D, FF), D ** -0.5, 0.15625, ((0, 8), (1, 4))),
        "w_down": normal_values(keys[9], (D, FF), FF ** -0.5, 0.078125, ((0, 8), (1, 4))),
        "qk_gain": jnp.clip(0.8 + 0.8 * jax.random.uniform(keys[10], (D,), jnp.float32) ** steps_of(keys[10], (D,), ((0, 4),), -0.2, 0.2), 0.8, 1.6),
        "up_gain": jnp.clip(0.5 + 1.0 * jax.random.uniform(keys[11], (FF,), jnp.float32) ** steps_of(keys[11], (FF,), ((0, 4),), -0.2, 0.2), 0.5, 1.5),
        "gate_gain": jnp.clip(0.5 + 1.0 * jax.random.uniform(keys[12], (FF,), jnp.float32) ** steps_of(keys[12], (FF,), ((0, 4),), -0.2, 0.2), 0.5, 1.5),
        "att_rate": jnp.clip(jax.random.uniform(keys[13], (D,), jnp.float32, 0.2, 0.8), 0.2, 0.8),
        "mlp_rate": jnp.clip(jax.random.uniform(keys[14], (D,), jnp.float32, 0.2, 0.8), 0.2, 0.8),
    }


epsilon = 1e-06
highest = lax.Precision.HIGHEST

@jax.custom_vjp
def low(v):
    return lax.optimization_barrier(v.astype(jnp.bfloat16)).astype(jnp.float32)

@jax.custom_vjp
def low_back(v):
    return v

def low_keep(v):
    return (low(v), None)

def low_pass(kept, grad):
    return (grad,)

def back_keep(v):
    return (v, None)

def back_low(kept, grad):
    return (low(grad),)
low.defvjp(low_keep, low_pass)
low_back.defvjp(back_keep, back_low)

def row_norm(values):
    return values * lax.rsqrt(lax.optimization_barrier(jnp.mean(values * values, axis=-1, keepdims=True)) + epsilon)

def head_norm(values, gain):
    shaped = values.reshape(values.shape[0], HEADS, HD)
    normed = shaped * lax.rsqrt(lax.optimization_barrier(jnp.mean(shaped * shaped, axis=-1, keepdims=True)) + epsilon)
    return normed.reshape(values.shape[0], HEADS * HD) * gain

def settle(base, branch, rate):
    return row_norm(base + rate * (row_norm(branch) - base))

def swish_gate(up_raw, gate_raw, up_gain, gate_gain):
    lifted = gate_gain * gate_raw
    return up_gain * up_raw * (lifted * jax.nn.sigmoid(lifted))

def allowed(places):
    row_ids = jnp.arange(SEQ, dtype=jnp.int32)
    global_flags = jnp.any(places[:, None] == row_ids[None, :], axis=0)
    in_window = row_ids[:, None] - row_ids[None, :] < WINDOW
    causal = row_ids[None, :] <= row_ids[:, None]
    return causal & (in_window | global_flags[:, None] | global_flags[None, :])

def grouped(rows, weights):
    width = weights[0].shape[1] // N_TENSOR
    results = [[] for member in weights]
    for group in range(N_TENSOR):
        piece = low_back(rows)
        for which, weight in enumerate(weights):
            results[which].append(jnp.dot(piece, weight[:, group * width:(group + 1) * width], precision=highest))
    return tuple((jnp.concatenate(parts, axis=1) for parts in results))

def split_sum(left, weight):
    width = weight.shape[1] // N_TENSOR
    total = jnp.zeros((left.shape[0], weight.shape[0]), jnp.float32)
    for group in range(N_TENSOR):
        columns = slice(group * width, (group + 1) * width)
        total = total + low(jnp.dot(left[:, columns], weight[:, columns].T, precision=highest))
    return total

def forward(params, tokens, places):
    w_query, w_key, w_value, w_out, w_up, w_gate, w_down, qk_gain, up_gain, gate_gain, att_rate, mlp_rate = params
    rows_in = low(tokens)
    query_raw, key_raw, value_raw = grouped(rows_in, (w_query, w_key, w_value))
    query_raw = low_back(query_raw)
    key_raw = low_back(key_raw)
    value_raw = low_back(value_raw)
    queries = low(head_norm(query_raw, qk_gain)).reshape(SEQ, HEADS, HD)
    key_rows = low(head_norm(key_raw, qk_gain)).reshape(SEQ, HEADS, HD)
    value_rows = low(value_raw).reshape(SEQ, HEADS, HD)
    scores = jnp.einsum('qhd,khd->hqk', queries, key_rows, precision=highest) / math.sqrt(HD)
    scores = low_back(scores)
    masked = jnp.where(allowed(places)[None], scores, -1e+30)
    row_peak = lax.optimization_barrier(jnp.max(masked, axis=-1, keepdims=True))
    raised = jnp.exp(masked - row_peak)
    probs = raised / lax.optimization_barrier(jnp.sum(raised, axis=-1, keepdims=True))
    mixed = jnp.einsum('hqk,khd->qhd', low(probs), value_rows, precision=highest).reshape(SEQ, D)
    mixed = low(low_back(mixed))
    att_branch = low_back(split_sum(mixed, w_out))
    hidden_one = settle(tokens, att_branch, att_rate)
    hidden_low = low(hidden_one)
    up_raw, gate_raw = grouped(hidden_low, (w_up, w_gate))
    up_raw = low_back(up_raw)
    gate_raw = low_back(gate_raw)
    activated = low(swish_gate(up_raw, gate_raw, up_gain, gate_gain))
    mlp_branch = low_back(split_sum(activated, w_down))
    return settle(hidden_one, mlp_branch, mlp_rate)

def reference(block_in, out_grad, global_pos, w_query, w_key, w_value, w_out, w_up, w_gate, w_down, qk_gain, up_gain, gate_gain, att_rate, mlp_rate):
    params = tuple((member.astype(jnp.float32) for member in (w_query, w_key, w_value, w_out, w_up, w_gate, w_down, qk_gain, up_gain, gate_gain, att_rate, mlp_rate)))
    sequences = MB * BATCH
    inputs = block_in.reshape(sequences, SEQ, D).astype(jnp.float32)
    cotangents = out_grad.reshape(sequences, SEQ, D).astype(jnp.float32)
    positions = global_pos.reshape(sequences, NGLOB).astype(jnp.int32)
    initial = jax.tree.map(jnp.zeros_like, params)

    def one_sequence(totals, sample):
        tokens, cotangent, places = sample
        result, pullback = jax.vjp(lambda weights, values: forward(weights, values, places), params, tokens)
        gradients, token_grad = pullback(cotangent)
        return (jax.tree.map(jnp.add, totals, gradients), (result, token_grad))
    totals, (outputs, input_grads) = lax.scan(one_sequence, initial, (inputs, cotangents, positions))
    full_shape = (MB, BATCH, SEQ, D)
    return (outputs.reshape(full_shape), input_grads.reshape(full_shape), totals[0], totals[1], totals[2], totals[3], totals[4], totals[5], totals[6], totals[7], totals[8], totals[9], totals[10], totals[11])
```

```python
import math

import jax
import jax.numpy as jnp
from jax import lax
from jax.experimental import pallas as pl
from jax.experimental.pallas import tpu as pltpu
from jax.sharding import Mesh, PartitionSpec as P

HD = 64
WINDOW = 512
CHIPS = 4
LANES = 128
HALF = 64
EXTRA = 32
BLOCK = 256
VMEM_LIMIT = 48 * 2**20

DP = ("outer", "chip", "core")
ALL = DP + ("tensor",)

epsilon = 1e-06
blocked = -1e30
low = jnp.bfloat16
wide = jnp.float32


def swap(value, bit):
    count = lax.axis_size(DP)
    return lax.ppermute(value, DP, [(i, i ^ bit) for i in range(count)])


def pick(flag, when_true, when_false):
    return jnp.where(flag, when_true, when_false)


def outer_gather(value):
    me = lax.axis_index(DP)
    bit = 8
    while bit < lax.axis_size(DP):
        other = swap(value, bit)
        upper = (me & bit) != 0
        value = pick(
            upper, jnp.concatenate([other, value]), jnp.concatenate([value, other])
        )
        bit *= 2
    return value


def outer_scatter(value):
    me = lax.axis_index(DP)
    bit = lax.axis_size(DP) // 2
    while bit >= 8:
        rows = value.shape[0] // 2
        upper = (me & bit) != 0
        keep = pick(upper, value[rows:], value[:rows])
        send = pick(upper, value[:rows], value[rows:])
        value = (keep.astype(wide) + swap(send, bit).astype(wide)).astype(value.dtype)
        bit //= 2
    return value


def full_rows(value):
    outer = lax.axis_size(DP) // 8
    count, rows, columns = value.shape
    if outer > 1:
        value = value.reshape(count, outer, rows // outer, columns).transpose(1, 0, 2, 3)
    return value.reshape(count * rows, columns)


def plane_rows(value):
    outer = lax.axis_size(DP) // 8
    total, columns = value.shape
    if outer > 1:
        value = value.reshape(outer, 8, total // 8 // outer, columns).transpose(1, 0, 2, 3)
    return value.reshape(8, total // 8, columns)


def plane_first(value):
    return value, swap(value, 2), swap(value, 4)


def plane_second(first):
    value, along_x, along_y = first
    half = value.shape[0] // 2
    return value, along_x, along_y, swap(along_y[:half], 2), swap(along_x[half:], 4)


def scatter_first(blocks):
    own, along_x, along_y, diagonal = blocks
    half = own.shape[0] // 2
    first = swap(jnp.concatenate([along_x[:half], diagonal[:half]]), 2)
    second = swap(jnp.concatenate([along_y[half:], diagonal[half:]]), 4)
    return blocks, first, second


def scatter_second(sent):
    (own, along_x, along_y, _), first, second = sent
    half = own.shape[0] // 2
    next_y = (along_y[:half].astype(wide) + first[half:].astype(wide)).astype(low)
    next_x = (along_x[half:].astype(wide) + second[half:].astype(wide)).astype(low)
    top = own[:half].astype(wide) + first[:half].astype(wide) + swap(next_y, 4).astype(wide)
    bottom = own[half:].astype(wide) + second[:half].astype(wide) + swap(next_x, 2).astype(wide)
    return jnp.concatenate([top, bottom])


def row_norm(values):
    return values * lax.rsqrt(jnp.mean(values * values, axis=-1, keepdims=True) + epsilon)


def settle(base, branch, rate):
    return row_norm(base + rate * (row_norm(branch) - base))


def nt(left, right):
    return lax.dot_general(left, right, (((1,), (1,)), ((), ())), preferred_element_type=wide)


def nn(left, right):
    return lax.dot_general(left, right, (((1,), (0,)), ((), ())), preferred_element_type=wide)


def tn(left, right):
    return lax.dot_general(left, right, (((0,), (0,)), ((), ())), preferred_element_type=wide)


def params():
    return pltpu.CompilerParams(vmem_limit_bytes=VMEM_LIMIT)


def cost(flops, moved):
    return pl.CostEstimate(flops=int(flops), bytes_accessed=int(moved), transcendentals=0)


def head_means(width):
    rows = lax.broadcasted_iota(jnp.int32, (width, width), 0) // HD
    columns = lax.broadcasted_iota(jnp.int32, (width, width), 1) // HD
    return jnp.where(rows == columns, 1.0 / HD, 0.0).astype(low)


def head_scale(raw, means):
    return lax.rsqrt(nn((raw * raw).astype(low), means) + epsilon)


def project_heads(rows, weight, gain):
    n, depth = rows.shape
    width = weight.shape[1]
    tile = 2 * LANES
    block = 256

    def kernel(rows_ref, weight_ref, gain_ref, out_ref, raw_ref):
        means = head_means(tile)
        for start in range(0, n, block):
            span = slice(start, start + block)
            raw = nn(rows_ref[span, :], weight_ref[...])
            raw_ref[span, :] = raw.astype(low)
            out_ref[span, :] = (raw * head_scale(raw, means) * gain_ref[...]).astype(low)

    out = pl.BlockSpec((n, tile), lambda j: (0, j))
    return pl.pallas_call(
        kernel,
        grid=(width // tile,),
        in_specs=[
            pl.BlockSpec((n, depth), lambda j: (0, 0)),
            pl.BlockSpec((depth, tile), lambda j: (0, j)),
            pl.BlockSpec((1, tile), lambda j: (0, j)),
        ],
        out_specs=[out, out],
        out_shape=[jax.ShapeDtypeStruct((n, width), low)] * 2,
        compiler_params=params(),
        cost_estimate=cost(2 * n * depth * width, 2 * (n * depth + depth * width + 2 * n * width)),
    )(rows, weight, gain[None])


def fill_bias(bias, flag_row, flag_col):
    @pl.when(pl.program_id(0) == 0)
    def _():
        for i in range(bias.shape[0] // BLOCK):
            for j in range(i + 1):
                keys = slice(j * BLOCK, (j + 1) * BLOCK)
                rows = slice(i * BLOCK, (i + 1) * BLOCK)
                key_ids = j * BLOCK + lax.broadcasted_iota(jnp.int32, (BLOCK, BLOCK), 0)
                row_ids = i * BLOCK + lax.broadcasted_iota(jnp.int32, (BLOCK, BLOCK), 1)
                flagged = jnp.maximum(flag_row[:, rows], flag_col[keys, :]) > 0.5
                allow = (key_ids <= row_ids) & ((row_ids - key_ids < WINDOW) | flagged)
                bias[keys, rows] = jnp.where(allow, 0.0, blocked)


def head_lanes(value, head):
    lane = lax.broadcasted_iota(jnp.int32, value.shape, 1)
    mine = (lane < HD) if head == 0 else (lane >= HD)
    return jnp.where(mine, value, jnp.zeros_like(value))


def flag_specs(seq_len):
    return [pl.BlockSpec((1, seq_len), lambda h: (0, 0)), pl.BlockSpec((seq_len, 1), lambda h: (0, 0))]


def attend_forward(heads, value_rows, flag_row, flag_col):
    seq_len, width = value_rows.shape
    pairs = width // LANES

    def kernel(q_ref, k_ref, v_ref, row_ref, col_ref, out_ref, lse_ref, bias, turned):
        fill_bias(bias, row_ref, col_ref)
        turned[...] = v_ref[...].astype(wide).T.astype(low)
        for i in range(seq_len // BLOCK):
            rows = slice(i * BLOCK, (i + 1) * BLOCK)
            reach = (i + 1) * BLOCK
            block = q_ref[rows, :] * jnp.asarray(1.0 / math.sqrt(HD), low)
            halves = []
            for head in range(2):
                scores = nt(k_ref[:reach, :], head_lanes(block, head)) + bias[:reach, rows]
                raised = jnp.exp(scores)
                total = jnp.sum(raised, axis=0, keepdims=True)
                mixed = nn(turned[head * HD : (head + 1) * HD, :reach], raised.astype(low))
                halves.append(mixed / total)
                lse_ref[0, head : head + 1, rows] = jnp.log(total)
            out_ref[rows, :] = jnp.concatenate(halves, axis=0).T.astype(low)

    block = pl.BlockSpec((seq_len, LANES), lambda h: (0, h))
    keys = pl.BlockSpec((seq_len, LANES), lambda h: (0, pairs + h))
    return pl.pallas_call(
        kernel,
        grid=(pairs,),
        in_specs=[block, keys, block] + flag_specs(seq_len),
        out_specs=[block, pl.BlockSpec((1, 8, seq_len), lambda h: (h, 0, 0))],
        out_shape=[
            jax.ShapeDtypeStruct((seq_len, width), low),
            jax.ShapeDtypeStruct((pairs, 8, seq_len), wide),
        ],
        scratch_shapes=[pltpu.VMEM((seq_len, seq_len), wide), pltpu.VMEM((LANES, seq_len), low)],
        compiler_params=params(),
        cost_estimate=cost(16 * seq_len * seq_len * width, 10 * seq_len * width),
    )(heads, heads, value_rows, flag_row, flag_col)


def attend_backward(heads, raw, value_rows, mixed, mixed_grad, lse, gain, flag_row, flag_col):
    seq_len, width = value_rows.shape
    pairs = width // LANES
    scale = 1.0 / math.sqrt(HD)

    def unnorm(grad, raw_block, gain_row, means):
        raw_block = raw_block.astype(wide)
        factor = head_scale(raw_block, means)
        normed = raw_block * factor
        term = jnp.sum(grad * normed, axis=0, keepdims=True)
        grad = grad * gain_row
        inner = nn((grad * normed).astype(low), means)
        return (factor * (grad - normed * inner)).astype(low), term

    def kernel(
        q_ref, k_ref, v_ref, qraw_ref, kraw_ref, m_ref, g_ref, lse_ref, gain_ref, row_ref, col_ref,
        heads_ref, dv_ref, term_ref, bias, turned, key_total, value_total, dq_ref, dk_ref, sems,
    ):
        step = pl.program_id(0)

        def stores(pair):
            return [
                pltpu.make_async_copy(
                    ref, heads_ref.at[:, pl.ds(pl.multiple_of((side * pairs + pair) * LANES, LANES), LANES)], sems.at[side]
                )
                for side, ref in enumerate((dq_ref, dk_ref))
            ]

        @pl.when(step > 0)
        def _():
            for store in stores(step - 1):
                store.wait()

        fill_bias(bias, row_ref, col_ref)
        turned[...] = k_ref[...].astype(wide).T.astype(low)
        means = head_means(LANES)
        gain_row = gain_ref[...]
        query_term = key_term = jnp.zeros((1, LANES), wide)
        count = seq_len // BLOCK
        for i in reversed(range(count)):
            rows = slice(i * BLOCK, (i + 1) * BLOCK)
            reach = (i + 1) * BLOCK
            block = q_ref[rows, :] * jnp.asarray(scale, low)
            grads = g_ref[rows, :]
            products = (grads.astype(wide) * m_ref[rows, :].astype(wide)).T
            halves = []
            key_parts = value_parts = None
            for head in range(2):
                inner = jnp.sum(products[head * HD : (head + 1) * HD], axis=0, keepdims=True)
                query = head_lanes(block, head)
                grad = head_lanes(grads, head)
                scores = nt(k_ref[:reach, :], query) + bias[:reach, rows]
                probs = jnp.exp(scores - lse_ref[0, head : head + 1, rows])
                prob_grad = nt(v_ref[:reach, :], grad)
                score_grad = (probs * (prob_grad - inner)).astype(low)
                halves.append(nn(turned[head * HD : (head + 1) * HD, :reach], score_grad))
                key_part = nn(score_grad, query)
                value_part = nn(probs.astype(low), grad)
                key_parts = key_part if key_parts is None else key_parts + key_part
                value_parts = value_part if value_parts is None else value_parts + value_part
            if i == count - 1:
                key_total[...] = key_parts
                value_total[...] = value_parts
            else:
                key_total[:reach, :] += key_parts
                value_total[:reach, :] += value_parts
            query_grad = jnp.concatenate(halves, axis=0).T * scale
            dq_ref[rows, :], term = unnorm(query_grad, qraw_ref[rows, :], gain_row, means)
            query_term = query_term + term
        dv_ref[...] = value_total[...].astype(low)
        for i in range(count):
            rows = slice(i * BLOCK, (i + 1) * BLOCK)
            dk_ref[rows, :], term = unnorm(key_total[rows, :], kraw_ref[rows, :], gain_row, means)
            key_term = key_term + term
        term_ref[...] = jnp.concatenate([query_term, key_term, jnp.zeros((6, LANES), wide)], axis=0)
        for store in stores(step):
            store.start()

        @pl.when(step == pairs - 1)
        def _():
            for store in stores(step):
                store.wait()

    block = pl.BlockSpec((seq_len, LANES), lambda h: (0, h))
    keys = pl.BlockSpec((seq_len, LANES), lambda h: (0, pairs + h))
    return pl.pallas_call(
        kernel,
        grid=(pairs,),
        in_specs=[block, keys, block, block, keys, block, block]
        + [pl.BlockSpec((1, 8, seq_len), lambda h: (h, 0, 0)), pl.BlockSpec((1, LANES), lambda h: (0, h))]
        + flag_specs(seq_len),
        out_specs=[pl.BlockSpec(memory_space=pl.ANY), block, pl.BlockSpec((8, LANES), lambda h: (0, h))],
        out_shape=[
            jax.ShapeDtypeStruct((seq_len, 2 * width), low),
            jax.ShapeDtypeStruct((seq_len, width), low),
            jax.ShapeDtypeStruct((8, width), wide),
        ],
        scratch_shapes=[
            pltpu.VMEM((seq_len, seq_len), wide),
            pltpu.VMEM((LANES, seq_len), low),
            pltpu.VMEM((seq_len, LANES), wide),
            pltpu.VMEM((seq_len, LANES), wide),
            pltpu.VMEM((seq_len, LANES), low),
            pltpu.VMEM((seq_len, LANES), low),
            pltpu.SemaphoreType.DMA((2,)),
        ],
        compiler_params=params(),
        cost_estimate=cost(32 * seq_len * seq_len * width, 20 * seq_len * width),
    )(heads, heads, value_rows, raw, raw, mixed, mixed_grad, lse, gain[None], flag_row, flag_col)


def sum_back(lefts, rights, n=None, first=0):
    n = n or lefts[0][0].shape[0]
    out_width = rights[0][0].shape[0]
    block = 256
    count = len(lefts)
    skip = first * n // block

    def kernel(*refs):
        total = nt(refs[0][...], refs[count][...])
        for i in range(1, count):
            total = total + nt(refs[i][...], refs[count + i][...])
        refs[2 * count][...] = total.astype(low)

    depth = sum(columns for _, _, columns in lefts)
    return pl.pallas_call(
        kernel,
        grid=(n // block,),
        in_specs=[
            pl.BlockSpec((block, columns), lambda r, at=at: (r + skip, at)) for _, at, columns in lefts
        ]
        + [pl.BlockSpec((out_width, columns), lambda r, at=at: (0, at)) for _, at, columns in rights],
        out_specs=pl.BlockSpec((block, out_width), lambda r: (r, 0)),
        out_shape=jax.ShapeDtypeStruct((n, out_width), low),
        compiler_params=params(),
        cost_estimate=cost(2 * n * out_width * depth, 2 * (n + out_width) * depth + 2 * n * out_width),
    )(*(matrix for matrix, _, _ in lefts + rights))


def rows_product(pairs):
    n, depth = pairs[0][0].shape
    width = pairs[0][1].shape[1]
    tile = 2 * LANES
    steps = depth // tile
    count = len(pairs)

    def kernel(*refs):
        for k in range(count):

            @pl.when(pl.program_id(0) // steps == k)
            def _():
                refs[2 * count][...] = tn(refs[2 * k][...], refs[2 * k + 1][...]).astype(low)

    def left_tile(k):
        return lambda j: (0, jnp.clip(j - k * steps, 0, steps - 1))

    specs = []
    for k in range(count):
        specs += [pl.BlockSpec((n, tile), left_tile(k)), pl.BlockSpec((n, width), lambda j: (0, 0))]
    return pl.pallas_call(
        kernel,
        grid=(count * steps,),
        in_specs=specs,
        out_specs=pl.BlockSpec((tile, width), lambda j: (j % steps, j // steps)),
        out_shape=jax.ShapeDtypeStruct((depth, count * width), low),
        compiler_params=params(),
        cost_estimate=cost(2 * n * depth * width * count, 2 * count * (n * (depth + width) + depth * width)),
    )(*(member for pair in pairs for member in pair))


def chunk_specs(blocks, width):
    return [pl.BlockSpec(block.shape, lambda j: (0, 0)) for block in blocks]


def mlp_forward(blocks, up_w, gate_w, scales, chunk, earlier):
    n = sum(block.shape[0] for block in blocks)
    depth, units = up_w.shape
    tile = 2 * LANES
    span = 512
    count = len(blocks)

    def kernel(*refs):
        ins, rest = refs[:count], refs[count:]
        up_ref, gate_ref, scale_ref = rest[:3]
        mid_ref, up_out, gate_out, act_out = rest[-4:]

        @pl.when(pl.program_id(0) == 0)
        def _():
            at = 0
            for ref in ins:
                mid_ref[at : at + ref.shape[0], :] = ref[...]
                at += ref.shape[0]

        for start in range(0, n, span):
            rows = slice(start, start + span)
            left = mid_ref[rows, :]
            up = nn(left, up_ref[...])
            gate = nn(left, gate_ref[...])
            lifted = scale_ref[1:2, :] * gate
            up_out[rows, :] = up.astype(low)
            gate_out[rows, :] = gate.astype(low)
            act_out[rows, :] = (scale_ref[0:1, :] * up * (lifted * jax.nn.sigmoid(lifted))).astype(low)

    weight = pl.BlockSpec((depth, tile), lambda j: (0, j))
    whole = pl.BlockSpec((n, depth), lambda j: (chunk, 0))
    tiles = pl.BlockSpec((n, tile), lambda j: (chunk, j))
    big = jax.ShapeDtypeStruct((2 * n, depth), low)
    wide_units = jax.ShapeDtypeStruct((2 * n, units), low)
    return pl.pallas_call(
        kernel,
        grid=(units // tile,),
        in_specs=chunk_specs(blocks, depth)
        + [weight] * 2
        + [pl.BlockSpec((2, tile), lambda j: (0, j))]
        + [pl.BlockSpec(memory_space=pl.ANY)] * len(earlier),
        out_specs=[whole, tiles, tiles, tiles],
        out_shape=[big, wide_units, wide_units, wide_units],
        input_output_aliases={count + 3 + i: i for i in range(len(earlier))},
        compiler_params=params(),
        cost_estimate=cost(4 * n * depth * units, 2 * (2 * n * depth + 2 * depth * units + 3 * n * units)),
    )(*blocks, up_w, gate_w, scales, *earlier)


def mlp_backward(blocks, up_w, gate_w, down_w, scales, up_raw, gate_raw, chunk, earlier):
    n = sum(block.shape[0] for block in blocks)
    depth, units = up_w.shape
    tile = 2 * LANES
    span = 512
    count = len(blocks)
    steps = units // tile

    def kernel(*refs):
        ins, rest = refs[:count], refs[count:]
        down_ref, scale_ref, up_raw_ref, gate_raw_ref, up_ref, gate_ref = rest[:6]
        branch_ref, up_out, gate_out, part_ref, gain_ref, kept, weights, sems = rest[-8:]
        step = pl.program_id(0)
        fetches = [
            pltpu.make_async_copy(ref, weights.at[i], sems.at[i]) for i, ref in enumerate((up_ref, gate_ref))
        ]

        @pl.when(step == 0)
        def _():
            for fetch in fetches:
                fetch.start()
            at = 0
            for ref in ins:
                branch_ref[at : at + ref.shape[0], :] = ref[...]
                at += ref.shape[0]

        up_gain, gate_gain = scale_ref[0:1, :], scale_ref[1:2, :]
        up_term = gate_term = jnp.zeros((1, tile), wide)
        for start in range(0, n, span):
            rows = slice(start, start + span)
            grad = nn(branch_ref[rows, :], down_ref[...])
            up = up_raw_ref[rows, :].astype(wide)
            gate = gate_raw_ref[rows, :].astype(wide)
            lifted = gate_gain * gate
            slope = jax.nn.sigmoid(lifted)
            swished = lifted * slope
            up_part = grad * swished
            lifted_grad = grad * up * (up_gain * (slope + swished * (1.0 - slope)))
            up_term = up_term + jnp.sum(up_part * up, axis=0, keepdims=True)
            gate_term = gate_term + jnp.sum(lifted_grad * gate, axis=0, keepdims=True)
            up_low = (up_part * up_gain).astype(low)
            gate_low = (lifted_grad * gate_gain).astype(low)
            up_out[rows, :] = up_low
            gate_out[rows, :] = gate_low
            kept[0, step, rows, :] = up_low
            kept[1, step, rows, :] = gate_low
        gain_ref[...] = jnp.concatenate([up_term, gate_term, jnp.zeros((6, tile), wide)], axis=0)

        @pl.when(step == steps - 1)
        def _():
            for fetch in fetches:
                fetch.wait()
            for start in range(0, n, span):
                rows = slice(start, start + span)
                ups, gates = (
                    jnp.concatenate([kept[i, k, rows, :] for k in range(steps)], axis=1) for i in range(2)
                )
                for at in range(0, depth, tile):
                    part = nt(ups, weights[0, at : at + tile, :]) + nt(gates, weights[1, at : at + tile, :])
                    part_ref[rows, at : at + tile] = part.astype(low)

    weight = pl.BlockSpec((depth, tile), lambda j: (0, j))
    anywhere = pl.BlockSpec(memory_space=pl.ANY)
    whole = pl.BlockSpec((n, depth), lambda j: (chunk, 0))
    tiles = pl.BlockSpec((n, tile), lambda j: (chunk, j))
    big = jax.ShapeDtypeStruct((2 * n, depth), low)
    wide_units = jax.ShapeDtypeStruct((2 * n, units), low)
    return pl.pallas_call(
        kernel,
        grid=(steps,),
        in_specs=chunk_specs(blocks, depth)
        + [weight, pl.BlockSpec((2, tile), lambda j: (0, j)), tiles, tiles, anywhere, anywhere]
        + [anywhere] * len(earlier),
        out_specs=[
            whole, tiles, tiles,
            pl.BlockSpec((n, depth), lambda j: (0, 0)), pl.BlockSpec((8, tile), lambda j: (0, j)),
        ],
        out_shape=[
            big, wide_units, wide_units,
            jax.ShapeDtypeStruct((n, depth), low), jax.ShapeDtypeStruct((8, units), wide),
        ],
        scratch_shapes=[
            pltpu.VMEM((2, steps, n, tile), low), pltpu.VMEM((2, depth, units), low),
            pltpu.SemaphoreType.DMA((2,)),
        ],
        input_output_aliases={count + 6 + i: i for i in range(len(earlier))},
        compiler_params=params(),
        cost_estimate=cost(6 * n * depth * units, 2 * (2 * n * depth + 3 * depth * units + 4 * n * units)),
    )(*blocks, down_w, scales, up_raw, gate_raw, up_w, gate_w, *earlier)


def dot(left, right):
    return jnp.dot(left, right, preferred_element_type=wide)


def dot_rows(left, right):
    return tn(left, right).astype(low)


def place(blocks, indices):
    ndim = min(block.ndim for block in blocks)
    n = len(indices)
    count = len(blocks)
    pieces = [
        (i, at) for i, block in enumerate(blocks) for at in ([None] if block.ndim == ndim else range(block.shape[0]))
    ]
    shape = blocks[-1].shape[-ndim:]
    where_to = jnp.stack([jnp.asarray(i, jnp.int32) for i in indices])

    def kernel(index_ref, *refs):
        out, sems = refs[count], refs[count + 1]
        copies = []
        for k, (i, at) in enumerate(pieces):
            source = refs[i] if at is None else refs[i].at[at]
            copies.append(pltpu.make_async_copy(source, out.at[index_ref[k]], sems.at[k]))
        for copy in copies:
            copy.start()
        for copy in copies:
            copy.wait()

    anywhere = pl.BlockSpec(memory_space=pl.ANY)
    out = jax.ShapeDtypeStruct((n,) + shape, blocks[0].dtype)
    return pl.pallas_call(
        kernel,
        in_specs=[pl.BlockSpec(memory_space=pltpu.SMEM)] + [anywhere] * count,
        out_specs=pl.BlockSpec(memory_space=pltpu.VMEM),
        out_shape=out,
        scratch_shapes=[pltpu.SemaphoreType.DMA((n,))],
        compiler_params=params(),
        cost_estimate=cost(0, 2 * out.size * out.dtype.itemsize),
    )(where_to, *blocks)


def half_tiles(first, second, first_upper, second_upper):
    first, second = first.astype(wide), second.astype(wide)
    axis = first.ndim - 1
    first = jnp.where(first_upper, pltpu.roll(first, HALF, axis), first)
    second = jnp.where(second_upper, second, pltpu.roll(second, HALF, axis))
    lane = lax.broadcasted_iota(jnp.int32, first.shape, axis)
    return jnp.where(lane < HALF, first, second).astype(low)


def unit_pack(weights):
    rows, units = weights[0].shape
    main = units // CHIPS // LANES * LANES
    n = len(weights)

    def kernel(*refs):
        out = refs[n]
        target = pl.program_id(0)
        for i in range(n):
            start = pl.multiple_of(target * main, LANES)
            out[0, :, i * main : (i + 1) * main] = refs[i][:, pl.ds(start, main)]
        tile = pl.multiple_of(CHIPS * main + (target // 2) * LANES, LANES)
        upper = (target & 1) == 1
        rests = [refs[i][:, pl.ds(tile, LANES)] for i in range(n)]
        out[0, :, n * main :] = half_tiles(rests[0], rests[-1], upper, upper)

    whole = pl.BlockSpec((rows, units), lambda k: (0, 0))
    return pl.pallas_call(
        kernel,
        grid=(CHIPS,),
        in_specs=[whole] * n,
        out_specs=pl.BlockSpec((1, rows, n * main + LANES), lambda k: (k, 0, 0)),
        out_shape=jax.ShapeDtypeStruct((CHIPS, rows, n * main + LANES), weights[0].dtype),
    )(*weights)


def unit_lay(n, mine, theirs, core):
    count, _, rows, columns = mine.shape
    main = (columns - LANES) // n
    units = count * main + count // 2 * LANES

    def kernel(core_ref, *refs):
        outs = refs[2:]
        for side in range(2):
            slot = core_ref[0] ^ side
            blocks = refs[side]
            for i in range(n):
                for k in range(count):
                    outs[i][slot, :, k * main : (k + 1) * main] = blocks[k, 0, :, i * main : (i + 1) * main]
                tile = n * main
                upper = i == 1
                for k in range(0, count, 2):
                    at = count * main + k // 2 * LANES
                    outs[i][slot, :, at : at + LANES] = half_tiles(
                        blocks[k, 0, :, tile : tile + LANES],
                        blocks[k + 1, 0, :, tile : tile + LANES],
                        upper,
                        upper,
                    )

    block = pl.BlockSpec((count, 1, rows, columns), lambda q: (0, q, 0, 0))
    out = pl.BlockSpec((2, rows, units), lambda q: (q, 0, 0))
    return pl.pallas_call(
        kernel,
        grid=(CHIPS,),
        in_specs=[pl.BlockSpec(memory_space=pltpu.SMEM)] + [block] * 2,
        out_specs=[out] * n,
        out_shape=[jax.ShapeDtypeStruct((2 * CHIPS, rows, units), low)] * n,
        compiler_params=params(),
        cost_estimate=cost(0, 14 * n * 8 * rows * units // 4),
    )(core.reshape(1), mine, theirs)


def unit_unlay(grads, core):
    count = lax.axis_size("tensor")
    _, rows, units = grads[0].shape
    n = len(grads)
    main = units // count // LANES * LANES
    columns = n * main + (n + 1) // 2 * LANES

    def kernel(core_ref, *refs):
        for side in range(2):
            slot = core_ref[0] ^ side
            out = refs[n + side]
            for k in range(count):
                for i in range(n):
                    out[k, 0, :, i * main : (i + 1) * main] = refs[i][slot, :, k * main : (k + 1) * main]
                at = count * main + k // 2 * LANES
                upper = k % 2 == 1
                rests = [refs[i][slot, :, at : at + LANES] for i in range(n)]
                for i in range(0, n, 2):
                    to = n * main + i // 2 * LANES
                    out[k, 0, :, to : to + LANES] = half_tiles(
                        rests[i], rests[min(i + 1, n - 1)], upper, upper
                    )

    block = pl.BlockSpec((2, rows, units), lambda q: (q, 0, 0))
    return pl.pallas_call(
        kernel,
        grid=(CHIPS,),
        in_specs=[pl.BlockSpec(memory_space=pltpu.SMEM)] + [block] * n,
        out_specs=[pl.BlockSpec((count, 1, rows, columns), lambda q: (0, q, 0, 0))] * 2,
        out_shape=[jax.ShapeDtypeStruct((count, CHIPS, rows, columns), low)] * 2,
        compiler_params=params(),
        cost_estimate=cost(0, 14 * n * 8 * rows * units // 4),
    )(core.reshape(1), *grads)


def unit_unpack(n, blocks):
    _, rows, columns = blocks.shape
    main = (columns - (n + 1) // 2 * LANES) // n
    units = CHIPS * main + CHIPS // 2 * LANES

    def kernel(block_ref, *outs):
        for i in range(n):
            for j in range(CHIPS):
                outs[i][:, j * main : (j + 1) * main] = block_ref[j, :, i * main : (i + 1) * main].astype(wide)
            tile = n * main + i // 2 * LANES
            upper = i % 2 == 1
            for j in range(0, CHIPS, 2):
                at = CHIPS * main + j // 2 * LANES
                outs[i][:, at : at + LANES] = half_tiles(
                    block_ref[j, :, tile : tile + LANES], block_ref[j + 1, :, tile : tile + LANES], upper, upper
                ).astype(wide)

    return pl.pallas_call(
        kernel,
        out_shape=[jax.ShapeDtypeStruct((rows, units), wide)] * n,
        compiler_params=params(),
    )(blocks)


def per_device(
    block_in, out_grad, global_pos,
    w_query, w_key, w_value, w_out, w_up, w_gate, w_down,
    qk_gain, up_gain, gate_gain, att_rate, mlp_rate,
):
    count = lax.axis_size("tensor")
    plane = lax.axis_size(DP)
    micro_count, _, local_rows, model_width = block_in.shape
    assert micro_count == 2 and count == 4
    seq_len = local_rows * count
    head_width = w_query.shape[1]
    core_heads = head_width * 2
    unit_width = w_up.shape[1]
    plane_unit = unit_width // CHIPS
    main = plane_unit // LANES * LANES
    rest = plane_unit - main
    me = lax.axis_index(DP)
    z = lax.axis_index("tensor")
    core = me & 1
    chip = (me >> 1) & 3
    early = z < 2

    def across(value, pairs):
        return lax.ppermute(
            value, ALL, [(a * count + b, c * count + d) for (a, b), (c, d) in pairs]
        )

    def home(far):
        return [
            ((p, t), ((p & ~1) | (t & 1), ((t & 2) ^ (2 if far else 0)) | (p & 1)))
            for p in range(plane)
            for t in range(count)
        ]

    def seq_near(value):
        return across(lax.dynamic_index_in_dim(value, z >> 1, 0, keepdims=False), home(False))

    def seq_far(value):
        return across(lax.dynamic_index_in_dim(value, 1 - (z >> 1), 0, keepdims=False), home(True))

    def seq_join(near, far):
        return pick(early, near, far), pick(early, far, near)

    def from_sequence(first, second):
        near = across(pick(early, first, second), [(b, a) for a, b in home(False)])
        far = across(pick(early, second, first), [(b, a) for a, b in home(True)])
        return pick(early, jnp.stack([near, far]), jnp.stack([far, near]))

    def both_cores(first, second):
        return place(
            [first, second, swap(first, 1), swap(second, 1)], [core, core + 2, 1 - core, 3 - core]
        ).reshape(seq_len, model_width)

    def core_scatter(partial):
        split = partial.reshape(2, 2, local_rows, model_width)
        got = swap(lax.dynamic_index_in_dim(split, 1 - core, 1, keepdims=False), 1)
        mine = lax.dynamic_index_in_dim(split, core, 1, keepdims=False)
        return tuple(mine[i].astype(wide) + got[i].astype(wide) for i in range(2))

    def head_pairs(other_core, second):
        return [
            ((p ^ other_core, (t + 2 * (p & 1) + second) % count), (p, t))
            for p in range(plane)
            for t in range(count)
        ]

    def paired(a, b):
        return jnp.concatenate(
            [a[:, :head_width], b[:, :head_width], a[:, head_width:], b[:, head_width:]], axis=1
        )

    def attn_fetch(first, second):
        packed = outer_gather(jnp.concatenate([first, second], axis=1))
        groups = [[across(packed, head_pairs(side, which)) for which in range(2)] for side in range(2)]
        return jnp.stack([paired(*group) for group in groups])

    def attn_first(sides):
        return sides, swap(sides, 2), swap(sides, 4)

    def attn_second(first):
        sides, along_x, along_y = first
        return sides, along_x, along_y, swap(along_y[0], 2), swap(along_x[1], 4)

    def attn_lay(gathered):
        sides, along_x, along_y, d_own, d_other = gathered
        return full_rows(
            place(
                [sides, along_x, along_y, d_own, d_other],
                [2 * (chip ^ (i // 2)) + (core ^ (i % 2)) for i in range(8)],
            )
        )

    def attn_spread(packed, extra):
        columns = packed.shape[1]
        by_chip = plane_rows(packed).reshape(CHIPS, -1, columns)
        pieces = []
        for k in range(CHIPS):
            block = lax.dynamic_index_in_dim(by_chip, chip ^ k, 0, keepdims=False)
            pieces.append(jnp.concatenate([block, extra.astype(low)]))
        return scatter_second(scatter_first(pieces)).astype(low)

    def attn_scatter(spread):
        rows = (spread.shape[0] - EXTRA) // 2
        cores = spread[: 2 * rows].reshape(2, rows, -1)
        got = []
        for other_core in range(2):
            side = lax.dynamic_index_in_dim(cores, core ^ other_core, 0, keepdims=False)
            side = jnp.concatenate([side, spread[2 * rows :]])
            for which in range(2):
                at = which * head_width
                piece = jnp.concatenate(
                    [side[:, at : at + head_width], side[:, core_heads + at : core_heads + at + head_width]],
                    axis=1,
                )
                pairs = [(b, a) for a, b in head_pairs(other_core, which)]
                got.append(across(piece, pairs).astype(wide))
        grads = outer_scatter(sum(piece[:rows] for piece in got))
        small = jnp.stack([piece[rows:] for piece in got])
        total = jnp.zeros(small.shape[1:], wide)
        for t in range(count):
            back = (z - t) % count
            index = 2 * ((back >> 1) ^ core) + (back & 1)
            total = total + lax.dynamic_index_in_dim(small, index, 0, keepdims=False)
        bit = 8
        while bit < plane:
            total = total + swap(total, bit)
            bit *= 2
        return grads[:, :head_width], grads[:, head_width:], total

    def unit_send(weights):
        packed = unit_pack([outer_gather(w) for w in weights])
        return lax.all_to_all(packed, "chip", 0, 0, tiled=True)

    def unit_join(n, mine):
        return [full_rows(w) for w in unit_lay(n, mine, swap(mine, 1), core)]

    def unit_collect(grads):
        keep, send = unit_unlay([plane_rows(g) for g in grads], core)
        return (keep.astype(wide) + swap(send, 1).astype(wide)).astype(low)

    def unit_return(n, total):
        return [outer_scatter(g) for g in unit_unpack(n, lax.all_to_all(total, "chip", 0, 0, tiled=True))]

    tie = lax.optimization_barrier

    def shifted(value, step):
        return lax.ppermute(value, "tensor", [((i + step) % count, i) for i in range(count)])

    qk_sides = attn_fetch(w_query, w_key)
    far = seq_far(block_in[:, 0])
    ug_laid = unit_send([w_up, w_gate])
    down_laid = unit_send([w_down])
    qk_sides, ug_laid, block_in, qk_gain, global_pos = tie((qk_sides, ug_laid, block_in, qk_gain, global_pos))
    qk_first = attn_first(qk_sides)
    near = seq_near(block_in[:, 0])
    mains = lax.dynamic_slice_in_dim(jnp.stack([up_gain, gate_gain]), chip * main, main, 1)
    rests = lax.dynamic_slice_in_dim(jnp.stack([up_gain, gate_gain]), CHIPS * main + chip * rest, rest, 1)
    gains = jnp.concatenate([jnp.concatenate([mains, rests], axis=1).reshape(1, -1), qk_gain[None]], axis=1)
    gains = [gains] + [shifted(gains, k) for k in range(1, count)]
    places_here = global_pos[:, 0]
    places_there = swap(places_here, 1)
    qk_first, near, far, w_value, w_out, gains, places_there = tie(
        (qk_first, near, far, w_value, w_out, gains, places_there)
    )
    vo_sides = attn_fetch(w_value, w_out)
    qk_gathered = attn_second(qk_first)
    tokens = seq_join(near, far)
    sequence = both_cores(*tokens)
    vo_sides, qk_gathered, sequence, ug_laid, down_laid, gains = tie(
        (vo_sides, qk_gathered, sequence, ug_laid, down_laid, gains)
    )
    ug_shifted = lax.all_gather(ug_laid, "tensor")
    down_shifted = lax.all_gather(down_laid, "tensor")
    vo_first = attn_first(vo_sides)
    qk_w = attn_lay(qk_gathered)
    gains = jnp.concatenate(gains)
    gains = lax.dynamic_slice_in_dim(jnp.concatenate([gains, gains]), count - z, count, 0)
    unit_gains = gains[:, : 2 * plane_unit].reshape(count, 2, plane_unit).transpose(1, 0, 2)
    scales = jnp.concatenate(
        [unit_gains[..., :main].reshape(2, -1), unit_gains[..., main:].reshape(2, -1)], axis=1
    )
    head_gain = gains[:, 2 * plane_unit :]
    head_gain = lax.dynamic_slice_in_dim(
        jnp.concatenate([head_gain, head_gain]), z + 2 * core, 2, 0
    ).reshape(core_heads)
    places = lax.dynamic_index_in_dim(
        pick((z & 1) == core, places_here, places_there), z >> 1, 0, keepdims=False
    )
    flags = jnp.any(places[:, None] == jnp.arange(seq_len, dtype=jnp.int32)[None, :], axis=0).astype(wide)
    flag_row, flag_col = flags[None], flags[:, None]

    heads, raw = project_heads(sequence, qk_w, jnp.concatenate([head_gain, head_gain]))
    vo_w = attn_lay(attn_second(vo_first))
    value_w, out_w = vo_w[:, :core_heads], vo_w[:, core_heads:]
    value_rows = dot(sequence, value_w).astype(low)
    mixed, lse = attend_forward(heads, value_rows, flag_row, flag_col)
    att_branch = core_scatter(sum_back([(mixed, 0, core_heads)], [(vo_w, 1, core_heads)]))
    hidden, att_pull = zip(
        *(jax.vjp(settle, tokens[i].astype(wide), att_branch[i], att_rate) for i in range(2))
    )

    first_mid = plane_first(hidden[0].astype(low))
    first_mid, second_hidden = tie((first_mid, hidden[1]))
    mids = [plane_second(first_mid), plane_second(plane_first(second_hidden.astype(low)))]
    up_w, gate_w = unit_join(2, ug_shifted)
    laid = ()
    for i in range(2):
        laid = mlp_forward(mids[i], up_w, gate_w, scales, i, laid)
    laid, out_grad, down_shifted = tie((laid, out_grad, down_shifted))
    mid, up_raw, gate_raw, activated = laid
    units, chunk_rows = activated.shape[1], CHIPS * local_rows
    cotangent = seq_join(seq_near(out_grad[:, 0].astype(low)), seq_far(out_grad[:, 0].astype(low)))
    (down_w,) = unit_join(1, down_shifted)

    def by_chip(value):
        return [value[k * local_rows : (k + 1) * local_rows] for k in range(CHIPS)]

    def back(i):
        return sum_back([(activated, 0, units)], [(down_w, 0, units)], chunk_rows, i)

    def turn(i, sent):
        rows, pull = jax.vjp(settle, hidden[i], scatter_second(sent), mlp_rate)
        direct, branch_grad, term = pull(cotangent[i].astype(wide))
        return rows, direct, term, plane_first(branch_grad.astype(low))

    sent = scatter_first(by_chip(back(0)))
    sent, second_part = tie((sent, back(1)))
    second_sent = scatter_first(by_chip(second_part))
    rows_a, direct_a, term_a, first_a = turn(0, sent)
    rows_b, direct_b, term_b, first_b = turn(1, second_sent)

    branch_a = plane_second(first_a)
    branch_a, first_b = tie((branch_a, first_b))
    branch_b = plane_second(first_b)
    weights = (up_w, gate_w, down_w, scales, up_raw, gate_raw)
    *laid, part, unit_term_a = mlp_backward(branch_a, *weights, 0, ())
    sent = scatter_first(by_chip(part))
    laid, rows_a, rows_b = tie((laid, rows_a, rows_b))
    *laid, part, unit_term_b = mlp_backward(branch_b, *weights, 1, laid)
    block_out = from_sequence(rows_a.astype(low), rows_b.astype(low)).astype(wide)
    branch, up_low, gate_low = laid
    sent, part = tie((sent, part))
    second_sent = scatter_first(by_chip(part))
    down_grad = dot_rows(branch, activated)
    sent, second_sent, down_grad, mid = tie((sent, second_sent, down_grad, mid))
    hidden_total = [direct_a + scatter_second(sent), direct_b + scatter_second(second_sent)]
    up_w_grad, gate_w_grad = dot_rows(mid, up_low), dot_rows(mid, gate_low)
    input_direct, att_grad, att_rate_terms = zip(*(att_pull[i](hidden_total[i]) for i in range(2)))
    att_low = both_cores(*(grad.astype(low) for grad in att_grad))
    unit_blocks = unit_collect([up_w_grad, gate_w_grad, down_grad])
    att_low, unit_blocks = tie((att_low, unit_blocks))
    units_back = lax.psum_scatter(unit_blocks, "tensor", scatter_dimension=0)
    mixed_grad = dot(att_low, out_w).astype(low)
    heads_low, vraw_low, head_terms = attend_backward(
        heads, raw, value_rows, mixed, mixed_grad, lse, head_gain, flag_row, flag_col
    )
    in_part = sum_back(
        [(heads_low, 0, 2 * core_heads), (vraw_low, 0, core_heads)],
        [(qk_w, 0, 2 * core_heads), (vo_w, 0, core_heads)],
    )
    in_rows = [input_direct[i] + part for i, part in enumerate(core_scatter(in_part))]
    in_grad = from_sequence(*(rows.astype(low) for rows in in_rows)).astype(wide)
    unit_terms = [unit_term_a[:2], unit_term_b[:2]]
    mlp_rate_terms = [term_a, term_b]

    small = jnp.concatenate(
        [
            unit_terms[0] + unit_terms[1],
            (att_rate_terms[0] + att_rate_terms[1])[None],
            (mlp_rate_terms[0] + mlp_rate_terms[1])[None],
        ]
    )
    small = small + swap(small, 1)
    unit_rows = jnp.concatenate(
        [small[:2, : count * main].reshape(2, count, main), small[:2, count * main :].reshape(2, count, rest)],
        axis=2,
    )
    unit_rows = lax.dynamic_slice_in_dim(
        jnp.concatenate([unit_rows, unit_rows], axis=1), z + 2 * core, 2, 1
    ).reshape(1, 4 * plane_unit)
    rate_rows = jnp.broadcast_to(small[2:].reshape(4, 2, 1, head_width), (4, 2, 2, head_width))
    rate_rows = rate_rows.reshape(1, 4, 4 * head_width)
    own_chip = jnp.arange(CHIPS)[:, None] == chip
    vo_extra = jnp.concatenate(
        [
            jnp.where(own_chip, unit_rows, 0.0),
            jnp.where(own_chip[..., None], rate_rows, 0.0).reshape(4 * CHIPS, -1),
            jnp.zeros((EXTRA - 5 * CHIPS, 4 * head_width), wide),
        ]
    )
    qk_extra = jnp.concatenate(
        [
            jnp.where(own_chip, head_terms[:2].reshape(1, 4 * head_width), 0.0),
            jnp.zeros((EXTRA - CHIPS, 4 * head_width), wide),
        ]
    )
    vo_spread = attn_spread(rows_product([(sequence, vraw_low), (att_low, mixed)]), vo_extra)
    qk_spread = attn_spread(dot_rows(sequence, heads_low), qk_extra)
    grad_value, grad_out, vo_small = attn_scatter(vo_spread)
    grad_query, grad_key, qk_small = attn_scatter(qk_spread)
    grad_up, grad_gate, grad_down = unit_return(3, units_back)

    units = vo_small[:CHIPS].reshape(CHIPS, 2, plane_unit).transpose(1, 0, 2)
    units = jnp.concatenate([units[..., :main].reshape(2, -1), units[..., main:].reshape(2, -1)], axis=1)
    rates = jnp.sum(vo_small[CHIPS : 5 * CHIPS].reshape(CHIPS, 2, model_width), axis=0)
    head_sums = jnp.sum(qk_small[:CHIPS], axis=0)
    grad_qk_gain = head_sums[:head_width] + head_sums[head_width:]
    return (
        block_out[:, None], in_grad[:, None],
        grad_query, grad_key, grad_value, grad_out, grad_up, grad_gate, grad_down,
        grad_qk_gain, units[0], units[1], rates[0], rates[1],
    )


def solution(mesh):
    shape = dict(mesh.shape)
    plane, count = shape["dp"], shape["tensor"]
    split = Mesh(mesh.devices.reshape(plane // 8, CHIPS, 2, count), ALL)
    tokens = P(None, DP, "tensor", None)
    matrix = P(DP, "tensor")
    in_specs = (tokens, tokens, P(None, DP, None)) + (matrix,) * 7 + (P("tensor"),) * 3 + (P(), P())
    out_specs = (tokens, tokens) + (matrix,) * 7 + (P("tensor"),) * 3 + (P(), P())
    return jax.shard_map(
        per_device, mesh=split, in_specs=in_specs, out_specs=out_specs, check_vma=False
    )
```

```python
import math

import jax
import jax.numpy as jnp
from jax import lax
from jax.experimental import pallas as pl
from jax.experimental.pallas import tpu as pltpu
from jax.sharding import Mesh, PartitionSpec as P

HD = 64
WINDOW = 512
CHIPS = 4
LANES = 128
HALF = 64
EXTRA = 32
BLOCK = 256
VMEM_LIMIT = 48 * 2**20

DP = ("outer", "chip", "core")
ALL = DP + ("tensor",)

epsilon = 1e-06
blocked = -1e30
low = jnp.bfloat16
wide = jnp.float32


def swap(value, bit):
    count = lax.axis_size(DP)
    return lax.ppermute(value, DP, [(i, i ^ bit) for i in range(count)])


def pick(flag, when_true, when_false):
    return jnp.where(flag, when_true, when_false)


def outer_gather(value):
    me = lax.axis_index(DP)
    bit = 8
    while bit < lax.axis_size(DP):
        other = swap(value, bit)
        upper = (me & bit) != 0
        value = pick(
            upper, jnp.concatenate([other, value]), jnp.concatenate([value, other])
        )
        bit *= 2
    return value


def outer_scatter(value):
    me = lax.axis_index(DP)
    bit = lax.axis_size(DP) // 2
    while bit >= 8:
        rows = value.shape[0] // 2
        upper = (me & bit) != 0
        keep = pick(upper, value[rows:], value[:rows])
        send = pick(upper, value[:rows], value[rows:])
        value = (keep.astype(wide) + swap(send, bit).astype(wide)).astype(value.dtype)
        bit //= 2
    return value


def full_rows(value):
    outer = lax.axis_size(DP) // 8
    count, rows, columns = value.shape
    if outer > 1:
        value = value.reshape(count, outer, rows // outer, columns).transpose(1, 0, 2, 3)
    return value.reshape(count * rows, columns)


def plane_rows(value):
    outer = lax.axis_size(DP) // 8
    total, columns = value.shape
    if outer > 1:
        value = value.reshape(outer, 8, total // 8 // outer, columns).transpose(1, 0, 2, 3)
    return value.reshape(8, total // 8, columns)


def plane_first(value):
    return value, swap(value, 2), swap(value, 4)


def plane_second(first):
    value, along_x, along_y = first
    half = value.shape[0] // 2
    return value, along_x, along_y, swap(along_y[:half], 2), swap(along_x[half:], 4)


def scatter_first(blocks, then=()):
    own, along_x, along_y, diagonal = blocks
    half = own.shape[0] // 2
    first, second, then = lax.optimization_barrier(
        (
            jnp.concatenate([along_x[:half], diagonal[:half]]),
            jnp.concatenate([along_y[half:], diagonal[half:]]),
            then,
        )
    )
    return (blocks, swap(first, 2), swap(second, 4)), then


def scatter_last(sent):
    (own, along_x, along_y, _), first, second = sent
    half = own.shape[0] // 2
    next_y = (along_y[:half].astype(wide) + first[half:].astype(wide)).astype(low)
    next_x = (along_x[half:].astype(wide) + second[half:].astype(wide)).astype(low)
    return own, first, second, swap(next_y, 4), swap(next_x, 2)


def scatter_second(sent):
    own, first, second, last_y, last_x = scatter_last(sent)
    half = own.shape[0] // 2
    top = own[:half].astype(wide) + first[:half].astype(wide) + last_y.astype(wide)
    bottom = own[half:].astype(wide) + second[:half].astype(wide) + last_x.astype(wide)
    return jnp.concatenate([top, bottom])


def nt(left, right):
    return lax.dot_general(left, right, (((1,), (1,)), ((), ())), preferred_element_type=wide)


def nn(left, right):
    return lax.dot_general(left, right, (((1,), (0,)), ((), ())), preferred_element_type=wide)


def tn(left, right):
    return lax.dot_general(left, right, (((0,), (0,)), ((), ())), preferred_element_type=wide)


def params():
    return pltpu.CompilerParams(vmem_limit_bytes=VMEM_LIMIT)


def cost(flops, moved):
    return pl.CostEstimate(flops=1, bytes_accessed=1, transcendentals=0)


def head_means(width):
    rows = lax.broadcasted_iota(jnp.int32, (width, width), 0) // HD
    columns = lax.broadcasted_iota(jnp.int32, (width, width), 1) // HD
    return jnp.where(rows == columns, 1.0 / HD, 0.0).astype(low)


def head_scale(raw, means):
    return lax.rsqrt(nn((raw * raw).astype(low), means) + epsilon)


def project_heads(rows, weight, gain):
    n, depth = rows.shape
    width = weight.shape[1]
    tile = 2 * LANES
    block = 512

    def kernel(rows_ref, weight_ref, gain_ref, out_ref, raw_ref):
        means = head_means(tile)
        for start in range(0, n, block):
            span = slice(start, start + block)
            raw = nn(rows_ref[span, :], weight_ref[...])
            raw_ref[span, :] = raw.astype(low)
            out_ref[span, :] = (raw * head_scale(raw, means) * gain_ref[...]).astype(low)

    out = pl.BlockSpec((n, tile), lambda j: (0, j))
    return pl.pallas_call(
        kernel,
        grid=(width // tile,),
        in_specs=[
            pl.BlockSpec((n, depth), lambda j: (0, 0)),
            pl.BlockSpec((depth, tile), lambda j: (0, j)),
            pl.BlockSpec((1, tile), lambda j: (0, j)),
        ],
        out_specs=[out, out],
        out_shape=[jax.ShapeDtypeStruct((n, width), low)] * 2,
        compiler_params=params(),
        cost_estimate=cost(2 * n * depth * width, 2 * (n * depth + depth * width + 2 * n * width)),
    )(rows, weight, gain[None])


def fill_bias(bias, flag_row, flag_col):
    @pl.when(pl.program_id(0) == 0)
    def _():
        for i in range(bias.shape[0] // BLOCK):
            for j in range(i + 1):
                keys = slice(j * BLOCK, (j + 1) * BLOCK)
                rows = slice(i * BLOCK, (i + 1) * BLOCK)
                key_ids = j * BLOCK + lax.broadcasted_iota(jnp.int32, (BLOCK, BLOCK), 0)
                row_ids = i * BLOCK + lax.broadcasted_iota(jnp.int32, (BLOCK, BLOCK), 1)
                flagged = jnp.maximum(flag_row[:, rows], flag_col[keys, :]) > 0.5
                allow = (key_ids <= row_ids) & ((row_ids - key_ids < WINDOW) | flagged)
                bias[keys, rows] = jnp.where(allow, 0.0, blocked)


def head_lanes(value, head):
    lane = lax.broadcasted_iota(jnp.int32, value.shape, 1)
    mine = (lane < HD) if head == 0 else (lane >= HD)
    return jnp.where(mine, value, jnp.zeros_like(value))


def flag_specs(seq_len):
    return [pl.BlockSpec((1, seq_len), lambda h: (0, 0)), pl.BlockSpec((seq_len, 1), lambda h: (0, 0))]


def attend_forward(heads, value_rows, flag_row, flag_col):
    seq_len, width = value_rows.shape
    pairs = width // LANES

    def kernel(q_ref, k_ref, v_ref, row_ref, col_ref, out_ref, lse_ref, bias, turned):
        fill_bias(bias, row_ref, col_ref)
        turned[...] = v_ref[...].astype(wide).T.astype(low)
        for i in range(seq_len // BLOCK):
            rows = slice(i * BLOCK, (i + 1) * BLOCK)
            reach = (i + 1) * BLOCK
            block = q_ref[rows, :] * jnp.asarray(1.0 / math.sqrt(HD), low)
            halves = []
            for head in range(2):
                scores = nt(k_ref[:reach, :], head_lanes(block, head)) + bias[:reach, rows]
                raised = jnp.exp(scores)
                total = jnp.sum(raised, axis=0, keepdims=True)
                mixed = nn(turned[head * HD : (head + 1) * HD, :reach], raised.astype(low))
                halves.append(mixed / total)
                lse_ref[0, head : head + 1, rows] = jnp.log(total)
            out_ref[rows, :] = jnp.concatenate(halves, axis=0).T.astype(low)

    block = pl.BlockSpec((seq_len, LANES), lambda h: (0, h))
    keys = pl.BlockSpec((seq_len, LANES), lambda h: (0, pairs + h))
    return pl.pallas_call(
        kernel,
        grid=(pairs,),
        in_specs=[block, keys, block] + flag_specs(seq_len),
        out_specs=[block, pl.BlockSpec((1, 8, seq_len), lambda h: (h, 0, 0))],
        out_shape=[
            jax.ShapeDtypeStruct((seq_len, width), low),
            jax.ShapeDtypeStruct((pairs, 8, seq_len), wide),
        ],
        scratch_shapes=[pltpu.VMEM((seq_len, seq_len), wide), pltpu.VMEM((LANES, seq_len), low)],
        compiler_params=params(),
        cost_estimate=cost(16 * seq_len * seq_len * width, 10 * seq_len * width),
    )(heads, heads, value_rows, flag_row, flag_col)


def attend_backward(heads, raw, value_rows, mixed, mixed_grad, lse, gain, flag_row, flag_col):
    seq_len, width = value_rows.shape
    pairs = width // LANES
    scale = 1.0 / math.sqrt(HD)

    def unnorm(grad, raw_block, gain_row, means):
        raw_block = raw_block.astype(wide)
        factor = head_scale(raw_block, means)
        normed = raw_block * factor
        term = jnp.sum(grad * normed, axis=0, keepdims=True)
        grad = grad * gain_row
        inner = nn((grad * normed).astype(low), means)
        return (factor * (grad - normed * inner)).astype(low), term

    def kernel(
        q_ref, k_ref, v_ref, qraw_ref, kraw_ref, m_ref, g_ref, lse_ref, gain_ref, row_ref, col_ref,
        heads_ref, dv_ref, term_ref, bias, turned, key_total, value_total, dq_ref, dk_ref, sems,
    ):
        step = pl.program_id(0)

        def stores(pair):
            return [
                pltpu.make_async_copy(
                    ref, heads_ref.at[:, pl.ds(pl.multiple_of((side * pairs + pair) * LANES, LANES), LANES)], sems.at[side]
                )
                for side, ref in enumerate((dq_ref, dk_ref))
            ]

        @pl.when(step > 0)
        def _():
            for store in stores(step - 1):
                store.wait()

        fill_bias(bias, row_ref, col_ref)
        turned[...] = k_ref[...].astype(wide).T.astype(low)
        means = head_means(LANES)
        gain_row = gain_ref[...]
        query_term = key_term = jnp.zeros((1, LANES), wide)
        count = seq_len // BLOCK
        for i in reversed(range(count)):
            rows = slice(i * BLOCK, (i + 1) * BLOCK)
            reach = (i + 1) * BLOCK
            block = q_ref[rows, :] * jnp.asarray(scale, low)
            grads = g_ref[rows, :]
            products = (grads.astype(wide) * m_ref[rows, :].astype(wide)).T
            halves = []
            key_parts = value_parts = None
            for head in range(2):
                inner = jnp.sum(products[head * HD : (head + 1) * HD], axis=0, keepdims=True)
                query = head_lanes(block, head)
                grad = head_lanes(grads, head)
                scores = nt(k_ref[:reach, :], query) + bias[:reach, rows]
                probs = jnp.exp(scores - lse_ref[0, head : head + 1, rows])
                prob_grad = nt(v_ref[:reach, :], grad)
                score_grad = (probs * (prob_grad - inner)).astype(low)
                halves.append(nn(turned[head * HD : (head + 1) * HD, :reach], score_grad))
                key_part = nn(score_grad, query)
                value_part = nn(probs.astype(low), grad)
                key_parts = key_part if key_parts is None else key_parts + key_part
                value_parts = value_part if value_parts is None else value_parts + value_part
            if i == count - 1:
                key_total[...] = key_parts
                value_total[...] = value_parts
            else:
                key_total[:reach, :] += key_parts
                value_total[:reach, :] += value_parts
            query_grad = jnp.concatenate(halves, axis=0).T * scale
            dq_ref[rows, :], term = unnorm(query_grad, qraw_ref[rows, :], gain_row, means)
            query_term = query_term + term
        dv_ref[...] = value_total[...].astype(low)
        for i in range(count):
            rows = slice(i * BLOCK, (i + 1) * BLOCK)
            dk_ref[rows, :], term = unnorm(key_total[rows, :], kraw_ref[rows, :], gain_row, means)
            key_term = key_term + term
        term_ref[...] = jnp.concatenate([query_term, key_term, jnp.zeros((6, LANES), wide)], axis=0)
        for store in stores(step):
            store.start()

        @pl.when(step == pairs - 1)
        def _():
            for store in stores(step):
                store.wait()

    block = pl.BlockSpec((seq_len, LANES), lambda h: (0, h))
    keys = pl.BlockSpec((seq_len, LANES), lambda h: (0, pairs + h))
    return pl.pallas_call(
        kernel,
        grid=(pairs,),
        in_specs=[block, keys, block, block, keys, block, block]
        + [pl.BlockSpec((1, 8, seq_len), lambda h: (h, 0, 0)), pl.BlockSpec((1, LANES), lambda h: (0, h))]
        + flag_specs(seq_len),
        out_specs=[pl.BlockSpec(memory_space=pl.ANY), block, pl.BlockSpec((8, LANES), lambda h: (0, h))],
        out_shape=[
            jax.ShapeDtypeStruct((seq_len, 2 * width), low),
            jax.ShapeDtypeStruct((seq_len, width), low),
            jax.ShapeDtypeStruct((8, width), wide),
        ],
        scratch_shapes=[
            pltpu.VMEM((seq_len, seq_len), wide),
            pltpu.VMEM((LANES, seq_len), low),
            pltpu.VMEM((seq_len, LANES), wide),
            pltpu.VMEM((seq_len, LANES), wide),
            pltpu.VMEM((seq_len, LANES), low),
            pltpu.VMEM((seq_len, LANES), low),
            pltpu.SemaphoreType.DMA((2,)),
        ],
        compiler_params=params(),
        cost_estimate=cost(32 * seq_len * seq_len * width, 20 * seq_len * width),
    )(heads, heads, value_rows, raw, raw, mixed, mixed_grad, lse, gain[None], flag_row, flag_col)


def sum_back(lefts, rights, n=None, first=0):
    n = n or lefts[0][0].shape[0]
    out_width = rights[0][0].shape[0]
    tile = 2 * LANES
    count = len(lefts)

    def kernel(*refs):
        total = nt(refs[0][...], refs[count][...])
        for i in range(1, count):
            total = total + nt(refs[i][...], refs[count + i][...])
        refs[2 * count][...] = total.astype(low)

    depth = sum(columns for _, _, columns in lefts)
    return pl.pallas_call(
        kernel,
        grid=(out_width // tile,),
        in_specs=[pl.BlockSpec((n, columns), lambda j, at=at: (first, at)) for _, at, columns in lefts]
        + [pl.BlockSpec((tile, columns), lambda j, at=at: (j, at)) for _, at, columns in rights],
        out_specs=pl.BlockSpec((n, tile), lambda j: (0, j)),
        out_shape=jax.ShapeDtypeStruct((n, out_width), low),
        compiler_params=params(),
        cost_estimate=cost(2 * n * out_width * depth, 2 * (n + out_width) * depth + 2 * n * out_width),
    )(*(matrix for matrix, _, _ in lefts + rights))


def add_low(first, second):
    columns = first.shape[-1]
    flat = (first.size // columns, columns)
    block = flat[0] // 8

    def kernel(a_ref, b_ref, out_ref):
        out_ref[...] = (a_ref[...].astype(wide) + b_ref[...].astype(wide)).astype(low)

    spec = pl.BlockSpec((block, columns), lambda r: (r, 0))
    out = pl.pallas_call(
        kernel,
        grid=(8,),
        in_specs=[spec, spec],
        out_specs=spec,
        out_shape=jax.ShapeDtypeStruct(flat, low),
        compiler_params=params(),
        cost_estimate=cost(first.size, 6 * first.size),
    )(first.reshape(flat), second.reshape(flat))
    return out.reshape(first.shape)


def rows_product(pairs, tile):
    n, depth = pairs[0][0].shape
    lefts = [left for left, _ in pairs]
    rights = [right for _, group in pairs for right in group]
    owner = [k for k, (_, group) in enumerate(pairs) for _ in group]
    steps = [right.shape[1] // tile for right in rights]
    starts = [sum(steps[:i]) for i in range(len(steps))]
    chunk = 256

    def kernel(*refs):
        left_refs, right_refs = refs[: len(lefts)], refs[len(lefts) : len(lefts) + len(rights)]
        out, turned = refs[-2:]
        step = pl.program_id(0)
        for i, right in enumerate(right_refs):
            if i == 0 or owner[i] != owner[i - 1]:

                @pl.when(step == starts[i])
                def _(left=left_refs[owner[i]]):
                    for at in range(0, n, chunk):
                        turned[:, at : at + chunk] = left[at : at + chunk, :].T

            @pl.when((step >= starts[i]) & (step < starts[i] + steps[i]))
            def _(right=right):
                out[...] = nn(turned[...], right[...]).astype(low)

    def tile_of(i):
        return lambda j: (0, jnp.clip(j - starts[i], 0, steps[i] - 1))

    width = sum(right.shape[1] for right in rights)
    return pl.pallas_call(
        kernel,
        grid=(sum(steps),),
        in_specs=[pl.BlockSpec((n, depth), lambda j: (0, 0))] * len(lefts)
        + [pl.BlockSpec((n, tile), tile_of(i)) for i in range(len(rights))],
        out_specs=pl.BlockSpec((depth, tile), lambda j: (0, j)),
        out_shape=jax.ShapeDtypeStruct((depth, width), low),
        scratch_shapes=[pltpu.VMEM((depth, n), low)],
        compiler_params=params(),
        cost_estimate=cost(2 * n * depth * width, 2 * (n * (depth + width) + depth * width)),
    )(*lefts, *rights)


def product(left, right, at):
    n, depth = left.shape
    width = right.shape[1] // 2

    def kernel(left_ref, right_ref, out_ref):
        out_ref[...] = nn(left_ref[...], right_ref[...]).astype(low)

    return pl.pallas_call(
        kernel,
        grid=(1,),
        in_specs=[pl.BlockSpec((n, depth), lambda j: (0, 0)), pl.BlockSpec((depth, width), lambda j: (0, at))],
        out_specs=pl.BlockSpec((n, width), lambda j: (0, 0)),
        out_shape=jax.ShapeDtypeStruct((n, width), low),
        compiler_params=params(),
        cost_estimate=cost(2 * n * depth * width, 2 * (n * depth + depth * width + n * width)),
    )(left, right)


def chunk_specs(blocks, width):
    return [pl.BlockSpec(block.shape, lambda j: (0, 0)) for block in blocks]


def row_scale(values):
    return lax.rsqrt(jnp.mean(values * values, axis=-1, keepdims=True) + epsilon)


def unscale(grad, normed, scale):
    return scale * (grad - normed * jnp.mean(grad * normed, axis=-1, keepdims=True))


def settle_step(base, branch, rate):
    branch_scale = row_scale(branch)
    normed = branch * branch_scale
    moved = base + rate * (normed - base)
    scale = row_scale(moved)
    return moved * scale, (normed, branch_scale, scale)


def settle_back(grad, result, base, rate, saved):
    normed, branch_scale, scale = saved
    grad = unscale(grad, result, scale)
    return grad * (1.0 - rate), unscale(grad * rate, normed, branch_scale), grad * (normed - base)


def rate_rows(terms):
    return jnp.concatenate([jnp.sum(terms, axis=0, keepdims=True), jnp.zeros((7, terms.shape[1]), wide)])


def settle_attention(partial, got, tokens, rate, core):
    _, _, n, depth = partial.shape
    block = n // 2

    def kernel(core_ref, part_ref, got_ref, token_ref, rate_ref, hidden_ref, low_ref, branch_ref):
        branch = part_ref[0, 0].astype(wide) + got_ref[0].astype(wide)
        hidden, _ = settle_step(token_ref[...].astype(wide), branch, rate_ref[...])
        hidden_ref[...] = hidden
        low_ref[...] = hidden.astype(low)
        branch_ref[...] = branch

    rows = pl.BlockSpec((block, depth), lambda j, r, core_ref: (2 * j + r, 0))
    return pl.pallas_call(
        kernel,
        grid_spec=pltpu.PrefetchScalarGridSpec(
            num_scalar_prefetch=1,
            grid=(2, 2),
            in_specs=[
                pl.BlockSpec((1, 1, block, depth), lambda j, r, core_ref: (j, core_ref[0], r, 0)),
                pl.BlockSpec((1, block, depth), lambda j, r, core_ref: (j, r, 0)),
                rows,
                pl.BlockSpec((1, depth), lambda j, r, core_ref: (0, 0)),
            ],
            out_specs=[rows] * 3,
        ),
        out_shape=[
            jax.ShapeDtypeStruct((2 * n, depth), wide),
            jax.ShapeDtypeStruct((2 * n, depth), low),
            jax.ShapeDtypeStruct((2 * n, depth), wide),
        ],
        compiler_params=params(),
        cost_estimate=cost(0, 0),
    )(core.reshape(1), partial, got, tokens, rate[None])


def arrived_specs(n, depth):
    half = n // 2
    piece = pl.BlockSpec((half, depth), lambda h, *_: (0, 0))
    return [pl.BlockSpec((half, depth), lambda h, *_: (h, 0))] + [piece] * 4


def arrived_sum(h, own, first, second, last_y, last_x):
    top, bottom = (a[...].astype(wide) + b[...].astype(wide) for a, b in ((first, last_y), (second, last_x)))
    return own[...].astype(wide) + jnp.where(h == 0, top, bottom)


def settle_units(arrived, hidden, near, far, early, rate):
    n, depth = hidden.shape
    half = n // 2

    def kernel(early_ref, *refs):
        h = pl.program_id(0)
        branch = arrived_sum(h, *refs[:5])
        hidden_ref, near_ref, far_ref, rate_ref, out_ref, direct_ref, grad_ref, term_ref = refs[5:]
        base, rates = hidden_ref[...], rate_ref[...]
        result, saved = settle_step(base, branch, rates)
        cotangent = jnp.where((h == 0) == (early_ref[0] == 1), near_ref[...], far_ref[...])
        direct, grad, terms = settle_back(cotangent.astype(wide), result, base, rates, saved)
        out_ref[...] = result.astype(low)
        direct_ref[...] = direct
        grad_ref[...] = grad.astype(low)

        @pl.when(h == 0)
        def _():
            term_ref[...] = rate_rows(terms)

        @pl.when(h != 0)
        def _():
            term_ref[...] += rate_rows(terms)

    rows = pl.BlockSpec((half, depth), lambda h, *_: (h, 0))
    piece = pl.BlockSpec((half, depth), lambda h, *_: (0, 0))
    return pl.pallas_call(
        kernel,
        grid_spec=pltpu.PrefetchScalarGridSpec(
            num_scalar_prefetch=1,
            grid=(2,),
            in_specs=arrived_specs(n, depth)
            + [rows, piece, piece, pl.BlockSpec((1, depth), lambda h, *_: (0, 0))],
            out_specs=[rows, rows, rows, pl.BlockSpec((8, depth), lambda h, *_: (0, 0))],
        ),
        out_shape=[
            jax.ShapeDtypeStruct((n, depth), low),
            jax.ShapeDtypeStruct((n, depth), wide),
            jax.ShapeDtypeStruct((n, depth), low),
            jax.ShapeDtypeStruct((8, depth), wide),
        ],
        compiler_params=params(),
        cost_estimate=cost(0, 0),
    )(early.astype(jnp.int32).reshape(1), *arrived, hidden, near, far, rate[None])


def settle_attention_back(arrived, direct, hidden, tokens, branch, rate):
    n, depth = hidden.shape
    half = n // 2

    def kernel(*refs):
        h = pl.program_id(0)
        direct_ref, token_ref, branch_ref, rate_ref, out_ref, grad_ref, term_ref = refs[5:]
        grad = direct_ref[...] + arrived_sum(h, *refs[:5])
        base, rates = token_ref[...].astype(wide), rate_ref[...]
        result, saved = settle_step(base, branch_ref[...], rates)
        back, branch_grad, terms = settle_back(grad, result, base, rates, saved)
        out_ref[...] = back
        grad_ref[...] = branch_grad.astype(low)

        @pl.when(h == 0)
        def _():
            term_ref[...] = rate_rows(terms)

        @pl.when(h != 0)
        def _():
            term_ref[...] += rate_rows(terms)

    rows = pl.BlockSpec((half, depth), lambda h: (h, 0))
    return pl.pallas_call(
        kernel,
        grid=(2,),
        in_specs=arrived_specs(n, depth) + [rows] * 3 + [pl.BlockSpec((1, depth), lambda h: (0, 0))],
        out_specs=[rows, rows, pl.BlockSpec((8, depth), lambda h: (0, 0))],
        out_shape=[
            jax.ShapeDtypeStruct((n, depth), wide),
            jax.ShapeDtypeStruct((n, depth), low),
            jax.ShapeDtypeStruct((8, depth), wide),
        ],
        compiler_params=params(),
        cost_estimate=cost(0, 0),
    )(*arrived, direct, tokens, branch, rate[None])


def lay_rows(refs, out):
    @pl.when(pl.program_id(0) == 0)
    def _():
        at = 0
        for ref in refs:
            out[at : at + ref.shape[0], :] = ref[...]
            at += ref.shape[0]


def mlp_forward(blocks, up_w, gate_w, scales, total, first, earlier):
    n = sum(block.shape[0] for block in blocks)
    depth, units = up_w.shape
    tile = 2 * LANES
    count = len(blocks)

    def kernel(*refs):
        ins, rest = refs[:count], refs[count:]
        up_ref, gate_ref, scale_ref = rest[:3]
        mid_ref, act_all, act_out, up_out, gate_out = rest[-5:]
        lay_rows(ins, mid_ref)
        left = mid_ref[...]
        up = nn(left, up_ref[...])
        gate = nn(left, gate_ref[...])
        lifted = scale_ref[1:2, :] * gate
        up_out[...] = up.astype(low)
        gate_out[...] = gate.astype(low)
        act = (scale_ref[0:1, :] * up * (lifted * jax.nn.sigmoid(lifted))).astype(low)
        act_out[...] = act
        act_all[...] = act

    weight = pl.BlockSpec((depth, tile), lambda j: (0, j))
    alone = pl.BlockSpec((n, tile), lambda j: (0, j))
    return pl.pallas_call(
        kernel,
        grid=(units // tile,),
        in_specs=chunk_specs(blocks, depth)
        + [weight] * 2
        + [pl.BlockSpec((2, tile), lambda j: (0, j))]
        + [pl.BlockSpec(memory_space=pl.ANY)] * len(earlier),
        out_specs=[
            pl.BlockSpec((n, depth), lambda j: (first, 0)), pl.BlockSpec((n, tile), lambda j: (first, j)),
            alone, alone, alone,
        ],
        out_shape=[jax.ShapeDtypeStruct((total, depth), low), jax.ShapeDtypeStruct((total, units), low)]
        + [jax.ShapeDtypeStruct((n, units), low)] * 3,
        input_output_aliases={count + 3 + i: i for i in range(len(earlier))},
        compiler_params=params(),
        cost_estimate=cost(4 * n * depth * units, 2 * (2 * n * depth + 2 * depth * units + 3 * n * units)),
    )(*blocks, up_w, gate_w, scales, *earlier)


def mlp_backward(blocks, up_w, gate_w, down_w, scales, up_raw, gate_raw, total, first, earlier):
    n = sum(block.shape[0] for block in blocks)
    depth, units = up_w.shape
    tile = 2 * LANES
    count = len(blocks)
    steps = units // tile

    def kernel(*refs):
        ins, rest = refs[:count], refs[count:]
        down_ref, scale_ref, up_raw_ref, gate_raw_ref, up_ref, gate_ref = rest[:6]
        branch_ref, up_out, gate_out, part_ref, gain_ref, kept, weights, sems = rest[-8:]
        step = pl.program_id(0)
        fetches = [
            pltpu.make_async_copy(ref, weights.at[i], sems.at[i]) for i, ref in enumerate((up_ref, gate_ref))
        ]

        @pl.when(step == 0)
        def _():
            for fetch in fetches:
                fetch.start()

        lay_rows(ins, branch_ref)
        up_gain, gate_gain = scale_ref[0:1, :], scale_ref[1:2, :]
        grad = nn(branch_ref[...], down_ref[...])
        up = up_raw_ref[...].astype(wide)
        gate = gate_raw_ref[...].astype(wide)
        lifted = gate_gain * gate
        slope = jax.nn.sigmoid(lifted)
        swished = lifted * slope
        up_part = grad * swished
        lifted_grad = grad * up * (up_gain * (slope + swished * (1.0 - slope)))
        up_term = jnp.sum(up_part * up, axis=0, keepdims=True)
        gate_term = jnp.sum(lifted_grad * gate, axis=0, keepdims=True)
        up_low = (up_part * up_gain).astype(low)
        gate_low = (lifted_grad * gate_gain).astype(low)
        up_out[...] = up_low
        gate_out[...] = gate_low
        kept[0, step] = up_low
        kept[1, step] = gate_low
        gain_ref[...] = jnp.concatenate([up_term, gate_term, jnp.zeros((6, tile), wide)], axis=0)

        @pl.when(step == steps - 1)
        def _():
            for fetch in fetches:
                fetch.wait()
            ups, gates = (jnp.concatenate([kept[i, k] for k in range(steps)], axis=1) for i in range(2))
            for at in range(0, depth, tile):
                part = nt(ups, weights[0, at : at + tile, :]) + nt(gates, weights[1, at : at + tile, :])
                part_ref[:, at : at + tile] = part.astype(low)

    anywhere = pl.BlockSpec(memory_space=pl.ANY)
    tiles = pl.BlockSpec((n, tile), lambda j: (first, j))
    alone = pl.BlockSpec((n, tile), lambda j: (0, j))
    all_units = jax.ShapeDtypeStruct((total, units), low)
    return pl.pallas_call(
        kernel,
        grid=(steps,),
        in_specs=chunk_specs(blocks, depth)
        + [
            pl.BlockSpec((depth, tile), lambda j: (0, j)), pl.BlockSpec((2, tile), lambda j: (0, j)),
            alone, alone, anywhere, anywhere,
        ]
        + [anywhere] * len(earlier),
        out_specs=[
            pl.BlockSpec((n, depth), lambda j: (first, 0)), tiles, tiles,
            pl.BlockSpec((n, depth), lambda j: (0, 0)), pl.BlockSpec((8, tile), lambda j: (0, j)),
        ],
        out_shape=[
            jax.ShapeDtypeStruct((total, depth), low), all_units, all_units,
            jax.ShapeDtypeStruct((n, depth), low), jax.ShapeDtypeStruct((8, units), wide),
        ],
        scratch_shapes=[
            pltpu.VMEM((2, steps, n, tile), low), pltpu.VMEM((2, depth, units), low),
            pltpu.SemaphoreType.DMA((2,)),
        ],
        input_output_aliases={count + 6 + i: i for i in range(len(earlier))},
        compiler_params=params(),
        cost_estimate=cost(6 * n * depth * units, 2 * (2 * n * depth + 3 * depth * units + 4 * n * units)),
    )(*blocks, down_w, scales, up_raw, gate_raw, up_w, gate_w, *earlier)


def place(blocks, indices):
    ndim = 2
    n = len(indices)
    count = len(blocks)
    pieces = [
        (i, at) for i, block in enumerate(blocks) for at in ([None] if block.ndim == ndim else range(block.shape[0]))
    ]
    shape = blocks[0].shape[-ndim:]
    where_to = jnp.stack([jnp.asarray(i, jnp.int32) for i in indices])

    def kernel(index_ref, *refs):
        out, sems = refs[count], refs[count + 1]
        copies = []
        for k, (i, at) in enumerate(pieces):
            source = refs[i] if at is None else refs[i].at[at]
            copies.append(pltpu.make_async_copy(source, out.at[index_ref[k]], sems.at[k]))
        for copy in copies:
            copy.start()
        for copy in copies:
            copy.wait()

    anywhere = pl.BlockSpec(memory_space=pl.ANY)
    out = jax.ShapeDtypeStruct((n,) + shape, blocks[0].dtype)
    return pl.pallas_call(
        kernel,
        in_specs=[pl.BlockSpec(memory_space=pltpu.SMEM)] + [anywhere] * count,
        out_specs=pl.BlockSpec(memory_space=pltpu.VMEM),
        out_shape=out,
        scratch_shapes=[pltpu.SemaphoreType.DMA((n,))],
        compiler_params=params(),
        cost_estimate=cost(0, 2 * out.size * out.dtype.itemsize),
    )(where_to, *blocks)


def spread_pack(grad, extra, chip):
    _, _, rows, columns = grad.shape
    total = rows + extra.shape[0]
    tile = 2 * LANES

    def kernel(chip_ref, grad_ref, extra_ref, first, second, keep):
        plan = [(first, 1, 0), (first, 3, 0), (second, 2, 1), (second, 3, 1)]
        plan += [(keep, 0, 0), (keep, 0, 1), (keep, 2, 0), (keep, 1, 1)]
        used = {}
        for out, k, half in plan:
            slot = used.get(id(out), 0)
            used[id(out)] = slot + 1
            out[slot, :rows, :] = grad_ref[chip_ref[0] ^ k, half]
            out[slot, rows:, :] = extra_ref[...]

    def out(n):
        return pl.BlockSpec((n, total, tile), lambda j, *_: (0, 0, j))

    return pl.pallas_call(
        kernel,
        grid_spec=pltpu.PrefetchScalarGridSpec(
            num_scalar_prefetch=1,
            grid=(columns // tile,),
            in_specs=[
                pl.BlockSpec((CHIPS, 2, rows, tile), lambda j, *_: (0, 0, 0, j)),
                pl.BlockSpec((extra.shape[0], tile), lambda j, *_: (0, j)),
            ],
            out_specs=[out(2), out(2), out(4)],
        ),
        out_shape=[jax.ShapeDtypeStruct((n, total, columns), low) for n in (2, 2, 4)],
        compiler_params=params(),
        cost_estimate=cost(0, 0),
    )(chip.reshape(1), grad, extra.astype(low))


def spread_turn(first, second, keep):
    _, total, columns = first.shape
    tile = 2 * LANES

    def kernel(first_ref, second_ref, keep_ref, y_ref, x_ref):
        y_ref[...] = (keep_ref[2].astype(wide) + first_ref[1].astype(wide)).astype(low)
        x_ref[...] = (keep_ref[3].astype(wide) + second_ref[1].astype(wide)).astype(low)

    def spec(n):
        return pl.BlockSpec((n, total, tile), lambda j: (0, 0, j))

    out = pl.BlockSpec((total, tile), lambda j: (0, j))
    return pl.pallas_call(
        kernel,
        grid=(columns // tile,),
        in_specs=[spec(2), spec(2), spec(4)],
        out_specs=[out] * 2,
        out_shape=[jax.ShapeDtypeStruct((total, columns), low)] * 2,
        compiler_params=params(),
        cost_estimate=cost(0, 0),
    )(first, second, keep)


def spread_finish(first, second, keep, last_y, last_x, width, core):
    _, total, columns = first.shape
    out_width = columns // 2

    def kernel(core_ref, first_ref, second_ref, keep_ref, y_ref, x_ref, *outs):
        for half in range(2):
            got, last = ((first_ref, y_ref), (second_ref, x_ref))[half]
            value = keep_ref[half].astype(wide) + got[0].astype(wide) + last[...].astype(wide)
            for which in range(2):
                piece = jnp.concatenate(
                    [
                        value[:, at + which * width : at + (which + 1) * width]
                        for at in range(0, columns, 2 * width)
                    ],
                    axis=1,
                ).astype(low)
                for side in range(2):

                    @pl.when((core_ref[0] ^ side) == half)
                    def _(side=side, which=which, piece=piece):
                        outs[2 * side + which][...] = piece

    whole = pl.BlockSpec(memory_space=pltpu.VMEM)
    return pl.pallas_call(
        kernel,
        in_specs=[pl.BlockSpec(memory_space=pltpu.SMEM)] + [whole] * 5,
        out_specs=[whole] * 4,
        out_shape=[jax.ShapeDtypeStruct((total, out_width), low)] * 4,
        compiler_params=params(),
        cost_estimate=cost(0, 0),
    )(core.reshape(1), first, second, keep, last_y, last_x)


def half_tiles(first, second, first_upper, second_upper):
    first, second = first.astype(wide), second.astype(wide)
    axis = first.ndim - 1
    first = jnp.where(first_upper, pltpu.roll(first, HALF, axis), first)
    second = jnp.where(second_upper, second, pltpu.roll(second, HALF, axis))
    lane = lax.broadcasted_iota(jnp.int32, first.shape, axis)
    return jnp.where(lane < HALF, first, second).astype(low)


def unit_pack(groups):
    weights = [weight for group in groups for weight in group]
    rows, units = weights[0].shape
    main = units // CHIPS // LANES * LANES
    width = len(weights) * main + len(groups) * LANES

    def kernel(*refs):
        out, at, first = refs[-1], 0, 0
        target = pl.program_id(0)
        start = pl.multiple_of(target * main, LANES)
        tile = pl.multiple_of(CHIPS * main + (target // 2) * LANES, LANES)
        upper = (target & 1) == 1
        for group in groups:
            members = refs[first : first + len(group)]
            first += len(group)
            for ref in members:
                out[0, :, at : at + main] = ref[:, pl.ds(start, main)]
                at += main
            rests = [ref[:, pl.ds(tile, LANES)] for ref in members]
            out[0, :, at : at + LANES] = half_tiles(rests[0], rests[-1], upper, upper)
            at += LANES

    whole = pl.BlockSpec((rows, units), lambda k: (0, 0))
    return pl.pallas_call(
        kernel,
        grid=(CHIPS,),
        in_specs=[whole] * len(weights),
        out_specs=pl.BlockSpec((1, rows, width), lambda k: (k, 0, 0)),
        out_shape=jax.ShapeDtypeStruct((CHIPS, rows, width), weights[0].dtype),
        cost_estimate=cost(0, 0),
    )(*weights)


def unit_lay(n, mine, theirs, core):
    count, _, rows, columns = mine.shape
    main = (columns - LANES) // n
    units = count * main + count // 2 * LANES

    def kernel(core_ref, *refs):
        outs = refs[2:]
        for side in range(2):
            slot = core_ref[0] ^ side
            blocks = refs[side]
            for i in range(n):
                for k in range(count):
                    outs[i][slot, :, k * main : (k + 1) * main] = blocks[k, 0, :, i * main : (i + 1) * main]
                tile = n * main
                upper = i == 1
                for k in range(0, count, 2):
                    at = count * main + k // 2 * LANES
                    outs[i][slot, :, at : at + LANES] = half_tiles(
                        blocks[k, 0, :, tile : tile + LANES],
                        blocks[k + 1, 0, :, tile : tile + LANES],
                        upper,
                        upper,
                    )

    block = pl.BlockSpec((count, 1, rows, columns), lambda q: (0, q, 0, 0))
    out = pl.BlockSpec((2, rows, units), lambda q: (q, 0, 0))
    return pl.pallas_call(
        kernel,
        grid=(CHIPS,),
        in_specs=[pl.BlockSpec(memory_space=pltpu.SMEM)] + [block] * 2,
        out_specs=[out] * n,
        out_shape=[jax.ShapeDtypeStruct((2 * CHIPS, rows, units), low)] * n,
        compiler_params=params(),
        cost_estimate=cost(0, 14 * n * 8 * rows * units // 4),
    )(core.reshape(1), mine, theirs)


def unit_unlay(grads, n, core):
    count = lax.axis_size("tensor")
    _, rows, units = grads.shape
    units = units // n
    main = units // count // LANES * LANES
    columns = n * main + (n + 1) // 2 * LANES

    def kernel(core_ref, *refs):
        for side in range(2):
            slot = core_ref[0] ^ side
            out = refs[1 + side]
            for k in range(count):
                for i in range(n):
                    out[k, 0, :, i * main : (i + 1) * main] = refs[0][slot, :, i * units + k * main : i * units + (k + 1) * main]
                at = count * main + k // 2 * LANES
                upper = k % 2 == 1
                rests = [refs[0][slot, :, i * units + at : i * units + at + LANES] for i in range(n)]
                for i in range(0, n, 2):
                    to = n * main + i // 2 * LANES
                    out[k, 0, :, to : to + LANES] = half_tiles(
                        rests[i], rests[min(i + 1, n - 1)], upper, upper
                    )

    block = pl.BlockSpec((2, rows, n * units), lambda q: (q, 0, 0))
    return pl.pallas_call(
        kernel,
        grid=(CHIPS,),
        in_specs=[pl.BlockSpec(memory_space=pltpu.SMEM)] + [block],
        out_specs=[pl.BlockSpec((count, 1, rows, columns), lambda q: (0, q, 0, 0))] * 2,
        out_shape=[jax.ShapeDtypeStruct((count, CHIPS, rows, columns), low)] * 2,
        compiler_params=params(),
        cost_estimate=cost(0, 14 * n * 8 * rows * units // 4),
    )(core.reshape(1), grads)


def unit_unpack(n, blocks):
    _, rows, columns = blocks.shape
    main = (columns - (n + 1) // 2 * LANES) // n
    units = CHIPS * main + CHIPS // 2 * LANES

    def kernel(block_ref, *outs):
        for i in range(n):
            for j in range(CHIPS):
                outs[i][:, j * main : (j + 1) * main] = block_ref[j, :, i * main : (i + 1) * main].astype(wide)
            tile = n * main + i // 2 * LANES
            upper = i % 2 == 1
            for j in range(0, CHIPS, 2):
                at = CHIPS * main + j // 2 * LANES
                outs[i][:, at : at + LANES] = half_tiles(
                    block_ref[j, :, tile : tile + LANES], block_ref[j + 1, :, tile : tile + LANES], upper, upper
                ).astype(wide)

    return pl.pallas_call(
        kernel,
        out_shape=[jax.ShapeDtypeStruct((rows, units), wide)] * n,
        compiler_params=params(),
    )(blocks)


def per_device(
    block_in, out_grad, global_pos,
    w_query, w_key, w_value, w_out, w_up, w_gate, w_down,
    qk_gain, up_gain, gate_gain, att_rate, mlp_rate,
):
    count = lax.axis_size("tensor")
    plane = lax.axis_size(DP)
    micro_count, _, local_rows, model_width = block_in.shape
    assert micro_count == 2 and count == 4
    seq_len = local_rows * count
    head_width = w_query.shape[1]
    core_heads = head_width * 2
    unit_width = w_up.shape[1]
    plane_unit = unit_width // CHIPS
    main = plane_unit // LANES * LANES
    rest = plane_unit - main
    me = lax.axis_index(DP)
    z = lax.axis_index("tensor")
    core = me & 1
    chip = (me >> 1) & 3
    early = z < 2

    def across(value, pairs):
        return lax.ppermute(
            value, ALL, [(a * count + b, c * count + d) for (a, b), (c, d) in pairs]
        )

    def home(far):
        return [
            ((p, t), ((p & ~1) | (t & 1), ((t & 2) ^ (2 if far else 0)) | (p & 1)))
            for p in range(plane)
            for t in range(count)
        ]

    def seq_near(value):
        return across(lax.dynamic_index_in_dim(value, z >> 1, 0, keepdims=False), home(False))

    def seq_far(value):
        return across(lax.dynamic_index_in_dim(value, 1 - (z >> 1), 0, keepdims=False), home(True))

    def seq_join(near, far):
        return pick(early, jnp.concatenate([near, far]), jnp.concatenate([far, near]))

    def from_sequence(value):
        first, second = value[:local_rows], value[local_rows:]
        near = across(pick(early, first, second), [(b, a) for a, b in home(False)])
        far = across(pick(early, second, first), [(b, a) for a, b in home(True)])
        return near, far

    def by_micro(near, far):
        return pick(early, jnp.stack([near, far]), jnp.stack([far, near])).astype(wide)

    def both_cores(value):
        value = value.reshape(2, local_rows, model_width)
        return place([value, swap(value, 1)], [core, core + 2, 1 - core, 3 - core]).reshape(
            seq_len, model_width
        )

    def core_scatter(partial):
        split = partial.reshape(2, 2, local_rows, model_width)
        got = swap(lax.dynamic_index_in_dim(split, 1 - core, 1, keepdims=False), 1)
        mine = lax.dynamic_index_in_dim(split, core, 1, keepdims=False)
        return (mine.astype(wide) + got.astype(wide)).reshape(2 * local_rows, model_width)

    def head_pairs(other_core, second):
        return [
            ((p ^ other_core, (t + 2 * (p & 1) + second) % count), (p, t))
            for p in range(plane)
            for t in range(count)
        ]

    def paired(a, b):
        return jnp.concatenate(
            [a[..., :head_width], b[..., :head_width], a[..., head_width:], b[..., head_width:]], axis=-1
        )

    def attn_fetch(first, second):
        packed = outer_gather(jnp.concatenate([first, second], axis=1))
        groups = [[across(packed, head_pairs(side, which)) for which in range(2)] for side in range(2)]
        return jnp.stack([paired(*pair) for pair in groups])

    def attn_pair(first, second, extra):
        packed = jnp.concatenate([outer_gather(jnp.concatenate([first, second], axis=1)), extra])
        return jnp.stack([packed, swap(packed, 1)])

    def attn_fetch_packed(packed, rows):
        groups = [across(packed, head_pairs(0, which)) for which in range(2)]
        return paired(*(group[:, :rows] for group in groups)), [group[0, rows:] for group in groups]

    def attn_first(sides):
        return sides, swap(sides, 2), swap(sides, 4)

    def attn_second(first):
        sides, along_x, along_y = first
        return sides, along_x, along_y, swap(along_y[0], 2), swap(along_x[1], 4)

    def attn_lay(gathered):
        sides, along_x, along_y, d_own, d_other = gathered
        return full_rows(
            place(
                [sides, along_x, along_y, d_own, d_other],
                [2 * (chip ^ (i // 2)) + (core ^ (i % 2)) for i in range(8)],
            )
        )

    def attn_pack(packed, extra):
        grad = plane_rows(packed).reshape(CHIPS, 2, -1, packed.shape[1])
        return spread_pack(grad, extra, chip)

    def attn_send(messages):
        first, second, keep = messages
        return swap(first, 2), swap(second, 4), keep

    def attn_turn(messages):
        to_y, to_x = messages
        return swap(to_y, 4), swap(to_x, 2)

    def attn_scatter(sent, turned):
        pieces = spread_finish(*sent, *turned, head_width, core)
        return [
            across(pieces[2 * side + which], [(b, a) for a, b in head_pairs(side, which)])
            for side in range(2)
            for which in range(2)
        ]

    def attn_join(got, extra_rows):
        got = [piece.astype(wide) for piece in got]
        rows = got[0].shape[0] - extra_rows
        small = jnp.stack([piece[rows:] for piece in got])
        extra = jnp.zeros(small.shape[1:], wide)
        for t in range(count):
            back = (z - t) % count
            index = 2 * ((back >> 1) ^ core) + (back & 1)
            extra = extra + lax.dynamic_index_in_dim(small, index, 0, keepdims=False)
        return attn_own(sum(piece[:rows] for piece in got), extra)

    def attn_own(grads, extra):
        grads = outer_scatter(grads)
        bit = 8
        while bit < plane:
            extra = extra + swap(extra, bit)
            bit *= 2
        return grads[:, :head_width], grads[:, head_width:], extra

    def unit_join(n, mine):
        return [full_rows(w) for w in unit_lay(n, mine, swap(mine, 1), core)]

    def unit_collect(grads):
        keep, send = unit_unlay([plane_rows(g) for g in grads], core)
        return add_low(keep, swap(send, 1))

    def unit_return(n, total):
        return [outer_scatter(g) for g in unit_unpack(n, lax.all_to_all(total, "chip", 0, 0, tiled=True))]

    tie = lax.optimization_barrier

    def halved(value):
        upper_part = lax.reduce_precision(value, 8, 7)
        return jnp.stack([upper_part, value - upper_part]).astype(low)

    qk_sides = attn_fetch(w_query, w_key)
    unit_blocks = unit_pack([[outer_gather(w_up), outer_gather(w_gate)], [outer_gather(w_down)]])
    mains = lax.dynamic_slice_in_dim(jnp.stack([up_gain, gate_gain]), chip * main, main, 1)
    rests = lax.dynamic_slice_in_dim(jnp.stack([up_gain, gate_gain]), CHIPS * main + chip * rest, rest, 1)
    unit_gains = halved(jnp.concatenate([mains, rests], axis=1).reshape(-1))
    gain_rows = jnp.concatenate(
        [unit_gains, halved(qk_gain).reshape(1, -1), jnp.zeros((13, 2 * head_width), low)]
    )
    vo_packed = attn_pair(w_value, w_out, gain_rows)
    unit_blocks = lax.all_to_all(unit_blocks, "chip", 0, 0, tiled=True)
    places_here = global_pos[:, 0]
    places_there = swap(places_here, 1)
    qk_sides, vo_packed, places_there, unit_blocks, block_in = tie(
        (qk_sides, vo_packed, places_there, unit_blocks, block_in)
    )
    qk_first = attn_first(qk_sides)
    vo_sides, gain_groups = attn_fetch_packed(vo_packed, qk_sides.shape[1])
    near = seq_near(block_in[:, 0])
    ug_columns = 2 * main + LANES
    ug_laid, down_laid = unit_blocks[..., :ug_columns], unit_blocks[..., ug_columns:]
    qk_first, vo_sides, gain_groups, near, block_in, ug_laid, down_laid = tie(
        (qk_first, vo_sides, gain_groups, near, block_in, ug_laid, down_laid)
    )
    far = seq_far(block_in[:, 0])
    qk_w = attn_lay(attn_second(qk_first))
    vo_w = attn_lay(attn_second(attn_first(vo_sides)))
    gain_here = jnp.stack(gain_groups)[:, :2].astype(wide).sum(axis=1)
    gain_there = swap(gain_here, 1)
    qk_w, vo_w, gain_there, far, near, ug_laid, down_laid = tie(
        (qk_w, vo_w, gain_there, far, near, ug_laid, down_laid)
    )
    tokens = seq_join(near, far)
    sequence = both_cores(tokens)
    ug_shifted = lax.all_gather(ug_laid, "tensor")
    down_shifted = lax.all_gather(down_laid, "tensor")
    unit_gains = pick(
        core == 0, jnp.concatenate([gain_here, gain_there]), jnp.concatenate([gain_there, gain_here])
    )
    unit_gains = lax.dynamic_slice_in_dim(jnp.concatenate([unit_gains, unit_gains]), count - z, count, 0)
    unit_gains = unit_gains.reshape(count, 2, plane_unit).transpose(1, 0, 2)
    scales = jnp.concatenate(
        [unit_gains[..., :main].reshape(2, -1), unit_gains[..., main:].reshape(2, -1)], axis=1
    )
    head_gain = jnp.stack(gain_groups)[:, 2].astype(wide).reshape(2, 2, head_width).sum(axis=1)
    head_gain = head_gain.reshape(core_heads)
    places = lax.dynamic_index_in_dim(
        pick((z & 1) == core, places_here, places_there), z >> 1, 0, keepdims=False
    )
    flags = jnp.any(places[:, None] == jnp.arange(seq_len, dtype=jnp.int32)[None, :], axis=0).astype(wide)
    flag_row, flag_col = flags[None], flags[:, None]

    heads, raw = project_heads(sequence, qk_w, jnp.concatenate([head_gain, head_gain]))
    value_rows = product(sequence, vo_w, 0)
    mixed, lse = attend_forward(heads, value_rows, flag_row, flag_col)
    partial = sum_back([(mixed, 0, core_heads)], [(vo_w, 1, core_heads)])
    partial = partial.reshape(2, 2, local_rows, model_width)
    got = swap(lax.dynamic_index_in_dim(partial, 1 - core, 1, keepdims=False), 1)
    hidden, hidden_low, att_branch = settle_attention(partial, got, tokens, att_rate, core)

    own_rows = 2 * local_rows
    all_rows = CHIPS * own_rows
    hidden_low, ug_shifted = tie((hidden_low, ug_shifted))
    first = plane_first(hidden_low)
    up_w, gate_w = unit_join(2, ug_shifted)
    earlier, saved, acts = (), [], []

    def forward(blocks, at):
        nonlocal earlier
        *earlier, act, up_raw, gate_raw = mlp_forward(blocks, up_w, gate_w, scales, all_rows, at, earlier)
        saved.append((up_raw, gate_raw))
        return act

    def back(act):
        return sum_back([(act, 0, act.shape[1])], [(down_w, 0, act.shape[1])])

    def by_chip(own, both, diagonal):
        return [own, both[:own_rows], both[own_rows:], diagonal]

    act_own = forward([hidden_low], 2)
    out_grad_low = out_grad[:, 0].astype(low)
    first, act_own, out_grad_low = tie((first, act_own, out_grad_low))
    _, along_x, along_y, *diagonal = plane_second(first)
    act_both = forward([along_x, along_y], 0)
    diagonal, act_both, down_shifted = tie((diagonal, act_both, down_shifted))
    (down_w,) = unit_join(1, down_shifted)
    act_diagonal = forward(diagonal, 3)
    mid, activated = earlier
    parts = [back(act) for act in (act_own, act_both, act_diagonal)]
    parts, out_grad_low = tie((parts, out_grad_low))
    sent, _ = scatter_first(by_chip(*parts))
    cotangent = seq_near(out_grad_low), seq_far(out_grad_low)
    sent, cotangent = tie((sent, cotangent))
    block_rows, direct, branch_grad, mlp_rate_term = settle_units(
        scatter_last(sent), hidden, *cotangent, early, mlp_rate
    )

    first = plane_first(branch_grad)
    returned = from_sequence(block_rows)
    earlier, unit_terms = (), []

    def backward(blocks, at, raws):
        nonlocal earlier
        *earlier, part, unit_term = mlp_backward(
            blocks, up_w, gate_w, down_w, scales, *raws, all_rows, at, earlier
        )
        unit_terms.append(unit_term[:2])
        return part

    part_own = backward([branch_grad], 2, saved[0])
    first, part_own = tie((first, part_own))
    _, along_x, along_y, *diagonal = plane_second(first)
    part_both = backward([along_x, along_y], 0, saved[1])
    diagonal, part_both, returned = tie((diagonal, part_both, returned))
    part_diagonal = backward(diagonal, 3, saved[2])
    branch, up_low, gate_low = earlier
    sent, (branch, mid) = scatter_first(by_chip(part_own, part_both, part_diagonal), (branch, mid))
    down_blocks = unit_unlay(plane_rows(rows_product([(branch, [activated])], 2 * LANES)), 1, core)
    ug_grad = rows_product([(mid, [up_low, gate_low])], 2 * LANES)
    sent, down_blocks, ug_grad = tie((sent, down_blocks, ug_grad))
    arrived = scatter_last(sent)
    down_blocks = add_low(down_blocks[0], swap(down_blocks[1], 1))
    ug_blocks = unit_unlay(plane_rows(ug_grad), 2, core)
    arrived, ug_blocks, down_blocks = tie((arrived, ug_blocks, down_blocks))
    down_back = lax.psum_scatter(down_blocks, "tensor", scatter_dimension=0)
    ug_there = swap(ug_blocks[1], 1)
    input_direct, att_grad, att_rate_term = settle_attention_back(
        arrived, direct, hidden, tokens, att_branch, att_rate
    )
    att_low = both_cores(att_grad)
    ug_blocks = add_low(ug_blocks[0], ug_there)
    att_low, ug_blocks = tie((att_low, ug_blocks))
    ug_back = lax.psum_scatter(ug_blocks, "tensor", scatter_dimension=0)
    mixed_grad = product(att_low, vo_w, 1)
    heads_low, vraw_low, head_terms = attend_backward(
        heads, raw, value_rows, mixed, mixed_grad, lse, head_gain, flag_row, flag_col
    )
    block_out = by_micro(*returned)

    small = jnp.concatenate(
        [
            sum(unit_terms),
            att_rate_term[:1],
            mlp_rate_term[:1],
        ]
    )
    small = small + swap(small, 1)
    unit_rows = jnp.concatenate(
        [small[:2, : count * main].reshape(2, count, main), small[:2, count * main :].reshape(2, count, rest)],
        axis=2,
    )
    unit_rows = lax.dynamic_slice_in_dim(
        jnp.concatenate([unit_rows, unit_rows], axis=1), z + 2 * core, 2, 1
    ).reshape(1, 4 * plane_unit)
    rate_rows = jnp.broadcast_to(small[2:].reshape(4, 2, 1, head_width), (4, 2, 2, head_width))
    rate_rows = rate_rows.reshape(1, 4, 4 * head_width)
    own_chip = jnp.arange(CHIPS)[:, None] == chip
    vo_extra = jnp.concatenate(
        [
            jnp.where(own_chip, unit_rows, 0.0),
            jnp.where(own_chip[..., None], rate_rows, 0.0).reshape(4 * CHIPS, -1),
            jnp.zeros((EXTRA - 5 * CHIPS, 4 * head_width), wide),
        ]
    )
    qk_extra = jnp.concatenate(
        [
            jnp.where(own_chip, head_terms[:2].reshape(1, 4 * head_width), 0.0),
            jnp.zeros((EXTRA // 2 - CHIPS, 4 * head_width), wide),
        ]
    )
    heads_low, vraw_low, down_back = tie((heads_low, vraw_low, down_back))
    vo_grad = rows_product([(sequence, [vraw_low]), (att_low, [mixed])], core_heads)
    vo_messages, vraw_low = tie((attn_pack(vo_grad, vo_extra), vraw_low))
    vo_sent = attn_send(vo_messages)
    in_part = sum_back(
        [(heads_low, 0, 2 * core_heads), (vraw_low, 0, core_heads)],
        [(qk_w, 0, 2 * core_heads), (vo_w, 0, core_heads)],
    )
    vo_sent, heads_low, in_part, ug_back, block_out = tie((vo_sent, heads_low, in_part, ug_back, block_out))
    vo_messages, heads_low, in_part = tie((spread_turn(*vo_sent), heads_low, in_part))
    vo_turned = attn_turn(vo_messages)
    in_rows = (input_direct + core_scatter(in_part)).astype(low)
    qk_messages = attn_pack(rows_product([(sequence, [heads_low])], 2 * LANES), qk_extra)
    vo_turned, in_rows, qk_messages = tie((vo_turned, in_rows, qk_messages))
    qk_sent = attn_send(qk_messages)
    returned_in = from_sequence(in_rows)
    vo_got = attn_scatter(vo_sent, vo_turned)
    qk_sent, down_back, ug_back = tie((qk_sent, down_back, ug_back))
    qk_turned = attn_turn(spread_turn(*qk_sent))
    (grad_down,) = unit_return(1, down_back)
    qk_turned, returned_in, vo_got, grad_down = tie((qk_turned, returned_in, vo_got, grad_down))
    qk_got = attn_scatter(qk_sent, qk_turned)
    grad_up, grad_gate = unit_return(2, ug_back)
    in_grad = by_micro(*returned_in)
    grad_value, grad_out, vo_small = attn_join(vo_got, EXTRA)
    grad_query, grad_key, qk_small = attn_join(qk_got, EXTRA // 2)

    units = vo_small[:CHIPS].reshape(CHIPS, 2, plane_unit).transpose(1, 0, 2)
    units = jnp.concatenate([units[..., :main].reshape(2, -1), units[..., main:].reshape(2, -1)], axis=1)
    rates = jnp.sum(vo_small[CHIPS : 5 * CHIPS].reshape(CHIPS, 2, model_width), axis=0)
    head_sums = jnp.sum(qk_small[:CHIPS], axis=0)
    grad_qk_gain = head_sums[:head_width] + head_sums[head_width:]
    return (
        block_out[:, None], in_grad[:, None],
        grad_query, grad_key, grad_value, grad_out, grad_up, grad_gate, grad_down,
        grad_qk_gain, units[0], units[1], rates[0], rates[1],
    )


def solution(mesh):
    shape = dict(mesh.shape)
    plane, count = shape["dp"], shape["tensor"]
    split = Mesh(mesh.devices.reshape(plane // 8, CHIPS, 2, count), ALL)
    tokens = P(None, DP, "tensor", None)
    matrix = P(DP, "tensor")
    in_specs = (tokens, tokens, P(None, DP, None)) + (matrix,) * 7 + (P("tensor"),) * 3 + (P(), P())
    out_specs = (tokens, tokens) + (matrix,) * 7 + (P("tensor"),) * 3 + (P(), P())
    return jax.shard_map(
        per_device, mesh=split, in_specs=in_specs, out_specs=out_specs, check_vma=False
    )
```

```python
import math

import jax
import jax.numpy as jnp
from jax import lax
from jax.experimental import pallas as pl
from jax.experimental.pallas import tpu as pltpu
from jax.sharding import Mesh, PartitionSpec as P

HD = 64
WINDOW = 512
CHIPS = 4
LANES = 128
HALF = 64
EXTRA = 16
BLOCK = 256
VMEM_LIMIT = 48 * 2**20

DP = ("outer", "chip", "core")
ALL = DP + ("tensor",)

epsilon = 1e-06
blocked = -1e30
low = jnp.bfloat16
wide = jnp.float32


def swap(value, bit):
    count = lax.axis_size(DP)
    return lax.ppermute(value, DP, [(i, i ^ bit) for i in range(count)])


def pick(flag, when_true, when_false):
    return jnp.where(flag, when_true, when_false)


def outer_gather(value):
    me = lax.axis_index(DP)
    bit = 8
    while bit < lax.axis_size(DP):
        other = swap(value, bit)
        upper = (me & bit) != 0
        value = pick(
            upper, jnp.concatenate([other, value]), jnp.concatenate([value, other])
        )
        bit *= 2
    return value


def outer_scatter(value):
    me = lax.axis_index(DP)
    bit = lax.axis_size(DP) // 2
    while bit >= 8:
        rows = value.shape[0] // 2
        upper = (me & bit) != 0
        keep = pick(upper, value[rows:], value[:rows])
        send = pick(upper, value[:rows], value[rows:])
        value = (keep.astype(wide) + swap(send, bit).astype(wide)).astype(value.dtype)
        bit //= 2
    return value


def full_rows(value):
    outer = lax.axis_size(DP) // 8
    count, rows, columns = value.shape
    if outer > 1:
        value = value.reshape(count, outer, rows // outer, columns).transpose(1, 0, 2, 3)
    return value.reshape(count * rows, columns)


def plane_rows(value):
    outer = lax.axis_size(DP) // 8
    total, columns = value.shape
    if outer > 1:
        value = value.reshape(outer, 8, total // 8 // outer, columns).transpose(1, 0, 2, 3)
    return value.reshape(8, total // 8, columns)


def plane_first(value):
    return value, swap(value, 2), swap(value, 4)


def plane_second(first):
    value, along_x, along_y = first
    half = value.shape[0] // 2
    return value, along_x, along_y, swap(along_y[:half], 2), swap(along_x[half:], 4)


def scatter_first(blocks, then=()):
    own, along_x, along_y, diagonal = blocks
    half = own.shape[0] // 2
    first, second, then = lax.optimization_barrier(
        (
            jnp.concatenate([along_x[:half], diagonal[:half]]),
            jnp.concatenate([along_y[half:], diagonal[half:]]),
            then,
        )
    )
    return (blocks, swap(first, 2), swap(second, 4)), then


def scatter_last(sent):
    (own, along_x, along_y, _), first, second = sent
    half = own.shape[0] // 2
    next_y = (along_y[:half].astype(wide) + first[half:].astype(wide)).astype(low)
    next_x = (along_x[half:].astype(wide) + second[half:].astype(wide)).astype(low)
    return own, first, second, swap(next_y, 4), swap(next_x, 2)


def scatter_second(sent):
    own, first, second, last_y, last_x = scatter_last(sent)
    half = own.shape[0] // 2
    top = own[:half].astype(wide) + first[:half].astype(wide) + last_y.astype(wide)
    bottom = own[half:].astype(wide) + second[:half].astype(wide) + last_x.astype(wide)
    return jnp.concatenate([top, bottom])


def nt(left, right):
    return lax.dot_general(left, right, (((1,), (1,)), ((), ())), preferred_element_type=wide)


def nn(left, right):
    return lax.dot_general(left, right, (((1,), (0,)), ((), ())), preferred_element_type=wide)


def tn(left, right):
    return lax.dot_general(left, right, (((0,), (0,)), ((), ())), preferred_element_type=wide)


def params():
    return pltpu.CompilerParams(vmem_limit_bytes=VMEM_LIMIT)


def cost(flops, moved):
    return pl.CostEstimate(flops=1, bytes_accessed=1, transcendentals=0)


def head_means(width):
    rows = lax.broadcasted_iota(jnp.int32, (width, width), 0) // HD
    columns = lax.broadcasted_iota(jnp.int32, (width, width), 1) // HD
    return jnp.where(rows == columns, 1.0 / HD, 0.0).astype(low)


def head_scale(raw, means):
    return lax.rsqrt(nn((raw * raw).astype(low), means) + epsilon)


def project_heads(rows, weight, gain):
    n, depth = rows.shape
    width = weight.shape[1]
    tile = 2 * LANES
    block = 512

    def kernel(rows_ref, weight_ref, gain_ref, out_ref, raw_ref):
        means = head_means(tile)
        for start in range(0, n, block):
            span = slice(start, start + block)
            raw = nn(rows_ref[span, :], weight_ref[...])
            raw_ref[span, :] = raw.astype(low)
            out_ref[span, :] = (raw * head_scale(raw, means) * gain_ref[...]).astype(low)

    out = pl.BlockSpec((n, tile), lambda j: (0, j))
    return pl.pallas_call(
        kernel,
        grid=(width // tile,),
        in_specs=[
            pl.BlockSpec((n, depth), lambda j: (0, 0)),
            pl.BlockSpec((depth, tile), lambda j: (0, j)),
            pl.BlockSpec((1, tile), lambda j: (0, j)),
        ],
        out_specs=[out, out],
        out_shape=[jax.ShapeDtypeStruct((n, width), low)] * 2,
        compiler_params=params(),
        cost_estimate=cost(2 * n * depth * width, 2 * (n * depth + depth * width + 2 * n * width)),
    )(rows, weight, gain[None])


def fill_bias(bias, flag_row, flag_col):
    @pl.when(pl.program_id(0) == 0)
    def _():
        for i in range(bias.shape[0] // BLOCK):
            for j in range(i + 1):
                keys = slice(j * BLOCK, (j + 1) * BLOCK)
                rows = slice(i * BLOCK, (i + 1) * BLOCK)
                key_ids = j * BLOCK + lax.broadcasted_iota(jnp.int32, (BLOCK, BLOCK), 0)
                row_ids = i * BLOCK + lax.broadcasted_iota(jnp.int32, (BLOCK, BLOCK), 1)
                flagged = jnp.maximum(flag_row[:, rows], flag_col[keys, :]) > 0.5
                allow = (key_ids <= row_ids) & ((row_ids - key_ids < WINDOW) | flagged)
                bias[keys, rows] = jnp.where(allow, 0.0, blocked)


def head_lanes(value, head):
    lane = lax.broadcasted_iota(jnp.int32, value.shape, 1)
    mine = (lane < HD) if head == 0 else (lane >= HD)
    return jnp.where(mine, value, jnp.zeros_like(value))


def flag_specs(seq_len):
    return [pl.BlockSpec((1, seq_len), lambda h: (0, 0)), pl.BlockSpec((seq_len, 1), lambda h: (0, 0))]


def attend_forward(heads, value_rows, flag_row, flag_col):
    seq_len, width = value_rows.shape
    pairs = width // LANES

    def kernel(q_ref, k_ref, v_ref, row_ref, col_ref, out_ref, lse_ref, bias, turned):
        fill_bias(bias, row_ref, col_ref)
        turned[...] = v_ref[...].astype(wide).T.astype(low)
        for i in range(seq_len // BLOCK):
            rows = slice(i * BLOCK, (i + 1) * BLOCK)
            reach = (i + 1) * BLOCK
            block = q_ref[rows, :] * jnp.asarray(1.0 / math.sqrt(HD), low)
            halves = []
            for head in range(2):
                scores = nt(k_ref[:reach, :], head_lanes(block, head)) + bias[:reach, rows]
                raised = jnp.exp(scores)
                total = jnp.sum(raised, axis=0, keepdims=True)
                mixed = nn(turned[head * HD : (head + 1) * HD, :reach], raised.astype(low))
                halves.append(mixed / total)
                lse_ref[0, head : head + 1, rows] = jnp.log(total)
            out_ref[rows, :] = jnp.concatenate(halves, axis=0).T.astype(low)

    block = pl.BlockSpec((seq_len, LANES), lambda h: (0, h))
    keys = pl.BlockSpec((seq_len, LANES), lambda h: (0, pairs + h))
    return pl.pallas_call(
        kernel,
        grid=(pairs,),
        in_specs=[block, keys, block] + flag_specs(seq_len),
        out_specs=[block, pl.BlockSpec((1, 8, seq_len), lambda h: (h, 0, 0))],
        out_shape=[
            jax.ShapeDtypeStruct((seq_len, width), low),
            jax.ShapeDtypeStruct((pairs, 8, seq_len), wide),
        ],
        scratch_shapes=[pltpu.VMEM((seq_len, seq_len), wide), pltpu.VMEM((LANES, seq_len), low)],
        compiler_params=params(),
        cost_estimate=cost(16 * seq_len * seq_len * width, 10 * seq_len * width),
    )(heads, heads, value_rows, flag_row, flag_col)


def attend_backward(heads, raw, value_rows, mixed, mixed_grad, lse, gain, flag_row, flag_col):
    seq_len, width = value_rows.shape
    pairs = width // LANES
    scale = 1.0 / math.sqrt(HD)

    def unnorm(grad, raw_block, gain_row, means):
        raw_block = raw_block.astype(wide)
        factor = head_scale(raw_block, means)
        normed = raw_block * factor
        term = jnp.sum(grad * normed, axis=0, keepdims=True)
        grad = grad * gain_row
        inner = nn((grad * normed).astype(low), means)
        return (factor * (grad - normed * inner)).astype(low), term

    def kernel(
        q_ref, k_ref, v_ref, qraw_ref, kraw_ref, m_ref, g_ref, lse_ref, gain_ref, row_ref, col_ref,
        heads_ref, dv_ref, term_ref, bias, turned, key_total, value_total, dq_ref, dk_ref, sems,
    ):
        step = pl.program_id(0)

        def stores(pair):
            return [
                pltpu.make_async_copy(
                    ref, heads_ref.at[:, pl.ds(pl.multiple_of((side * pairs + pair) * LANES, LANES), LANES)], sems.at[side]
                )
                for side, ref in enumerate((dq_ref, dk_ref))
            ]

        @pl.when(step > 0)
        def _():
            for store in stores(step - 1):
                store.wait()

        fill_bias(bias, row_ref, col_ref)
        turned[...] = k_ref[...].astype(wide).T.astype(low)
        means = head_means(LANES)
        gain_row = gain_ref[...]
        query_term = key_term = jnp.zeros((1, LANES), wide)
        count = seq_len // BLOCK
        for i in reversed(range(count)):
            rows = slice(i * BLOCK, (i + 1) * BLOCK)
            reach = (i + 1) * BLOCK
            block = q_ref[rows, :] * jnp.asarray(scale, low)
            grads = g_ref[rows, :]
            products = (grads.astype(wide) * m_ref[rows, :].astype(wide)).T
            halves = []
            key_parts = value_parts = None
            for head in range(2):
                inner = jnp.sum(products[head * HD : (head + 1) * HD], axis=0, keepdims=True)
                query = head_lanes(block, head)
                grad = head_lanes(grads, head)
                scores = nt(k_ref[:reach, :], query) + bias[:reach, rows]
                probs = jnp.exp(scores - lse_ref[0, head : head + 1, rows])
                prob_grad = nt(v_ref[:reach, :], grad)
                score_grad = (probs * (prob_grad - inner)).astype(low)
                halves.append(nn(turned[head * HD : (head + 1) * HD, :reach], score_grad))
                key_part = nn(score_grad, query)
                value_part = nn(probs.astype(low), grad)
                key_parts = key_part if key_parts is None else key_parts + key_part
                value_parts = value_part if value_parts is None else value_parts + value_part
            if i == count - 1:
                key_total[...] = key_parts
                value_total[...] = value_parts
            else:
                key_total[:reach, :] += key_parts
                value_total[:reach, :] += value_parts
            query_grad = jnp.concatenate(halves, axis=0).T * scale
            dq_ref[rows, :], term = unnorm(query_grad, qraw_ref[rows, :], gain_row, means)
            query_term = query_term + term
        dv_ref[...] = value_total[...].astype(low)
        for i in range(count):
            rows = slice(i * BLOCK, (i + 1) * BLOCK)
            dk_ref[rows, :], term = unnorm(key_total[rows, :], kraw_ref[rows, :], gain_row, means)
            key_term = key_term + term
        term_ref[...] = jnp.concatenate([query_term, key_term, jnp.zeros((6, LANES), wide)], axis=0)
        for store in stores(step):
            store.start()

        @pl.when(step == pairs - 1)
        def _():
            for store in stores(step):
                store.wait()

    block = pl.BlockSpec((seq_len, LANES), lambda h: (0, h))
    keys = pl.BlockSpec((seq_len, LANES), lambda h: (0, pairs + h))
    return pl.pallas_call(
        kernel,
        grid=(pairs,),
        in_specs=[block, keys, block, block, keys, block, block]
        + [pl.BlockSpec((1, 8, seq_len), lambda h: (h, 0, 0)), pl.BlockSpec((1, LANES), lambda h: (0, h))]
        + flag_specs(seq_len),
        out_specs=[pl.BlockSpec(memory_space=pl.ANY), block, pl.BlockSpec((8, LANES), lambda h: (0, h))],
        out_shape=[
            jax.ShapeDtypeStruct((seq_len, 2 * width), low),
            jax.ShapeDtypeStruct((seq_len, width), low),
            jax.ShapeDtypeStruct((8, width), wide),
        ],
        scratch_shapes=[
            pltpu.VMEM((seq_len, seq_len), wide),
            pltpu.VMEM((LANES, seq_len), low),
            pltpu.VMEM((seq_len, LANES), wide),
            pltpu.VMEM((seq_len, LANES), wide),
            pltpu.VMEM((seq_len, LANES), low),
            pltpu.VMEM((seq_len, LANES), low),
            pltpu.SemaphoreType.DMA((2,)),
        ],
        compiler_params=params(),
        cost_estimate=cost(32 * seq_len * seq_len * width, 20 * seq_len * width),
    )(heads, heads, value_rows, raw, raw, mixed, mixed_grad, lse, gain[None], flag_row, flag_col)


def sum_back(lefts, rights, n=None, first=0):
    n = n or lefts[0][0].shape[0]
    out_width = rights[0][0].shape[0]
    tile = 2 * LANES
    count = len(lefts)

    def kernel(*refs):
        total = nt(refs[0][...], refs[count][...])
        for i in range(1, count):
            total = total + nt(refs[i][...], refs[count + i][...])
        refs[2 * count][...] = total.astype(low)

    depth = sum(columns for _, _, columns in lefts)
    return pl.pallas_call(
        kernel,
        grid=(out_width // tile,),
        in_specs=[pl.BlockSpec((n, columns), lambda j, at=at: (first, at)) for _, at, columns in lefts]
        + [pl.BlockSpec((tile, columns), lambda j, at=at: (j, at)) for _, at, columns in rights],
        out_specs=pl.BlockSpec((n, tile), lambda j: (0, j)),
        out_shape=jax.ShapeDtypeStruct((n, out_width), low),
        compiler_params=params(),
        cost_estimate=cost(2 * n * out_width * depth, 2 * (n + out_width) * depth + 2 * n * out_width),
    )(*(matrix for matrix, _, _ in lefts + rights))


def add_low(first, second):
    columns = first.shape[-1]
    flat = (first.size // columns, columns)
    block = flat[0] // 8

    def kernel(a_ref, b_ref, out_ref):
        out_ref[...] = (a_ref[...].astype(wide) + b_ref[...].astype(wide)).astype(low)

    spec = pl.BlockSpec((block, columns), lambda r: (r, 0))
    out = pl.pallas_call(
        kernel,
        grid=(8,),
        in_specs=[spec, spec],
        out_specs=spec,
        out_shape=jax.ShapeDtypeStruct(flat, low),
        compiler_params=params(),
        cost_estimate=cost(first.size, 6 * first.size),
    )(first.reshape(flat), second.reshape(flat))
    return out.reshape(first.shape)


def rows_product(pairs, tile):
    n, depth = pairs[0][0].shape
    lefts = [left for left, _ in pairs]
    rights = [right for _, group in pairs for right in group]
    owner = [k for k, (_, group) in enumerate(pairs) for _ in group]
    steps = [right.shape[1] // tile for right in rights]
    starts = [sum(steps[:i]) for i in range(len(steps))]
    chunk = 256

    def kernel(*refs):
        left_refs, right_refs = refs[: len(lefts)], refs[len(lefts) : len(lefts) + len(rights)]
        out, turned = refs[-2:]
        step = pl.program_id(0)
        for i, right in enumerate(right_refs):
            if i == 0 or owner[i] != owner[i - 1]:

                @pl.when(step == starts[i])
                def _(left=left_refs[owner[i]]):
                    for at in range(0, n, chunk):
                        turned[:, at : at + chunk] = left[at : at + chunk, :].T

            @pl.when((step >= starts[i]) & (step < starts[i] + steps[i]))
            def _(right=right):
                out[...] = nn(turned[...], right[...]).astype(low)

    def tile_of(i):
        return lambda j: (0, jnp.clip(j - starts[i], 0, steps[i] - 1))

    width = sum(right.shape[1] for right in rights)
    return pl.pallas_call(
        kernel,
        grid=(sum(steps),),
        in_specs=[pl.BlockSpec((n, depth), lambda j: (0, 0))] * len(lefts)
        + [pl.BlockSpec((n, tile), tile_of(i)) for i in range(len(rights))],
        out_specs=pl.BlockSpec((depth, tile), lambda j: (0, j)),
        out_shape=jax.ShapeDtypeStruct((depth, width), low),
        scratch_shapes=[pltpu.VMEM((depth, n), low)],
        compiler_params=params(),
        cost_estimate=cost(2 * n * depth * width, 2 * (n * (depth + width) + depth * width)),
    )(*lefts, *rights)


def product(left, right):
    n, depth = left.shape
    width = right.shape[1]

    def kernel(left_ref, right_ref, out_ref):
        out_ref[...] = nn(left_ref[...], right_ref[...]).astype(low)

    return pl.pallas_call(
        kernel,
        grid=(1,),
        in_specs=[pl.BlockSpec((n, depth), lambda j: (0, 0)), pl.BlockSpec((depth, width), lambda j: (0, 0))],
        out_specs=pl.BlockSpec((n, width), lambda j: (0, 0)),
        out_shape=jax.ShapeDtypeStruct((n, width), low),
        compiler_params=params(),
        cost_estimate=cost(2 * n * depth * width, 2 * (n * depth + depth * width + n * width)),
    )(left, right)


def chunk_specs(blocks, width):
    return [pl.BlockSpec(block.shape, lambda j: (0, 0)) for block in blocks]


def row_scale(values):
    return lax.rsqrt(jnp.mean(values * values, axis=-1, keepdims=True) + epsilon)


def unscale(grad, normed, scale):
    return scale * (grad - normed * jnp.mean(grad * normed, axis=-1, keepdims=True))


def settle_step(base, branch, rate):
    branch_scale = row_scale(branch)
    normed = branch * branch_scale
    moved = base + rate * (normed - base)
    scale = row_scale(moved)
    return moved * scale, (normed, branch_scale, scale)


def settle_back(grad, result, base, rate, saved):
    normed, branch_scale, scale = saved
    grad = unscale(grad, result, scale)
    return grad * (1.0 - rate), unscale(grad * rate, normed, branch_scale), grad * (normed - base)


def rate_rows(terms):
    return jnp.concatenate([jnp.sum(terms, axis=0, keepdims=True), jnp.zeros((7, terms.shape[1]), wide)])


def settle_attention(partial, got, tokens, rate, core):
    _, _, n, depth = partial.shape
    block = n // 2

    def kernel(core_ref, part_ref, got_ref, token_ref, rate_ref, hidden_ref, low_ref, branch_ref):
        branch = part_ref[0, 0].astype(wide) + got_ref[0].astype(wide)
        hidden, _ = settle_step(token_ref[...].astype(wide), branch, rate_ref[...])
        hidden_ref[...] = hidden
        low_ref[...] = hidden.astype(low)
        branch_ref[...] = branch

    rows = pl.BlockSpec((block, depth), lambda j, r, core_ref: (2 * j + r, 0))
    return pl.pallas_call(
        kernel,
        grid_spec=pltpu.PrefetchScalarGridSpec(
            num_scalar_prefetch=1,
            grid=(2, 2),
            in_specs=[
                pl.BlockSpec((1, 1, block, depth), lambda j, r, core_ref: (j, core_ref[0], r, 0)),
                pl.BlockSpec((1, block, depth), lambda j, r, core_ref: (j, r, 0)),
                rows,
                pl.BlockSpec((1, depth), lambda j, r, core_ref: (0, 0)),
            ],
            out_specs=[rows] * 3,
        ),
        out_shape=[
            jax.ShapeDtypeStruct((2 * n, depth), wide),
            jax.ShapeDtypeStruct((2 * n, depth), low),
            jax.ShapeDtypeStruct((2 * n, depth), wide),
        ],
        compiler_params=params(),
        cost_estimate=cost(0, 0),
    )(core.reshape(1), partial, got, tokens, rate[None])


def arrived_specs(n, depth):
    block = n // 4
    piece = pl.BlockSpec((block, depth), lambda h, r, *_: (r, 0))
    return [pl.BlockSpec((block, depth), lambda h, r, *_: (2 * h + r, 0))] + [piece] * 4


def arrived_sum(h, own, first, second, last_y, last_x):
    top, bottom = (a[...].astype(wide) + b[...].astype(wide) for a, b in ((first, last_y), (second, last_x)))
    return own[...].astype(wide) + jnp.where(h == 0, top, bottom)


def settle_units(arrived, hidden, near, far, early, rate):
    n, depth = hidden.shape
    block = n // 4

    def kernel(early_ref, *refs):
        h = pl.program_id(0)
        branch = arrived_sum(h, *refs[:5])
        hidden_ref, near_ref, far_ref, rate_ref, out_ref, direct_ref, grad_ref, term_ref = refs[5:]
        base, rates = hidden_ref[...], rate_ref[...]
        result, saved = settle_step(base, branch, rates)
        cotangent = jnp.where((h == 0) == (early_ref[0] == 1), near_ref[...], far_ref[...])
        direct, grad, terms = settle_back(cotangent.astype(wide), result, base, rates, saved)
        out_ref[...] = result.astype(low)
        direct_ref[...] = direct
        grad_ref[...] = grad.astype(low)

        start = (h == 0) & (pl.program_id(1) == 0)

        @pl.when(start)
        def _():
            term_ref[...] = rate_rows(terms)

        @pl.when(jnp.logical_not(start))
        def _():
            term_ref[...] += rate_rows(terms)

    rows = pl.BlockSpec((block, depth), lambda h, r, *_: (2 * h + r, 0))
    piece = pl.BlockSpec((block, depth), lambda h, r, *_: (r, 0))
    return pl.pallas_call(
        kernel,
        grid_spec=pltpu.PrefetchScalarGridSpec(
            num_scalar_prefetch=1,
            grid=(2, 2),
            in_specs=arrived_specs(n, depth)
            + [rows, piece, piece, pl.BlockSpec((1, depth), lambda h, r, *_: (0, 0))],
            out_specs=[rows, rows, rows, pl.BlockSpec((8, depth), lambda h, r, *_: (0, 0))],
        ),
        out_shape=[
            jax.ShapeDtypeStruct((n, depth), low),
            jax.ShapeDtypeStruct((n, depth), wide),
            jax.ShapeDtypeStruct((n, depth), low),
            jax.ShapeDtypeStruct((8, depth), wide),
        ],
        compiler_params=params(),
        cost_estimate=cost(0, 0),
    )(early.astype(jnp.int32).reshape(1), *arrived, hidden, near, far, rate[None])


def settle_attention_back(arrived, direct, hidden, tokens, branch, rate):
    n, depth = hidden.shape
    block = n // 4

    def kernel(*refs):
        h = pl.program_id(0)
        direct_ref, token_ref, branch_ref, rate_ref, out_ref, grad_ref, term_ref = refs[5:]
        grad = direct_ref[...] + arrived_sum(h, *refs[:5])
        base, rates = token_ref[...].astype(wide), rate_ref[...]
        result, saved = settle_step(base, branch_ref[...], rates)
        back, branch_grad, terms = settle_back(grad, result, base, rates, saved)
        out_ref[...] = back
        grad_ref[...] = branch_grad.astype(low)

        start = (h == 0) & (pl.program_id(1) == 0)

        @pl.when(start)
        def _():
            term_ref[...] = rate_rows(terms)

        @pl.when(jnp.logical_not(start))
        def _():
            term_ref[...] += rate_rows(terms)

    rows = pl.BlockSpec((block, depth), lambda h, r: (2 * h + r, 0))
    return pl.pallas_call(
        kernel,
        grid=(2, 2),
        in_specs=arrived_specs(n, depth) + [rows] * 3 + [pl.BlockSpec((1, depth), lambda h, r: (0, 0))],
        out_specs=[rows, rows, pl.BlockSpec((8, depth), lambda h, r: (0, 0))],
        out_shape=[
            jax.ShapeDtypeStruct((n, depth), wide),
            jax.ShapeDtypeStruct((n, depth), low),
            jax.ShapeDtypeStruct((8, depth), wide),
        ],
        compiler_params=params(),
        cost_estimate=cost(0, 0),
    )(*arrived, direct, tokens, branch, rate[None])


def lay_rows(refs, out):
    @pl.when(pl.program_id(0) == 0)
    def _():
        at = 0
        for ref in refs:
            out[at : at + ref.shape[0], :] = ref[...]
            at += ref.shape[0]


def mlp_forward(blocks, up_w, gate_w, scales, total, first, earlier):
    n = sum(block.shape[0] for block in blocks)
    depth, units = up_w.shape
    tile = 2 * LANES
    count = len(blocks)

    def kernel(*refs):
        ins, rest = refs[:count], refs[count:]
        up_ref, gate_ref, scale_ref = rest[:3]
        mid_ref, act_all, act_out, up_out, gate_out = rest[-5:]
        lay_rows(ins, mid_ref)
        left = mid_ref[...]
        up = nn(left, up_ref[...])
        gate = nn(left, gate_ref[...])
        lifted = scale_ref[1:2, :] * gate
        up_out[...] = up.astype(low)
        gate_out[...] = gate.astype(low)
        act = (scale_ref[0:1, :] * up * (lifted * jax.nn.sigmoid(lifted))).astype(low)
        act_out[...] = act
        act_all[...] = act

    weight = pl.BlockSpec((depth, tile), lambda j: (0, j))
    alone = pl.BlockSpec((n, tile), lambda j: (0, j))
    return pl.pallas_call(
        kernel,
        grid=(units // tile,),
        in_specs=chunk_specs(blocks, depth)
        + [weight] * 2
        + [pl.BlockSpec((2, tile), lambda j: (0, j))]
        + [pl.BlockSpec(memory_space=pl.ANY)] * len(earlier),
        out_specs=[
            pl.BlockSpec((n, depth), lambda j: (first, 0)), pl.BlockSpec((n, tile), lambda j: (first, j)),
            alone, alone, alone,
        ],
        out_shape=[jax.ShapeDtypeStruct((total, depth), low), jax.ShapeDtypeStruct((total, units), low)]
        + [jax.ShapeDtypeStruct((n, units), low)] * 3,
        input_output_aliases={count + 3 + i: i for i in range(len(earlier))},
        compiler_params=params(),
        cost_estimate=cost(4 * n * depth * units, 2 * (2 * n * depth + 2 * depth * units + 3 * n * units)),
    )(*blocks, up_w, gate_w, scales, *earlier)


def mlp_backward(blocks, up_w, gate_w, down_w, scales, up_raw, gate_raw, total, first, earlier):
    n = sum(block.shape[0] for block in blocks)
    depth, units = up_w.shape
    tile = 2 * LANES
    count = len(blocks)
    steps = units // tile

    def kernel(*refs):
        ins, rest = refs[:count], refs[count:]
        down_ref, scale_ref, up_raw_ref, gate_raw_ref, up_ref, gate_ref = rest[:6]
        branch_ref, up_out, gate_out, part_ref, gain_ref, kept, weights, sems = rest[-8:]
        step = pl.program_id(0)
        fetches = [
            pltpu.make_async_copy(ref, weights.at[i], sems.at[i]) for i, ref in enumerate((up_ref, gate_ref))
        ]

        @pl.when(step == 0)
        def _():
            for fetch in fetches:
                fetch.start()

        lay_rows(ins, branch_ref)
        up_gain, gate_gain = scale_ref[0:1, :], scale_ref[1:2, :]
        grad = nn(branch_ref[...], down_ref[...])
        up = up_raw_ref[...].astype(wide)
        gate = gate_raw_ref[...].astype(wide)
        lifted = gate_gain * gate
        slope = jax.nn.sigmoid(lifted)
        swished = lifted * slope
        up_part = grad * swished
        lifted_grad = grad * up * (up_gain * (slope + swished * (1.0 - slope)))
        up_term = jnp.sum(up_part * up, axis=0, keepdims=True)
        gate_term = jnp.sum(lifted_grad * gate, axis=0, keepdims=True)
        up_low = (up_part * up_gain).astype(low)
        gate_low = (lifted_grad * gate_gain).astype(low)
        up_out[...] = up_low
        gate_out[...] = gate_low
        kept[0, step] = up_low
        kept[1, step] = gate_low
        gain_ref[...] = jnp.concatenate([up_term, gate_term, jnp.zeros((6, tile), wide)], axis=0)

        @pl.when(step == steps - 1)
        def _():
            for fetch in fetches:
                fetch.wait()
            ups, gates = (jnp.concatenate([kept[i, k] for k in range(steps)], axis=1) for i in range(2))
            for at in range(0, depth, tile):
                part = nt(ups, weights[0, at : at + tile, :]) + nt(gates, weights[1, at : at + tile, :])
                part_ref[:, at : at + tile] = part.astype(low)

    anywhere = pl.BlockSpec(memory_space=pl.ANY)
    tiles = pl.BlockSpec((n, tile), lambda j: (first, j))
    alone = pl.BlockSpec((n, tile), lambda j: (0, j))
    all_units = jax.ShapeDtypeStruct((total, units), low)
    return pl.pallas_call(
        kernel,
        grid=(steps,),
        in_specs=chunk_specs(blocks, depth)
        + [
            pl.BlockSpec((depth, tile), lambda j: (0, j)), pl.BlockSpec((2, tile), lambda j: (0, j)),
            alone, alone, anywhere, anywhere,
        ]
        + [anywhere] * len(earlier),
        out_specs=[
            pl.BlockSpec((n, depth), lambda j: (first, 0)), tiles, tiles,
            pl.BlockSpec((n, depth), lambda j: (0, 0)), pl.BlockSpec((8, tile), lambda j: (0, j)),
        ],
        out_shape=[
            jax.ShapeDtypeStruct((total, depth), low), all_units, all_units,
            jax.ShapeDtypeStruct((n, depth), low), jax.ShapeDtypeStruct((8, units), wide),
        ],
        scratch_shapes=[
            pltpu.VMEM((2, steps, n, tile), low), pltpu.VMEM((2, depth, units), low),
            pltpu.SemaphoreType.DMA((2,)),
        ],
        input_output_aliases={count + 6 + i: i for i in range(len(earlier))},
        compiler_params=params(),
        cost_estimate=cost(6 * n * depth * units, 2 * (2 * n * depth + 3 * depth * units + 4 * n * units)),
    )(*blocks, down_w, scales, up_raw, gate_raw, up_w, gate_w, *earlier)


def place(blocks, indices):
    ndim = 2
    n = len(indices)
    count = len(blocks)
    pieces = [
        (i, at) for i, block in enumerate(blocks) for at in ([None] if block.ndim == ndim else range(block.shape[0]))
    ]
    shape = blocks[0].shape[-ndim:]
    where_to = jnp.stack([jnp.asarray(i, jnp.int32) for i in indices])

    def kernel(index_ref, *refs):
        out, sems = refs[count], refs[count + 1]
        copies = []
        for k, (i, at) in enumerate(pieces):
            source = refs[i] if at is None else refs[i].at[at]
            copies.append(pltpu.make_async_copy(source, out.at[index_ref[k]], sems.at[k]))
        for copy in copies:
            copy.start()
        for copy in copies:
            copy.wait()

    anywhere = pl.BlockSpec(memory_space=pl.ANY)
    out = jax.ShapeDtypeStruct((n,) + shape, blocks[0].dtype)
    return pl.pallas_call(
        kernel,
        in_specs=[pl.BlockSpec(memory_space=pltpu.SMEM)] + [anywhere] * count,
        out_specs=pl.BlockSpec(memory_space=pltpu.VMEM),
        out_shape=out,
        scratch_shapes=[pltpu.SemaphoreType.DMA((n,))],
        compiler_params=params(),
        cost_estimate=cost(0, 2 * out.size * out.dtype.itemsize),
    )(where_to, *blocks)


def spread_pack(grad, extra, chip):
    _, _, rows, columns = grad.shape
    total = rows + extra.shape[0]
    tile = 2 * LANES

    def kernel(chip_ref, grad_ref, extra_ref, first, second, keep):
        plan = [(first, 1, 0), (first, 3, 0), (second, 2, 1), (second, 3, 1)]
        plan += [(keep, 0, 0), (keep, 0, 1), (keep, 2, 0), (keep, 1, 1)]
        used = {}
        for out, k, half in plan:
            slot = used.get(id(out), 0)
            used[id(out)] = slot + 1
            out[slot, :rows, :] = grad_ref[chip_ref[0] ^ k, half]
            out[slot, rows:, :] = extra_ref[...]

    def out(n):
        return pl.BlockSpec((n, total, tile), lambda j, *_: (0, 0, j))

    return pl.pallas_call(
        kernel,
        grid_spec=pltpu.PrefetchScalarGridSpec(
            num_scalar_prefetch=1,
            grid=(columns // tile,),
            in_specs=[
                pl.BlockSpec((CHIPS, 2, rows, tile), lambda j, *_: (0, 0, 0, j)),
                pl.BlockSpec((extra.shape[0], tile), lambda j, *_: (0, j)),
            ],
            out_specs=[out(2), out(2), out(4)],
        ),
        out_shape=[jax.ShapeDtypeStruct((n, total, columns), low) for n in (2, 2, 4)],
        compiler_params=params(),
        cost_estimate=cost(0, 0),
    )(chip.reshape(1), grad, extra.astype(low))


def spread_turn(first, second, keep):
    _, total, columns = first.shape
    tile = 2 * LANES

    def kernel(first_ref, second_ref, keep_ref, y_ref, x_ref):
        y_ref[...] = (keep_ref[2].astype(wide) + first_ref[1].astype(wide)).astype(low)
        x_ref[...] = (keep_ref[3].astype(wide) + second_ref[1].astype(wide)).astype(low)

    def spec(n):
        return pl.BlockSpec((n, total, tile), lambda j: (0, 0, j))

    out = pl.BlockSpec((total, tile), lambda j: (0, j))
    return pl.pallas_call(
        kernel,
        grid=(columns // tile,),
        in_specs=[spec(2), spec(2), spec(4)],
        out_specs=[out] * 2,
        out_shape=[jax.ShapeDtypeStruct((total, columns), low)] * 2,
        compiler_params=params(),
        cost_estimate=cost(0, 0),
    )(first, second, keep)


def spread_finish(first, second, keep, last_y, last_x, width, core):
    _, total, columns = first.shape
    out_width = columns // 2

    def kernel(core_ref, first_ref, second_ref, keep_ref, y_ref, x_ref, *outs):
        for half in range(2):
            got, last = ((first_ref, y_ref), (second_ref, x_ref))[half]
            value = keep_ref[half].astype(wide) + got[0].astype(wide) + last[...].astype(wide)
            for which in range(2):
                piece = jnp.concatenate(
                    [
                        value[:, at + which * width : at + (which + 1) * width]
                        for at in range(0, columns, 2 * width)
                    ],
                    axis=1,
                ).astype(low)
                for side in range(2):

                    @pl.when((core_ref[0] ^ side) == half)
                    def _(side=side, which=which, piece=piece):
                        outs[2 * side + which][...] = piece

    whole = pl.BlockSpec(memory_space=pltpu.VMEM)
    return pl.pallas_call(
        kernel,
        in_specs=[pl.BlockSpec(memory_space=pltpu.SMEM)] + [whole] * 5,
        out_specs=[whole] * 4,
        out_shape=[jax.ShapeDtypeStruct((total, out_width), low)] * 4,
        compiler_params=params(),
        cost_estimate=cost(0, 0),
    )(core.reshape(1), first, second, keep, last_y, last_x)


def half_tiles(first, second, first_upper, second_upper):
    first, second = first.astype(wide), second.astype(wide)
    axis = first.ndim - 1
    first = jnp.where(first_upper, pltpu.roll(first, HALF, axis), first)
    second = jnp.where(second_upper, second, pltpu.roll(second, HALF, axis))
    lane = lax.broadcasted_iota(jnp.int32, first.shape, axis)
    return jnp.where(lane < HALF, first, second).astype(low)


def unit_pack(groups):
    weights = [weight for group in groups for weight in group]
    rows, units = weights[0].shape
    main = units // CHIPS // LANES * LANES
    width = len(weights) * main + len(groups) * LANES

    def kernel(*refs):
        out, at, first = refs[-1], 0, 0
        target = pl.program_id(0)
        start = pl.multiple_of(target * main, LANES)
        tile = pl.multiple_of(CHIPS * main + (target // 2) * LANES, LANES)
        upper = (target & 1) == 1
        for group in groups:
            members = refs[first : first + len(group)]
            first += len(group)
            for ref in members:
                out[0, :, at : at + main] = ref[:, pl.ds(start, main)]
                at += main
            rests = [ref[:, pl.ds(tile, LANES)] for ref in members]
            out[0, :, at : at + LANES] = half_tiles(rests[0], rests[-1], upper, upper)
            at += LANES

    whole = pl.BlockSpec((rows, units), lambda k: (0, 0))
    return pl.pallas_call(
        kernel,
        grid=(CHIPS,),
        in_specs=[whole] * len(weights),
        out_specs=pl.BlockSpec((1, rows, width), lambda k: (k, 0, 0)),
        out_shape=jax.ShapeDtypeStruct((CHIPS, rows, width), weights[0].dtype),
        cost_estimate=cost(0, 0),
    )(*weights)


def unit_lay(n, mine, theirs, core):
    count, _, rows, columns = mine.shape
    main = (columns - LANES) // n
    units = count * main + count // 2 * LANES

    def kernel(core_ref, *refs):
        outs = refs[2:]
        for side in range(2):
            slot = core_ref[0] ^ side
            blocks = refs[side]
            for i in range(n):
                for k in range(count):
                    outs[i][slot, :, k * main : (k + 1) * main] = blocks[k, 0, :, i * main : (i + 1) * main]
                tile = n * main
                upper = i == 1
                for k in range(0, count, 2):
                    at = count * main + k // 2 * LANES
                    outs[i][slot, :, at : at + LANES] = half_tiles(
                        blocks[k, 0, :, tile : tile + LANES],
                        blocks[k + 1, 0, :, tile : tile + LANES],
                        upper,
                        upper,
                    )

    block = pl.BlockSpec((count, 1, rows, columns), lambda q: (0, q, 0, 0))
    out = pl.BlockSpec((2, rows, units), lambda q: (q, 0, 0))
    return pl.pallas_call(
        kernel,
        grid=(CHIPS,),
        in_specs=[pl.BlockSpec(memory_space=pltpu.SMEM)] + [block] * 2,
        out_specs=[out] * n,
        out_shape=[jax.ShapeDtypeStruct((2 * CHIPS, rows, units), low)] * n,
        compiler_params=params(),
        cost_estimate=cost(0, 14 * n * 8 * rows * units // 4),
    )(core.reshape(1), mine, theirs)


def unit_unlay(grads, n, core):
    count = lax.axis_size("tensor")
    _, rows, units = grads.shape
    units = units // n
    main = units // count // LANES * LANES
    columns = n * main + (n + 1) // 2 * LANES

    def kernel(core_ref, *refs):
        for side in range(2):
            slot = core_ref[0] ^ side
            out = refs[1 + side]
            for k in range(count):
                for i in range(n):
                    out[k, 0, :, i * main : (i + 1) * main] = refs[0][slot, :, i * units + k * main : i * units + (k + 1) * main]
                at = count * main + k // 2 * LANES
                upper = k % 2 == 1
                rests = [refs[0][slot, :, i * units + at : i * units + at + LANES] for i in range(n)]
                for i in range(0, n, 2):
                    to = n * main + i // 2 * LANES
                    out[k, 0, :, to : to + LANES] = half_tiles(
                        rests[i], rests[min(i + 1, n - 1)], upper, upper
                    )

    block = pl.BlockSpec((2, rows, n * units), lambda q: (q, 0, 0))
    return pl.pallas_call(
        kernel,
        grid=(CHIPS,),
        in_specs=[pl.BlockSpec(memory_space=pltpu.SMEM)] + [block],
        out_specs=[pl.BlockSpec((count, 1, rows, columns), lambda q: (0, q, 0, 0))] * 2,
        out_shape=[jax.ShapeDtypeStruct((count, CHIPS, rows, columns), low)] * 2,
        compiler_params=params(),
        cost_estimate=cost(0, 14 * n * 8 * rows * units // 4),
    )(core.reshape(1), grads)


def unit_unpack(n, blocks):
    _, rows, columns = blocks.shape
    main = (columns - (n + 1) // 2 * LANES) // n
    units = CHIPS * main + CHIPS // 2 * LANES

    def kernel(block_ref, *outs):
        for i in range(n):
            for j in range(CHIPS):
                outs[i][:, j * main : (j + 1) * main] = block_ref[j, :, i * main : (i + 1) * main].astype(wide)
            tile = n * main + i // 2 * LANES
            upper = i % 2 == 1
            for j in range(0, CHIPS, 2):
                at = CHIPS * main + j // 2 * LANES
                outs[i][:, at : at + LANES] = half_tiles(
                    block_ref[j, :, tile : tile + LANES], block_ref[j + 1, :, tile : tile + LANES], upper, upper
                ).astype(wide)

    return pl.pallas_call(
        kernel,
        out_shape=[jax.ShapeDtypeStruct((rows, units), wide)] * n,
        compiler_params=params(),
    )(blocks)


def per_device(
    block_in, out_grad, global_pos,
    w_query, w_key, w_value, w_out, w_up, w_gate, w_down,
    qk_gain, up_gain, gate_gain, att_rate, mlp_rate,
):
    count = lax.axis_size("tensor")
    plane = lax.axis_size(DP)
    micro_count, _, local_rows, model_width = block_in.shape
    assert micro_count == 2 and count == 4
    seq_len = local_rows * count
    head_width = w_query.shape[1]
    core_heads = head_width * 2
    unit_width = w_up.shape[1]
    plane_unit = unit_width // CHIPS
    main = plane_unit // LANES * LANES
    rest = plane_unit - main
    me = lax.axis_index(DP)
    z = lax.axis_index("tensor")
    core = me & 1
    chip = (me >> 1) & 3
    early = z < 2

    def across(value, pairs):
        return lax.ppermute(
            value, ALL, [(a * count + b, c * count + d) for (a, b), (c, d) in pairs]
        )

    def home(far):
        return [
            ((p, t), ((p & ~1) | (t & 1), ((t & 2) ^ (2 if far else 0)) | (p & 1)))
            for p in range(plane)
            for t in range(count)
        ]

    def seq_near(value):
        return across(lax.dynamic_index_in_dim(value, z >> 1, 0, keepdims=False), home(False))

    def seq_far(value):
        return across(lax.dynamic_index_in_dim(value, 1 - (z >> 1), 0, keepdims=False), home(True))

    def seq_join(near, far):
        return pick(early, jnp.concatenate([near, far]), jnp.concatenate([far, near]))

    def from_sequence(value):
        first, second = value[:local_rows], value[local_rows:]
        near = across(pick(early, first, second), [(b, a) for a, b in home(False)])
        far = across(pick(early, second, first), [(b, a) for a, b in home(True)])
        return near, far

    def by_micro(near, far):
        return pick(early, jnp.stack([near, far]), jnp.stack([far, near])).astype(wide)

    def both_cores(value):
        value = value.reshape(2, local_rows, model_width)
        return place([value, swap(value, 1)], [core, core + 2, 1 - core, 3 - core]).reshape(
            seq_len, model_width
        )

    def core_scatter(partial):
        split = partial.reshape(2, 2, local_rows, model_width)
        got = swap(lax.dynamic_index_in_dim(split, 1 - core, 1, keepdims=False), 1)
        mine = lax.dynamic_index_in_dim(split, core, 1, keepdims=False)
        return (mine.astype(wide) + got.astype(wide)).reshape(2 * local_rows, model_width)

    def head_pairs(other_core, second):
        return [
            ((p ^ other_core, (t + 2 * (p & 1) + second) % count), (p, t))
            for p in range(plane)
            for t in range(count)
        ]

    def paired(a, b):
        return jnp.concatenate(
            [a[..., :head_width], b[..., :head_width], a[..., head_width:], b[..., head_width:]], axis=-1
        )

    def attn_fetch(first, second):
        packed = outer_gather(jnp.concatenate([first, second], axis=1))
        groups = [[across(packed, head_pairs(side, which)) for which in range(2)] for side in range(2)]
        return jnp.stack([paired(*pair) for pair in groups])

    def attn_pair(first, second, extra):
        packed = jnp.concatenate([outer_gather(jnp.concatenate([first, second], axis=1)), extra])
        return jnp.stack([packed, swap(packed, 1)])

    def attn_fetch_packed(packed, rows):
        groups = [across(packed, head_pairs(0, which)) for which in range(2)]
        sides = [
            paired(*(group[:, :rows, at : at + head_width] for group in groups))
            for at in range(0, packed.shape[2], head_width)
        ]
        return *sides, [group[0, rows:] for group in groups]

    def attn_first(sides):
        return sides, swap(sides, 2), swap(sides, 4)

    def attn_second(first):
        sides, along_x, along_y = first
        return sides, along_x, along_y, swap(along_y[0], 2), swap(along_x[1], 4)

    def attn_lay(blocks):
        return full_rows(place(blocks, [2 * (chip ^ (i // 2)) + (core ^ (i % 2)) for i in range(8)]))

    def attn_pack(packed, extra):
        grad = plane_rows(packed).reshape(CHIPS, 2, -1, packed.shape[1])
        return spread_pack(grad, extra, chip)

    def attn_send(messages):
        first, second, keep = messages
        return swap(first, 2), swap(second, 4), keep

    def attn_turn(messages):
        to_y, to_x = messages
        return swap(to_y, 4), swap(to_x, 2)

    def attn_scatter(sent, turned):
        pieces = spread_finish(*sent, *turned, head_width, core)
        return [
            across(pieces[2 * side + which], [(b, a) for a, b in head_pairs(side, which)])
            for side in range(2)
            for which in range(2)
        ]

    def attn_join(got, extra_rows):
        got = [piece.astype(wide) for piece in got]
        rows = got[0].shape[0] - extra_rows
        small = jnp.stack([piece[rows:] for piece in got])
        extra = jnp.zeros(small.shape[1:], wide)
        for t in range(count):
            back = (z - t) % count
            index = 2 * ((back >> 1) ^ core) + (back & 1)
            extra = extra + lax.dynamic_index_in_dim(small, index, 0, keepdims=False)
        return attn_own(sum(piece[:rows] for piece in got), extra)

    def attn_own(grads, extra):
        grads = outer_scatter(grads)
        bit = 8
        while bit < plane:
            extra = extra + swap(extra, bit)
            bit *= 2
        return grads[:, :head_width], grads[:, head_width:], extra

    def unit_join(n, mine):
        return [full_rows(w) for w in unit_lay(n, mine, swap(mine, 1), core)]

    def unit_collect(grads):
        keep, send = unit_unlay([plane_rows(g) for g in grads], core)
        return add_low(keep, swap(send, 1))

    def unit_return(n, total):
        return [outer_scatter(g) for g in unit_unpack(n, lax.all_to_all(total, "chip", 0, 0, tiled=True))]

    tie = lax.optimization_barrier

    def halved(value):
        upper_part = lax.reduce_precision(value, 8, 7)
        return jnp.stack([upper_part, value - upper_part]).astype(low)

    qk_sides = attn_fetch(w_query, w_key)
    unit_blocks = unit_pack([[outer_gather(w_up), outer_gather(w_gate)]])
    mains = lax.dynamic_slice_in_dim(jnp.stack([up_gain, gate_gain]), chip * main, main, 1)
    rests = lax.dynamic_slice_in_dim(jnp.stack([up_gain, gate_gain]), CHIPS * main + chip * rest, rest, 1)
    unit_gains = halved(jnp.concatenate([mains, rests], axis=1).reshape(-1))
    gain_rows = jnp.concatenate(
        [unit_gains, halved(qk_gain).reshape(1, -1), jnp.zeros((13, 2 * head_width), low)]
    )
    vo_packed = attn_pair(w_value, w_out, gain_rows)
    places_here = global_pos[:, 0]
    places_there = swap(places_here, 1)
    qk_sides, vo_packed, places_there, unit_blocks, block_in = tie(
        (qk_sides, vo_packed, places_there, unit_blocks, block_in)
    )
    qk_first = attn_first(qk_sides)
    value_sides, out_sides, gain_groups = attn_fetch_packed(vo_packed, qk_sides.shape[1])
    near = seq_near(block_in[:, 0])
    qk_first, value_sides, out_sides, gain_groups, near, block_in, unit_blocks = tie(
        (qk_first, value_sides, out_sides, gain_groups, near, block_in, unit_blocks)
    )
    ug_laid = lax.all_to_all(unit_blocks, "chip", 0, 0, tiled=True)
    lower, upper_rows = block_in[:, 0, : local_rows // 2], block_in[:, 0, local_rows // 2 :]
    far_first, upper_rows = tie((seq_far(lower), upper_rows))
    far = jnp.concatenate([far_first, seq_far(upper_rows)])
    qk_w = attn_lay(attn_second(qk_first))
    value_w = attn_lay(attn_second(attn_first(value_sides)))
    qk_w, value_w, out_sides, gain_groups, far, near, ug_laid, w_down = tie(
        (qk_w, value_w, out_sides, gain_groups, far, near, ug_laid, w_down)
    )
    down_laid = lax.all_to_all(unit_pack([[outer_gather(w_down)]]), "chip", 0, 0, tiled=True)
    gain_here = jnp.stack(gain_groups)[:, :2].astype(wide).sum(axis=1)
    gain_there = swap(gain_here, 1)
    out_across = [out_sides] + [swap(out_sides, 2 * k) for k in range(1, CHIPS)]
    tokens = seq_join(near, far)
    sequence = both_cores(tokens)
    ug_shifted = lax.all_gather(ug_laid, "tensor")
    unit_gains = pick(
        core == 0, jnp.concatenate([gain_here, gain_there]), jnp.concatenate([gain_there, gain_here])
    )
    unit_gains = lax.dynamic_slice_in_dim(jnp.concatenate([unit_gains, unit_gains]), count - z, count, 0)
    unit_gains = unit_gains.reshape(count, 2, plane_unit).transpose(1, 0, 2)
    scales = jnp.concatenate(
        [unit_gains[..., :main].reshape(2, -1), unit_gains[..., main:].reshape(2, -1)], axis=1
    )
    head_gain = jnp.stack(gain_groups)[:, 2].astype(wide).reshape(2, 2, head_width).sum(axis=1)
    head_gain = head_gain.reshape(core_heads)
    places = lax.dynamic_index_in_dim(
        pick((z & 1) == core, places_here, places_there), z >> 1, 0, keepdims=False
    )
    flags = jnp.any(places[:, None] == jnp.arange(seq_len, dtype=jnp.int32)[None, :], axis=0).astype(wide)
    flag_row, flag_col = flags[None], flags[:, None]

    heads, raw = project_heads(sequence, qk_w, jnp.concatenate([head_gain, head_gain]))
    value_rows = product(sequence, value_w)
    mixed, lse = attend_forward(heads, value_rows, flag_row, flag_col)
    mixed, out_across, down_laid = tie((mixed, out_across, down_laid))
    down_shifted = lax.all_gather(down_laid, "tensor")
    out_w = attn_lay(out_across)
    partial = sum_back([(mixed, 0, core_heads)], [(out_w, 0, core_heads)])
    partial = partial.reshape(2, 2, local_rows, model_width)
    got = swap(lax.dynamic_index_in_dim(partial, 1 - core, 1, keepdims=False), 1)
    hidden, hidden_low, att_branch = settle_attention(partial, got, tokens, att_rate, core)

    own_rows = 2 * local_rows
    all_rows = CHIPS * own_rows
    hidden_low, ug_shifted = tie((hidden_low, ug_shifted))
    first = plane_first(hidden_low)
    up_w, gate_w = unit_join(2, ug_shifted)
    earlier, saved, acts = (), [], []

    def forward(blocks, at):
        nonlocal earlier
        *earlier, act, up_raw, gate_raw = mlp_forward(blocks, up_w, gate_w, scales, all_rows, at, earlier)
        saved.append((up_raw, gate_raw))
        return act

    def back(act):
        return sum_back([(act, 0, act.shape[1])], [(down_w, 0, act.shape[1])])

    def by_chip(own, both, diagonal):
        return [own, both[:own_rows], both[own_rows:], diagonal]

    act_own = forward([hidden_low], 2)
    out_grad_low = out_grad[:, 0].astype(low)
    first, act_own, out_grad_low = tie((first, act_own, out_grad_low))
    _, along_x, along_y, *diagonal = plane_second(first)
    act_both = forward([along_x, along_y], 0)
    diagonal, act_both, down_shifted = tie((diagonal, act_both, down_shifted))
    (down_w,) = unit_join(1, down_shifted)
    act_diagonal = forward(diagonal, 3)
    mid, activated = earlier
    parts = [back(act) for act in (act_own, act_both, act_diagonal)]
    parts, out_grad_low = tie((parts, out_grad_low))
    sent, _ = scatter_first(by_chip(*parts))
    cotangent = seq_near(out_grad_low), seq_far(out_grad_low)
    sent, cotangent = tie((sent, cotangent))
    block_rows, direct, branch_grad, mlp_rate_term = settle_units(
        scatter_last(sent), hidden, *cotangent, early, mlp_rate
    )

    first = plane_first(branch_grad)
    returned = from_sequence(block_rows)
    earlier, unit_terms = (), []

    def backward(blocks, at, raws):
        nonlocal earlier
        *earlier, part, unit_term = mlp_backward(
            blocks, up_w, gate_w, down_w, scales, *raws, all_rows, at, earlier
        )
        unit_terms.append(unit_term[:2])
        return part

    part_own = backward([branch_grad], 2, saved[0])
    first, part_own = tie((first, part_own))
    _, along_x, along_y, *diagonal = plane_second(first)
    part_both = backward([along_x, along_y], 0, saved[1])
    diagonal, part_both, returned = tie((diagonal, part_both, returned))
    part_diagonal = backward(diagonal, 3, saved[2])
    branch, up_low, gate_low = earlier
    sent, (branch, mid) = scatter_first(by_chip(part_own, part_both, part_diagonal), (branch, mid))
    down_blocks = unit_unlay(plane_rows(rows_product([(branch, [activated])], 2 * LANES)), 1, core)
    ug_grad = rows_product([(mid, [up_low, gate_low])], 2 * LANES)
    small = jnp.concatenate([sum(unit_terms), mlp_rate_term[:1]])
    small = small + swap(small, 1)
    sent, down_blocks, ug_grad, small = tie((sent, down_blocks, ug_grad, small))
    arrived = scatter_last(sent)
    down_blocks = add_low(down_blocks[0], swap(down_blocks[1], 1))
    ug_blocks = unit_unlay(plane_rows(ug_grad), 2, core)
    def rate_rows_of(term):
        rows = jnp.broadcast_to(term.reshape(2, 2, 1, head_width), (2, 2, 2, head_width))
        return jnp.where(own_chip[..., None], rows.reshape(1, 2, 4 * head_width), 0.0).reshape(2 * CHIPS, -1)

    own_chip = jnp.arange(CHIPS)[:, None] == chip
    empty_rows = jnp.zeros((EXTRA - 3 * CHIPS, 4 * head_width), wide)
    unit_rows = jnp.concatenate(
        [small[:2, : count * main].reshape(2, count, main), small[:2, count * main :].reshape(2, count, rest)],
        axis=2,
    )
    unit_rows = lax.dynamic_slice_in_dim(
        jnp.concatenate([unit_rows, unit_rows], axis=1), z + 2 * core, 2, 1
    ).reshape(1, 4 * plane_unit)
    vo_extra = jnp.concatenate([jnp.where(own_chip, unit_rows, 0.0), rate_rows_of(small[2:]), empty_rows])
    vo_extra = vo_extra.astype(low)
    arrived, ug_blocks, down_blocks, vo_extra = tie((arrived, ug_blocks, down_blocks, vo_extra))
    down_back = lax.psum_scatter(down_blocks, "tensor", scatter_dimension=0)
    ug_there = swap(ug_blocks[1], 1)
    input_direct, att_grad, att_rate_term = settle_attention_back(
        arrived, direct, hidden, tokens, att_branch, att_rate
    )
    att_low = both_cores(att_grad)
    ug_blocks = add_low(ug_blocks[0], ug_there)
    att_low, ug_blocks = tie((att_low, ug_blocks))
    ug_back = lax.psum_scatter(ug_blocks, "tensor", scatter_dimension=0)
    mixed_grad = product(att_low, out_w)
    heads_low, vraw_low, head_terms = attend_backward(
        heads, raw, value_rows, mixed, mixed_grad, lse, head_gain, flag_row, flag_col
    )
    block_out = by_micro(*returned)

    heads_low, vraw_low, down_back = tie((heads_low, vraw_low, down_back))
    vo_grad = rows_product([(sequence, [vraw_low]), (att_low, [mixed])], core_heads)
    vo_messages, vraw_low = tie((attn_pack(vo_grad, vo_extra), vraw_low))
    vo_sent = attn_send(vo_messages)
    in_part = sum_back(
        [(heads_low, 0, 2 * core_heads), (vraw_low, 0, core_heads)],
        [(qk_w, 0, 2 * core_heads), (value_w, 0, core_heads)],
    )
    vo_sent, heads_low, in_part, ug_back, block_out = tie((vo_sent, heads_low, in_part, ug_back, block_out))
    att_term = att_rate_term[:1] + swap(att_rate_term[:1], 1)
    vo_messages, heads_low, in_part, att_term = tie((spread_turn(*vo_sent), heads_low, in_part, att_term))
    qk_extra = jnp.concatenate(
        [
            jnp.where(own_chip, head_terms[:2].reshape(1, 4 * head_width), 0.0),
            rate_rows_of(att_term),
            empty_rows,
        ]
    )
    vo_turned = attn_turn(vo_messages)
    in_rows = (input_direct + core_scatter(in_part)).astype(low)
    qk_messages = attn_pack(rows_product([(sequence, [heads_low])], 2 * LANES), qk_extra)
    vo_turned, in_rows, qk_messages = tie((vo_turned, in_rows, qk_messages))
    qk_sent = attn_send(qk_messages)
    returned_in = from_sequence(in_rows)
    vo_got = attn_scatter(vo_sent, vo_turned)
    qk_sent, down_back, ug_back = tie((qk_sent, down_back, ug_back))
    qk_turned = attn_turn(spread_turn(*qk_sent))
    (grad_down,) = unit_return(1, down_back)
    qk_turned, returned_in, vo_got, grad_down = tie((qk_turned, returned_in, vo_got, grad_down))
    qk_got = attn_scatter(qk_sent, qk_turned)
    grad_up, grad_gate = unit_return(2, ug_back)
    in_grad = by_micro(*returned_in)
    vo_got, qk_got = tie((vo_got, qk_got))
    grad_value, grad_out, vo_small = attn_join(vo_got, EXTRA)
    grad_query, grad_key, qk_small = attn_join(qk_got, EXTRA)

    units = vo_small[:CHIPS].reshape(CHIPS, 2, plane_unit).transpose(1, 0, 2)
    units = jnp.concatenate([units[..., :main].reshape(2, -1), units[..., main:].reshape(2, -1)], axis=1)
    mlp_total, att_total = (
        jnp.sum(member[CHIPS : 3 * CHIPS].reshape(CHIPS, model_width), axis=0) for member in (vo_small, qk_small)
    )
    head_sums = jnp.sum(qk_small[:CHIPS], axis=0)
    grad_qk_gain = head_sums[:head_width] + head_sums[head_width:]
    return (
        block_out[:, None], in_grad[:, None],
        grad_query, grad_key, grad_value, grad_out, grad_up, grad_gate, grad_down,
        grad_qk_gain, units[0], units[1], att_total, mlp_total,
    )


def solution(mesh):
    shape = dict(mesh.shape)
    plane, count = shape["dp"], shape["tensor"]
    split = Mesh(mesh.devices.reshape(plane // 8, CHIPS, 2, count), ALL)
    tokens = P(None, DP, "tensor", None)
    matrix = P(DP, "tensor")
    in_specs = (tokens, tokens, P(None, DP, None)) + (matrix,) * 7 + (P("tensor"),) * 3 + (P(), P())
    out_specs = (tokens, tokens) + (matrix,) * 7 + (P("tensor"),) * 3 + (P(), P())
    return jax.shard_map(
        per_device, mesh=split, in_specs=in_specs, out_specs=out_specs, check_vma=False
    )
```

```python
import math

import jax
import jax.numpy as jnp
from jax import lax
from jax.experimental import pallas as pl
from jax.experimental.pallas import tpu as pltpu
from jax.sharding import Mesh, PartitionSpec as P

HD = 64
WINDOW = 512
CHIPS = 4
LANES = 128
HALF = 64
EXTRA = 16
BLOCK = 256
VMEM_LIMIT = 48 * 2**20

DP = ("outer", "chip", "core")
ALL = DP + ("tensor",)

epsilon = 1e-06
blocked = -1e30
low = jnp.bfloat16
wide = jnp.float32


def swap(value, bit):
    count = lax.axis_size(DP)
    return lax.ppermute(value, DP, [(i, i ^ bit) for i in range(count)])


def pick(flag, when_true, when_false):
    return jnp.where(flag, when_true, when_false)


def outer_gather(value):
    me = lax.axis_index(DP)
    bit = 8
    while bit < lax.axis_size(DP):
        other = swap(value, bit)
        upper = (me & bit) != 0
        value = pick(
            upper, jnp.concatenate([other, value]), jnp.concatenate([value, other])
        )
        bit *= 2
    return value


def outer_scatter(value):
    me = lax.axis_index(DP)
    bit = lax.axis_size(DP) // 2
    while bit >= 8:
        rows = value.shape[0] // 2
        upper = (me & bit) != 0
        keep = pick(upper, value[rows:], value[:rows])
        send = pick(upper, value[:rows], value[rows:])
        value = (keep.astype(wide) + swap(send, bit).astype(wide)).astype(value.dtype)
        bit //= 2
    return value


def full_rows(value):
    outer = lax.axis_size(DP) // 8
    count, rows, columns = value.shape
    if outer > 1:
        value = value.reshape(count, outer, rows // outer, columns).transpose(1, 0, 2, 3)
    return value.reshape(count * rows, columns)


def plane_rows(value):
    outer = lax.axis_size(DP) // 8
    total, columns = value.shape
    if outer > 1:
        value = value.reshape(outer, 8, total // 8 // outer, columns).transpose(1, 0, 2, 3)
    return value.reshape(8, total // 8, columns)


def plane_first(value):
    return value, swap(value, 2), swap(value, 4)


def plane_second(first):
    value, along_x, along_y = first
    half = value.shape[0] // 2
    return value, along_x, along_y, swap(along_y[:half], 2), swap(along_x[half:], 4)


def scatter_first(blocks, then=()):
    own, along_x, along_y, diagonal = blocks
    half = own.shape[0] // 2
    first, second, then = lax.optimization_barrier(
        (
            jnp.concatenate([along_x[:half], diagonal[:half]]),
            jnp.concatenate([along_y[half:], diagonal[half:]]),
            then,
        )
    )
    return (blocks, swap(first, 2), swap(second, 4)), then


def scatter_last(sent):
    (own, along_x, along_y, _), first, second = sent
    half = own.shape[0] // 2
    next_y = (along_y[:half].astype(wide) + first[half:].astype(wide)).astype(low)
    next_x = (along_x[half:].astype(wide) + second[half:].astype(wide)).astype(low)
    return own, first, second, swap(next_y, 4), swap(next_x, 2)


def scatter_second(sent):
    own, first, second, last_y, last_x = scatter_last(sent)
    half = own.shape[0] // 2
    top = own[:half].astype(wide) + first[:half].astype(wide) + last_y.astype(wide)
    bottom = own[half:].astype(wide) + second[:half].astype(wide) + last_x.astype(wide)
    return jnp.concatenate([top, bottom])


def nt(left, right):
    return lax.dot_general(left, right, (((1,), (1,)), ((), ())), preferred_element_type=wide)


def nn(left, right):
    return lax.dot_general(left, right, (((1,), (0,)), ((), ())), preferred_element_type=wide)


def tn(left, right):
    return lax.dot_general(left, right, (((0,), (0,)), ((), ())), preferred_element_type=wide)


def params():
    return pltpu.CompilerParams(vmem_limit_bytes=VMEM_LIMIT)


def cost(flops, moved):
    return pl.CostEstimate(flops=1, bytes_accessed=1, transcendentals=0)


def head_means(width):
    rows = lax.broadcasted_iota(jnp.int32, (width, width), 0) // HD
    columns = lax.broadcasted_iota(jnp.int32, (width, width), 1) // HD
    return jnp.where(rows == columns, 1.0 / HD, 0.0).astype(low)


def head_scale(raw, means):
    return lax.rsqrt(nn((raw * raw).astype(low), means) + epsilon)


def project_heads(rows, weight, gain):
    n, depth = rows.shape
    width = weight.shape[1]
    tile = 2 * LANES
    block = 512

    def kernel(rows_ref, weight_ref, gain_ref, out_ref, raw_ref):
        means = head_means(tile)
        for start in range(0, n, block):
            span = slice(start, start + block)
            raw = nn(rows_ref[span, :], weight_ref[...])
            raw_ref[span, :] = raw.astype(low)
            out_ref[span, :] = (raw * head_scale(raw, means) * gain_ref[...]).astype(low)

    out = pl.BlockSpec((n, tile), lambda j: (0, j))
    return pl.pallas_call(
        kernel,
        grid=(width // tile,),
        in_specs=[
            pl.BlockSpec((n, depth), lambda j: (0, 0)),
            pl.BlockSpec((depth, tile), lambda j: (0, j)),
            pl.BlockSpec((1, tile), lambda j: (0, j)),
        ],
        out_specs=[out, out],
        out_shape=[jax.ShapeDtypeStruct((n, width), low)] * 2,
        compiler_params=params(),
        cost_estimate=cost(2 * n * depth * width, 2 * (n * depth + depth * width + 2 * n * width)),
    )(rows, weight, gain[None])


def fill_bias(bias, flag_row, flag_col):
    @pl.when(pl.program_id(0) == 0)
    def _():
        for i in range(bias.shape[0] // BLOCK):
            for j in range(i + 1):
                keys = slice(j * BLOCK, (j + 1) * BLOCK)
                rows = slice(i * BLOCK, (i + 1) * BLOCK)
                key_ids = j * BLOCK + lax.broadcasted_iota(jnp.int32, (BLOCK, BLOCK), 0)
                row_ids = i * BLOCK + lax.broadcasted_iota(jnp.int32, (BLOCK, BLOCK), 1)
                flagged = jnp.maximum(flag_row[:, rows], flag_col[keys, :]) > 0.5
                allow = (key_ids <= row_ids) & ((row_ids - key_ids < WINDOW) | flagged)
                bias[keys, rows] = jnp.where(allow, 0.0, blocked)


def head_lanes(value, head):
    lane = lax.broadcasted_iota(jnp.int32, value.shape, 1)
    mine = (lane < HD) if head == 0 else (lane >= HD)
    return jnp.where(mine, value, jnp.zeros_like(value))


def flag_specs(seq_len):
    return [pl.BlockSpec((1, seq_len), lambda h: (0, 0)), pl.BlockSpec((seq_len, 1), lambda h: (0, 0))]


def attend_forward(heads, value_rows, flag_row, flag_col):
    seq_len, width = value_rows.shape
    pairs = width // LANES

    def kernel(q_ref, k_ref, v_ref, row_ref, col_ref, out_ref, lse_ref, bias, turned):
        fill_bias(bias, row_ref, col_ref)
        turned[...] = v_ref[...].astype(wide).T.astype(low)
        for i in range(seq_len // BLOCK):
            rows = slice(i * BLOCK, (i + 1) * BLOCK)
            reach = (i + 1) * BLOCK
            block = q_ref[rows, :] * jnp.asarray(1.0 / math.sqrt(HD), low)
            halves = []
            for head in range(2):
                scores = nt(k_ref[:reach, :], head_lanes(block, head)) + bias[:reach, rows]
                raised = jnp.exp(scores)
                total = jnp.sum(raised, axis=0, keepdims=True)
                mixed = nn(turned[head * HD : (head + 1) * HD, :reach], raised.astype(low))
                halves.append(mixed / total)
                lse_ref[0, head : head + 1, rows] = jnp.log(total)
            out_ref[rows, :] = jnp.concatenate(halves, axis=0).T.astype(low)

    block = pl.BlockSpec((seq_len, LANES), lambda h: (0, h))
    keys = pl.BlockSpec((seq_len, LANES), lambda h: (0, pairs + h))
    return pl.pallas_call(
        kernel,
        grid=(pairs,),
        in_specs=[block, keys, block] + flag_specs(seq_len),
        out_specs=[block, pl.BlockSpec((1, 8, seq_len), lambda h: (h, 0, 0))],
        out_shape=[
            jax.ShapeDtypeStruct((seq_len, width), low),
            jax.ShapeDtypeStruct((pairs, 8, seq_len), wide),
        ],
        scratch_shapes=[pltpu.VMEM((seq_len, seq_len), wide), pltpu.VMEM((LANES, seq_len), low)],
        compiler_params=params(),
        cost_estimate=cost(16 * seq_len * seq_len * width, 10 * seq_len * width),
    )(heads, heads, value_rows, flag_row, flag_col)


def attend_backward(heads, raw, value_rows, mixed, mixed_grad, lse, gain, flag_row, flag_col):
    seq_len, width = value_rows.shape
    pairs = width // LANES
    scale = 1.0 / math.sqrt(HD)

    def unnorm(grad, raw_block, gain_row, means):
        raw_block = raw_block.astype(wide)
        factor = head_scale(raw_block, means)
        normed = raw_block * factor
        term = jnp.sum(grad * normed, axis=0, keepdims=True)
        grad = grad * gain_row
        inner = nn((grad * normed).astype(low), means)
        return (factor * (grad - normed * inner)).astype(low), term

    def kernel(
        q_ref, k_ref, v_ref, qraw_ref, kraw_ref, m_ref, g_ref, lse_ref, gain_ref, row_ref, col_ref,
        heads_ref, dv_ref, term_ref, bias, turned, key_total, value_total, dq_ref, dk_ref, sems,
    ):
        step = pl.program_id(0)

        def stores(pair):
            return [
                pltpu.make_async_copy(
                    ref, heads_ref.at[:, pl.ds(pl.multiple_of((side * pairs + pair) * LANES, LANES), LANES)], sems.at[side]
                )
                for side, ref in enumerate((dq_ref, dk_ref))
            ]

        @pl.when(step > 0)
        def _():
            for store in stores(step - 1):
                store.wait()

        fill_bias(bias, row_ref, col_ref)
        turned[...] = k_ref[...].astype(wide).T.astype(low)
        means = head_means(LANES)
        gain_row = gain_ref[...]
        query_term = key_term = jnp.zeros((1, LANES), wide)
        count = seq_len // BLOCK
        for i in reversed(range(count)):
            rows = slice(i * BLOCK, (i + 1) * BLOCK)
            reach = (i + 1) * BLOCK
            block = q_ref[rows, :] * jnp.asarray(scale, low)
            grads = g_ref[rows, :]
            products = (grads.astype(wide) * m_ref[rows, :].astype(wide)).T
            halves = []
            key_parts = value_parts = None
            for head in range(2):
                inner = jnp.sum(products[head * HD : (head + 1) * HD], axis=0, keepdims=True)
                query = head_lanes(block, head)
                grad = head_lanes(grads, head)
                scores = nt(k_ref[:reach, :], query) + bias[:reach, rows]
                probs = jnp.exp(scores - lse_ref[0, head : head + 1, rows])
                prob_grad = nt(v_ref[:reach, :], grad)
                score_grad = (probs * (prob_grad - inner)).astype(low)
                halves.append(nn(turned[head * HD : (head + 1) * HD, :reach], score_grad))
                key_part = nn(score_grad, query)
                value_part = nn(probs.astype(low), grad)
                key_parts = key_part if key_parts is None else key_parts + key_part
                value_parts = value_part if value_parts is None else value_parts + value_part
            if i == count - 1:
                key_total[...] = key_parts
                value_total[...] = value_parts
            else:
                key_total[:reach, :] += key_parts
                value_total[:reach, :] += value_parts
            query_grad = jnp.concatenate(halves, axis=0).T * scale
            dq_ref[rows, :], term = unnorm(query_grad, qraw_ref[rows, :], gain_row, means)
            query_term = query_term + term
        dv_ref[...] = value_total[...].astype(low)
        for i in range(count):
            rows = slice(i * BLOCK, (i + 1) * BLOCK)
            dk_ref[rows, :], term = unnorm(key_total[rows, :], kraw_ref[rows, :], gain_row, means)
            key_term = key_term + term
        term_ref[...] = jnp.concatenate([query_term, key_term, jnp.zeros((6, LANES), wide)], axis=0)
        for store in stores(step):
            store.start()

        @pl.when(step == pairs - 1)
        def _():
            for store in stores(step):
                store.wait()

    block = pl.BlockSpec((seq_len, LANES), lambda h: (0, h))
    keys = pl.BlockSpec((seq_len, LANES), lambda h: (0, pairs + h))
    return pl.pallas_call(
        kernel,
        grid=(pairs,),
        in_specs=[block, keys, block, block, keys, block, block]
        + [pl.BlockSpec((1, 8, seq_len), lambda h: (h, 0, 0)), pl.BlockSpec((1, LANES), lambda h: (0, h))]
        + flag_specs(seq_len),
        out_specs=[pl.BlockSpec(memory_space=pl.ANY), block, pl.BlockSpec((8, LANES), lambda h: (0, h))],
        out_shape=[
            jax.ShapeDtypeStruct((seq_len, 2 * width), low),
            jax.ShapeDtypeStruct((seq_len, width), low),
            jax.ShapeDtypeStruct((8, width), wide),
        ],
        scratch_shapes=[
            pltpu.VMEM((seq_len, seq_len), wide),
            pltpu.VMEM((LANES, seq_len), low),
            pltpu.VMEM((seq_len, LANES), wide),
            pltpu.VMEM((seq_len, LANES), wide),
            pltpu.VMEM((seq_len, LANES), low),
            pltpu.VMEM((seq_len, LANES), low),
            pltpu.SemaphoreType.DMA((2,)),
        ],
        compiler_params=params(),
        cost_estimate=cost(32 * seq_len * seq_len * width, 20 * seq_len * width),
    )(heads, heads, value_rows, raw, raw, mixed, mixed_grad, lse, gain[None], flag_row, flag_col)


def sum_back(lefts, rights, n=None, first=0):
    n = n or lefts[0][0].shape[0]
    out_width = rights[0][0].shape[0]
    tile = 2 * LANES
    count = len(lefts)

    def kernel(*refs):
        total = nt(refs[0][...], refs[count][...])
        for i in range(1, count):
            total = total + nt(refs[i][...], refs[count + i][...])
        refs[2 * count][...] = total.astype(low)

    depth = sum(columns for _, _, columns in lefts)
    return pl.pallas_call(
        kernel,
        grid=(out_width // tile,),
        in_specs=[pl.BlockSpec((n, columns), lambda j, at=at: (first, at)) for _, at, columns in lefts]
        + [pl.BlockSpec((tile, columns), lambda j, at=at: (j, at)) for _, at, columns in rights],
        out_specs=pl.BlockSpec((n, tile), lambda j: (0, j)),
        out_shape=jax.ShapeDtypeStruct((n, out_width), low),
        compiler_params=params(),
        cost_estimate=cost(2 * n * out_width * depth, 2 * (n + out_width) * depth + 2 * n * out_width),
    )(*(matrix for matrix, _, _ in lefts + rights))


def add_low(first, second):
    columns = first.shape[-1]
    flat = (first.size // columns, columns)
    block = flat[0] // 8

    def kernel(a_ref, b_ref, out_ref):
        out_ref[...] = (a_ref[...].astype(wide) + b_ref[...].astype(wide)).astype(low)

    spec = pl.BlockSpec((block, columns), lambda r: (r, 0))
    out = pl.pallas_call(
        kernel,
        grid=(8,),
        in_specs=[spec, spec],
        out_specs=spec,
        out_shape=jax.ShapeDtypeStruct(flat, low),
        compiler_params=params(),
        cost_estimate=cost(first.size, 6 * first.size),
    )(first.reshape(flat), second.reshape(flat))
    return out.reshape(first.shape)


def rows_product(pairs, tile):
    n, depth = pairs[0][0].shape
    lefts = [left for left, _ in pairs]
    rights = [right for _, group in pairs for right in group]
    owner = [k for k, (_, group) in enumerate(pairs) for _ in group]
    steps = [right.shape[1] // tile for right in rights]
    starts = [sum(steps[:i]) for i in range(len(steps))]
    chunk = 256

    def kernel(*refs):
        left_refs, right_refs = refs[: len(lefts)], refs[len(lefts) : len(lefts) + len(rights)]
        out, turned = refs[-2:]
        step = pl.program_id(0)
        for i, right in enumerate(right_refs):
            if i == 0 or owner[i] != owner[i - 1]:

                @pl.when(step == starts[i])
                def _(left=left_refs[owner[i]]):
                    for at in range(0, n, chunk):
                        turned[:, at : at + chunk] = left[at : at + chunk, :].T

            @pl.when((step >= starts[i]) & (step < starts[i] + steps[i]))
            def _(right=right):
                out[...] = nn(turned[...], right[...]).astype(low)

    def tile_of(i):
        return lambda j: (0, jnp.clip(j - starts[i], 0, steps[i] - 1))

    width = sum(right.shape[1] for right in rights)
    return pl.pallas_call(
        kernel,
        grid=(sum(steps),),
        in_specs=[pl.BlockSpec((n, depth), lambda j: (0, 0))] * len(lefts)
        + [pl.BlockSpec((n, tile), tile_of(i)) for i in range(len(rights))],
        out_specs=pl.BlockSpec((depth, tile), lambda j: (0, j)),
        out_shape=jax.ShapeDtypeStruct((depth, width), low),
        scratch_shapes=[pltpu.VMEM((depth, n), low)],
        compiler_params=params(),
        cost_estimate=cost(2 * n * depth * width, 2 * (n * (depth + width) + depth * width)),
    )(*lefts, *rights)


def product(left, right):
    n, depth = left.shape
    width = right.shape[1]

    def kernel(left_ref, right_ref, out_ref):
        out_ref[...] = nn(left_ref[...], right_ref[...]).astype(low)

    return pl.pallas_call(
        kernel,
        grid=(1,),
        in_specs=[pl.BlockSpec((n, depth), lambda j: (0, 0)), pl.BlockSpec((depth, width), lambda j: (0, 0))],
        out_specs=pl.BlockSpec((n, width), lambda j: (0, 0)),
        out_shape=jax.ShapeDtypeStruct((n, width), low),
        compiler_params=params(),
        cost_estimate=cost(2 * n * depth * width, 2 * (n * depth + depth * width + n * width)),
    )(left, right)


def chunk_specs(blocks, width):
    return [pl.BlockSpec(block.shape, lambda j: (0, 0)) for block in blocks]


def row_scale(values):
    return lax.rsqrt(jnp.mean(values * values, axis=-1, keepdims=True) + epsilon)


def unscale(grad, normed, scale):
    return scale * (grad - normed * jnp.mean(grad * normed, axis=-1, keepdims=True))


def settle_step(base, branch, rate):
    branch_scale = row_scale(branch)
    normed = branch * branch_scale
    moved = base + rate * (normed - base)
    scale = row_scale(moved)
    return moved * scale, (normed, branch_scale, scale)


def settle_back(grad, result, base, rate, saved):
    normed, branch_scale, scale = saved
    grad = unscale(grad, result, scale)
    return grad * (1.0 - rate), unscale(grad * rate, normed, branch_scale), grad * (normed - base)


def rate_rows(terms):
    return jnp.concatenate([jnp.sum(terms, axis=0, keepdims=True), jnp.zeros((7, terms.shape[1]), wide)])


def settle_attention(partial, got, tokens, rate, core):
    _, _, n, depth = partial.shape
    block = n // 2

    def kernel(core_ref, part_ref, got_ref, token_ref, rate_ref, hidden_ref, low_ref, branch_ref):
        branch = part_ref[0, 0].astype(wide) + got_ref[0].astype(wide)
        hidden, _ = settle_step(token_ref[...].astype(wide), branch, rate_ref[...])
        hidden_ref[...] = hidden
        low_ref[...] = hidden.astype(low)
        branch_ref[...] = branch

    rows = pl.BlockSpec((block, depth), lambda j, r, core_ref: (2 * j + r, 0))
    return pl.pallas_call(
        kernel,
        grid_spec=pltpu.PrefetchScalarGridSpec(
            num_scalar_prefetch=1,
            grid=(2, 2),
            in_specs=[
                pl.BlockSpec((1, 1, block, depth), lambda j, r, core_ref: (j, core_ref[0], r, 0)),
                pl.BlockSpec((1, block, depth), lambda j, r, core_ref: (j, r, 0)),
                rows,
                pl.BlockSpec((1, depth), lambda j, r, core_ref: (0, 0)),
            ],
            out_specs=[rows] * 3,
        ),
        out_shape=[
            jax.ShapeDtypeStruct((2 * n, depth), wide),
            jax.ShapeDtypeStruct((2 * n, depth), low),
            jax.ShapeDtypeStruct((2 * n, depth), wide),
        ],
        compiler_params=params(),
        cost_estimate=cost(0, 0),
    )(core.reshape(1), partial, got, tokens, rate[None])


def arrived_specs(n, depth):
    block = n // 4
    piece = pl.BlockSpec((block, depth), lambda h, r, *_: (r, 0))
    return [pl.BlockSpec((block, depth), lambda h, r, *_: (2 * h + r, 0))] + [piece] * 4


def arrived_sum(h, own, first, second, last_y, last_x):
    top, bottom = (a[...].astype(wide) + b[...].astype(wide) for a, b in ((first, last_y), (second, last_x)))
    return own[...].astype(wide) + jnp.where(h == 0, top, bottom)


def settle_units(arrived, hidden, near, far, early, rate):
    n, depth = hidden.shape
    block = n // 4

    def kernel(early_ref, *refs):
        h = pl.program_id(0)
        branch = arrived_sum(h, *refs[:5])
        hidden_ref, near_ref, far_ref, rate_ref, out_ref, direct_ref, grad_ref, term_ref = refs[5:]
        base, rates = hidden_ref[...], rate_ref[...]
        result, saved = settle_step(base, branch, rates)
        cotangent = jnp.where((h == 0) == (early_ref[0] == 1), near_ref[...], far_ref[...])
        direct, grad, terms = settle_back(cotangent.astype(wide), result, base, rates, saved)
        out_ref[...] = result.astype(low)
        direct_ref[...] = direct
        grad_ref[...] = grad.astype(low)

        start = (h == 0) & (pl.program_id(1) == 0)

        @pl.when(start)
        def _():
            term_ref[...] = rate_rows(terms)

        @pl.when(jnp.logical_not(start))
        def _():
            term_ref[...] += rate_rows(terms)

    rows = pl.BlockSpec((block, depth), lambda h, r, *_: (2 * h + r, 0))
    piece = pl.BlockSpec((block, depth), lambda h, r, *_: (r, 0))
    return pl.pallas_call(
        kernel,
        grid_spec=pltpu.PrefetchScalarGridSpec(
            num_scalar_prefetch=1,
            grid=(2, 2),
            in_specs=arrived_specs(n, depth)
            + [rows, piece, piece, pl.BlockSpec((1, depth), lambda h, r, *_: (0, 0))],
            out_specs=[rows, rows, rows, pl.BlockSpec((8, depth), lambda h, r, *_: (0, 0))],
        ),
        out_shape=[
            jax.ShapeDtypeStruct((n, depth), low),
            jax.ShapeDtypeStruct((n, depth), wide),
            jax.ShapeDtypeStruct((n, depth), low),
            jax.ShapeDtypeStruct((8, depth), wide),
        ],
        compiler_params=params(),
        cost_estimate=cost(0, 0),
    )(early.astype(jnp.int32).reshape(1), *arrived, hidden, near, far, rate[None])


def settle_attention_back(arrived, direct, hidden, tokens, branch, rate):
    n, depth = hidden.shape
    block = n // 4

    def kernel(*refs):
        h = pl.program_id(0)
        direct_ref, token_ref, branch_ref, rate_ref, out_ref, grad_ref, term_ref = refs[5:]
        grad = direct_ref[...] + arrived_sum(h, *refs[:5])
        base, rates = token_ref[...].astype(wide), rate_ref[...]
        result, saved = settle_step(base, branch_ref[...], rates)
        back, branch_grad, terms = settle_back(grad, result, base, rates, saved)
        out_ref[...] = back
        grad_ref[...] = branch_grad.astype(low)

        start = (h == 0) & (pl.program_id(1) == 0)

        @pl.when(start)
        def _():
            term_ref[...] = rate_rows(terms)

        @pl.when(jnp.logical_not(start))
        def _():
            term_ref[...] += rate_rows(terms)

    rows = pl.BlockSpec((block, depth), lambda h, r: (2 * h + r, 0))
    return pl.pallas_call(
        kernel,
        grid=(2, 2),
        in_specs=arrived_specs(n, depth) + [rows] * 3 + [pl.BlockSpec((1, depth), lambda h, r: (0, 0))],
        out_specs=[rows, rows, pl.BlockSpec((8, depth), lambda h, r: (0, 0))],
        out_shape=[
            jax.ShapeDtypeStruct((n, depth), wide),
            jax.ShapeDtypeStruct((n, depth), low),
            jax.ShapeDtypeStruct((8, depth), wide),
        ],
        compiler_params=params(),
        cost_estimate=cost(0, 0),
    )(*arrived, direct, tokens, branch, rate[None])


def lay_rows(refs, out):
    @pl.when(pl.program_id(0) == 0)
    def _():
        at = 0
        for ref in refs:
            out[at : at + ref.shape[0], :] = ref[...]
            at += ref.shape[0]


def mlp_forward(blocks, up_w, gate_w, scales, total, first, earlier):
    n = sum(block.shape[0] for block in blocks)
    depth, units = up_w.shape
    tile = 2 * LANES
    count = len(blocks)

    def kernel(*refs):
        ins, rest = refs[:count], refs[count:]
        up_ref, gate_ref, scale_ref = rest[:3]
        mid_ref, act_all, act_out, up_out, gate_out = rest[-5:]
        lay_rows(ins, mid_ref)
        left = mid_ref[...]
        up = nn(left, up_ref[...])
        gate = nn(left, gate_ref[...])
        lifted = scale_ref[1:2, :] * gate
        up_out[...] = up.astype(low)
        gate_out[...] = gate.astype(low)
        act = (scale_ref[0:1, :] * up * (lifted * jax.nn.sigmoid(lifted))).astype(low)
        act_out[...] = act
        act_all[...] = act

    weight = pl.BlockSpec((depth, tile), lambda j: (0, j))
    alone = pl.BlockSpec((n, tile), lambda j: (0, j))
    return pl.pallas_call(
        kernel,
        grid=(units // tile,),
        in_specs=chunk_specs(blocks, depth)
        + [weight] * 2
        + [pl.BlockSpec((2, tile), lambda j: (0, j))]
        + [pl.BlockSpec(memory_space=pl.ANY)] * len(earlier),
        out_specs=[
            pl.BlockSpec((n, depth), lambda j: (first, 0)), pl.BlockSpec((n, tile), lambda j: (first, j)),
            alone, alone, alone,
        ],
        out_shape=[jax.ShapeDtypeStruct((total, depth), low), jax.ShapeDtypeStruct((total, units), low)]
        + [jax.ShapeDtypeStruct((n, units), low)] * 3,
        input_output_aliases={count + 3 + i: i for i in range(len(earlier))},
        compiler_params=params(),
        cost_estimate=cost(4 * n * depth * units, 2 * (2 * n * depth + 2 * depth * units + 3 * n * units)),
    )(*blocks, up_w, gate_w, scales, *earlier)


def mlp_backward(blocks, up_w, gate_w, down_w, scales, up_raw, gate_raw, total, first, earlier):
    n = sum(block.shape[0] for block in blocks)
    depth, units = up_w.shape
    tile = 2 * LANES
    count = len(blocks)
    steps = units // tile

    def kernel(*refs):
        ins, rest = refs[:count], refs[count:]
        down_ref, scale_ref, up_raw_ref, gate_raw_ref, up_ref, gate_ref = rest[:6]
        branch_ref, up_out, gate_out, part_ref, gain_ref, kept, weights, sems = rest[-8:]
        step = pl.program_id(0)
        fetches = [
            pltpu.make_async_copy(ref, weights.at[i], sems.at[i]) for i, ref in enumerate((up_ref, gate_ref))
        ]

        @pl.when(step == 0)
        def _():
            for fetch in fetches:
                fetch.start()

        lay_rows(ins, branch_ref)
        up_gain, gate_gain = scale_ref[0:1, :], scale_ref[1:2, :]
        grad = nn(branch_ref[...], down_ref[...])
        up = up_raw_ref[...].astype(wide)
        gate = gate_raw_ref[...].astype(wide)
        lifted = gate_gain * gate
        slope = jax.nn.sigmoid(lifted)
        swished = lifted * slope
        up_part = grad * swished
        lifted_grad = grad * up * (up_gain * (slope + swished * (1.0 - slope)))
        up_term = jnp.sum(up_part * up, axis=0, keepdims=True)
        gate_term = jnp.sum(lifted_grad * gate, axis=0, keepdims=True)
        up_low = (up_part * up_gain).astype(low)
        gate_low = (lifted_grad * gate_gain).astype(low)
        up_out[...] = up_low
        gate_out[...] = gate_low
        kept[0, step] = up_low
        kept[1, step] = gate_low
        gain_ref[...] = jnp.concatenate([up_term, gate_term, jnp.zeros((6, tile), wide)], axis=0)

        @pl.when(step == steps - 1)
        def _():
            for fetch in fetches:
                fetch.wait()
            ups, gates = (jnp.concatenate([kept[i, k] for k in range(steps)], axis=1) for i in range(2))
            for at in range(0, depth, tile):
                part = nt(ups, weights[0, at : at + tile, :]) + nt(gates, weights[1, at : at + tile, :])
                part_ref[:, at : at + tile] = part.astype(low)

    anywhere = pl.BlockSpec(memory_space=pl.ANY)
    tiles = pl.BlockSpec((n, tile), lambda j: (first, j))
    alone = pl.BlockSpec((n, tile), lambda j: (0, j))
    all_units = jax.ShapeDtypeStruct((total, units), low)
    return pl.pallas_call(
        kernel,
        grid=(steps,),
        in_specs=chunk_specs(blocks, depth)
        + [
            pl.BlockSpec((depth, tile), lambda j: (0, j)), pl.BlockSpec((2, tile), lambda j: (0, j)),
            alone, alone, anywhere, anywhere,
        ]
        + [anywhere] * len(earlier),
        out_specs=[
            pl.BlockSpec((n, depth), lambda j: (first, 0)), tiles, tiles,
            pl.BlockSpec((n, depth), lambda j: (0, 0)), pl.BlockSpec((8, tile), lambda j: (0, j)),
        ],
        out_shape=[
            jax.ShapeDtypeStruct((total, depth), low), all_units, all_units,
            jax.ShapeDtypeStruct((n, depth), low), jax.ShapeDtypeStruct((8, units), wide),
        ],
        scratch_shapes=[
            pltpu.VMEM((2, steps, n, tile), low), pltpu.VMEM((2, depth, units), low),
            pltpu.SemaphoreType.DMA((2,)),
        ],
        input_output_aliases={count + 6 + i: i for i in range(len(earlier))},
        compiler_params=params(),
        cost_estimate=cost(6 * n * depth * units, 2 * (2 * n * depth + 3 * depth * units + 4 * n * units)),
    )(*blocks, down_w, scales, up_raw, gate_raw, up_w, gate_w, *earlier)


def place(blocks, indices):
    ndim = 2
    n = len(indices)
    count = len(blocks)
    pieces = [
        (i, at) for i, block in enumerate(blocks) for at in ([None] if block.ndim == ndim else range(block.shape[0]))
    ]
    shape = blocks[0].shape[-ndim:]
    where_to = jnp.stack([jnp.asarray(i, jnp.int32) for i in indices])

    def kernel(index_ref, *refs):
        out, sems = refs[count], refs[count + 1]
        copies = []
        for k, (i, at) in enumerate(pieces):
            source = refs[i] if at is None else refs[i].at[at]
            copies.append(pltpu.make_async_copy(source, out.at[index_ref[k]], sems.at[k]))
        for copy in copies:
            copy.start()
        for copy in copies:
            copy.wait()

    anywhere = pl.BlockSpec(memory_space=pl.ANY)
    out = jax.ShapeDtypeStruct((n,) + shape, blocks[0].dtype)
    return pl.pallas_call(
        kernel,
        in_specs=[pl.BlockSpec(memory_space=pltpu.SMEM)] + [anywhere] * count,
        out_specs=pl.BlockSpec(memory_space=pltpu.VMEM),
        out_shape=out,
        scratch_shapes=[pltpu.SemaphoreType.DMA((n,))],
        compiler_params=params(),
        cost_estimate=cost(0, 2 * out.size * out.dtype.itemsize),
    )(where_to, *blocks)


def spread_pack(grad, extra, chip):
    _, _, rows, columns = grad.shape
    total = rows + extra.shape[0]
    tile = 2 * LANES

    def kernel(chip_ref, grad_ref, extra_ref, first, second, keep):
        plan = [(first, 1, 0), (first, 3, 0), (second, 2, 1), (second, 3, 1)]
        plan += [(keep, 0, 0), (keep, 0, 1), (keep, 2, 0), (keep, 1, 1)]
        used = {}
        for out, k, half in plan:
            slot = used.get(id(out), 0)
            used[id(out)] = slot + 1
            out[slot, :rows, :] = grad_ref[chip_ref[0] ^ k, half]
            out[slot, rows:, :] = extra_ref[...]

    def out(n):
        return pl.BlockSpec((n, total, tile), lambda j, *_: (0, 0, j))

    return pl.pallas_call(
        kernel,
        grid_spec=pltpu.PrefetchScalarGridSpec(
            num_scalar_prefetch=1,
            grid=(columns // tile,),
            in_specs=[
                pl.BlockSpec((CHIPS, 2, rows, tile), lambda j, *_: (0, 0, 0, j)),
                pl.BlockSpec((extra.shape[0], tile), lambda j, *_: (0, j)),
            ],
            out_specs=[out(2), out(2), out(4)],
        ),
        out_shape=[jax.ShapeDtypeStruct((n, total, columns), low) for n in (2, 2, 4)],
        compiler_params=params(),
        cost_estimate=cost(0, 0),
    )(chip.reshape(1), grad, extra.astype(low))


def spread_turn(first, second, keep):
    _, total, columns = first.shape
    tile = 2 * LANES

    def kernel(first_ref, second_ref, keep_ref, y_ref, x_ref):
        y_ref[...] = (keep_ref[2].astype(wide) + first_ref[1].astype(wide)).astype(low)
        x_ref[...] = (keep_ref[3].astype(wide) + second_ref[1].astype(wide)).astype(low)

    def spec(n):
        return pl.BlockSpec((n, total, tile), lambda j: (0, 0, j))

    out = pl.BlockSpec((total, tile), lambda j: (0, j))
    return pl.pallas_call(
        kernel,
        grid=(columns // tile,),
        in_specs=[spec(2), spec(2), spec(4)],
        out_specs=[out] * 2,
        out_shape=[jax.ShapeDtypeStruct((total, columns), low)] * 2,
        compiler_params=params(),
        cost_estimate=cost(0, 0),
    )(first, second, keep)


def spread_finish(first, second, keep, last_y, last_x, width, core):
    _, total, columns = first.shape
    out_width = columns // 2

    def kernel(core_ref, first_ref, second_ref, keep_ref, y_ref, x_ref, *outs):
        for half in range(2):
            got, last = ((first_ref, y_ref), (second_ref, x_ref))[half]
            value = keep_ref[half].astype(wide) + got[0].astype(wide) + last[...].astype(wide)
            for which in range(2):
                piece = jnp.concatenate(
                    [
                        value[:, at + which * width : at + (which + 1) * width]
                        for at in range(0, columns, 2 * width)
                    ],
                    axis=1,
                ).astype(low)
                for side in range(2):

                    @pl.when((core_ref[0] ^ side) == half)
                    def _(side=side, which=which, piece=piece):
                        outs[2 * side + which][...] = piece

    whole = pl.BlockSpec(memory_space=pltpu.VMEM)
    return pl.pallas_call(
        kernel,
        in_specs=[pl.BlockSpec(memory_space=pltpu.SMEM)] + [whole] * 5,
        out_specs=[whole] * 4,
        out_shape=[jax.ShapeDtypeStruct((total, out_width), low)] * 4,
        compiler_params=params(),
        cost_estimate=cost(0, 0),
    )(core.reshape(1), first, second, keep, last_y, last_x)


def half_tiles(first, second, first_upper, second_upper):
    first, second = first.astype(wide), second.astype(wide)
    axis = first.ndim - 1
    first = jnp.where(first_upper, pltpu.roll(first, HALF, axis), first)
    second = jnp.where(second_upper, second, pltpu.roll(second, HALF, axis))
    lane = lax.broadcasted_iota(jnp.int32, first.shape, axis)
    return jnp.where(lane < HALF, first, second).astype(low)


def unit_pack(groups):
    weights = [weight for group in groups for weight in group]
    rows, units = weights[0].shape
    main = units // CHIPS // LANES * LANES
    width = len(weights) * main + len(groups) * LANES

    def kernel(*refs):
        out, at, first = refs[-1], 0, 0
        target = pl.program_id(0)
        start = pl.multiple_of(target * main, LANES)
        tile = pl.multiple_of(CHIPS * main + (target // 2) * LANES, LANES)
        upper = (target & 1) == 1
        for group in groups:
            members = refs[first : first + len(group)]
            first += len(group)
            for ref in members:
                out[0, :, at : at + main] = ref[:, pl.ds(start, main)]
                at += main
            rests = [ref[:, pl.ds(tile, LANES)] for ref in members]
            out[0, :, at : at + LANES] = half_tiles(rests[0], rests[-1], upper, upper)
            at += LANES

    whole = pl.BlockSpec((rows, units), lambda k: (0, 0))
    return pl.pallas_call(
        kernel,
        grid=(CHIPS,),
        in_specs=[whole] * len(weights),
        out_specs=pl.BlockSpec((1, rows, width), lambda k: (k, 0, 0)),
        out_shape=jax.ShapeDtypeStruct((CHIPS, rows, width), weights[0].dtype),
        cost_estimate=cost(0, 0),
    )(*weights)


def unit_lay(n, mine, theirs, core):
    count, _, rows, columns = mine.shape
    main = (columns - LANES) // n
    units = count * main + count // 2 * LANES

    def kernel(core_ref, *refs):
        outs = refs[2:]
        for side in range(2):
            slot = core_ref[0] ^ side
            blocks = refs[side]
            for i in range(n):
                for k in range(count):
                    outs[i][slot, :, k * main : (k + 1) * main] = blocks[k, 0, :, i * main : (i + 1) * main]
                tile = n * main
                upper = i == 1
                for k in range(0, count, 2):
                    at = count * main + k // 2 * LANES
                    outs[i][slot, :, at : at + LANES] = half_tiles(
                        blocks[k, 0, :, tile : tile + LANES],
                        blocks[k + 1, 0, :, tile : tile + LANES],
                        upper,
                        upper,
                    )

    block = pl.BlockSpec((count, 1, rows, columns), lambda q: (0, q, 0, 0))
    out = pl.BlockSpec((2, rows, units), lambda q: (q, 0, 0))
    return pl.pallas_call(
        kernel,
        grid=(CHIPS,),
        in_specs=[pl.BlockSpec(memory_space=pltpu.SMEM)] + [block] * 2,
        out_specs=[out] * n,
        out_shape=[jax.ShapeDtypeStruct((2 * CHIPS, rows, units), low)] * n,
        compiler_params=params(),
        cost_estimate=cost(0, 14 * n * 8 * rows * units // 4),
    )(core.reshape(1), mine, theirs)


def unit_unlay(grads, n, core):
    count = lax.axis_size("tensor")
    _, rows, units = grads.shape
    units = units // n
    main = units // count // LANES * LANES
    columns = n * main + (n + 1) // 2 * LANES

    def kernel(core_ref, *refs):
        for side in range(2):
            slot = core_ref[0] ^ side
            out = refs[1 + side]
            for k in range(count):
                for i in range(n):
                    out[k, 0, :, i * main : (i + 1) * main] = refs[0][slot, :, i * units + k * main : i * units + (k + 1) * main]
                at = count * main + k // 2 * LANES
                upper = k % 2 == 1
                rests = [refs[0][slot, :, i * units + at : i * units + at + LANES] for i in range(n)]
                for i in range(0, n, 2):
                    to = n * main + i // 2 * LANES
                    out[k, 0, :, to : to + LANES] = half_tiles(
                        rests[i], rests[min(i + 1, n - 1)], upper, upper
                    )

    block = pl.BlockSpec((2, rows, n * units), lambda q: (q, 0, 0))
    return pl.pallas_call(
        kernel,
        grid=(CHIPS,),
        in_specs=[pl.BlockSpec(memory_space=pltpu.SMEM)] + [block],
        out_specs=[pl.BlockSpec((count, 1, rows, columns), lambda q: (0, q, 0, 0))] * 2,
        out_shape=[jax.ShapeDtypeStruct((count, CHIPS, rows, columns), low)] * 2,
        compiler_params=params(),
        cost_estimate=cost(0, 14 * n * 8 * rows * units // 4),
    )(core.reshape(1), grads)


def unit_unpack(n, blocks):
    _, rows, columns = blocks.shape
    main = (columns - (n + 1) // 2 * LANES) // n
    units = CHIPS * main + CHIPS // 2 * LANES

    def kernel(block_ref, *outs):
        for i in range(n):
            for j in range(CHIPS):
                outs[i][:, j * main : (j + 1) * main] = block_ref[j, :, i * main : (i + 1) * main].astype(wide)
            tile = n * main + i // 2 * LANES
            upper = i % 2 == 1
            for j in range(0, CHIPS, 2):
                at = CHIPS * main + j // 2 * LANES
                outs[i][:, at : at + LANES] = half_tiles(
                    block_ref[j, :, tile : tile + LANES], block_ref[j + 1, :, tile : tile + LANES], upper, upper
                ).astype(wide)

    return pl.pallas_call(
        kernel,
        out_shape=[jax.ShapeDtypeStruct((rows, units), wide)] * n,
        compiler_params=params(),
    )(blocks)


def per_device(
    block_in, out_grad, global_pos,
    w_query, w_key, w_value, w_out, w_up, w_gate, w_down,
    qk_gain, up_gain, gate_gain, att_rate, mlp_rate,
):
    count = lax.axis_size("tensor")
    plane = lax.axis_size(DP)
    micro_count, _, local_rows, model_width = block_in.shape
    assert micro_count == 2 and count == 4
    seq_len = local_rows * count
    head_width = w_query.shape[1]
    core_heads = head_width * 2
    unit_width = w_up.shape[1]
    plane_unit = unit_width // CHIPS
    main = plane_unit // LANES * LANES
    rest = plane_unit - main
    me = lax.axis_index(DP)
    z = lax.axis_index("tensor")
    core = me & 1
    chip = (me >> 1) & 3
    early = z < 2

    def across(value, pairs):
        return lax.ppermute(
            value, ALL, [(a * count + b, c * count + d) for (a, b), (c, d) in pairs]
        )

    def home(far):
        return [
            ((p, t), ((p & ~1) | (t & 1), ((t & 2) ^ (2 if far else 0)) | (p & 1)))
            for p in range(plane)
            for t in range(count)
        ]

    def seq_near(value):
        return across(lax.dynamic_index_in_dim(value, z >> 1, 0, keepdims=False), home(False))

    def seq_far(value):
        return across(lax.dynamic_index_in_dim(value, 1 - (z >> 1), 0, keepdims=False), home(True))

    def seq_join(near, far):
        return pick(early, jnp.concatenate([near, far]), jnp.concatenate([far, near]))

    def from_sequence(value):
        first, second = value[:local_rows], value[local_rows:]
        near = across(pick(early, first, second), [(b, a) for a, b in home(False)])
        far = across(pick(early, second, first), [(b, a) for a, b in home(True)])
        return near, far

    def by_micro(near, far):
        return pick(early, jnp.stack([near, far]), jnp.stack([far, near])).astype(wide)

    def both_cores(value):
        value = value.reshape(2, local_rows, model_width)
        return place([value, swap(value, 1)], [core, core + 2, 1 - core, 3 - core]).reshape(
            seq_len, model_width
        )

    def core_scatter(partial):
        split = partial.reshape(2, 2, local_rows, model_width)
        got = swap(lax.dynamic_index_in_dim(split, 1 - core, 1, keepdims=False), 1)
        mine = lax.dynamic_index_in_dim(split, core, 1, keepdims=False)
        return (mine.astype(wide) + got.astype(wide)).reshape(2 * local_rows, model_width)

    def head_pairs(other_core, second):
        return [
            ((p ^ other_core, (t + 2 * (p & 1) + second) % count), (p, t))
            for p in range(plane)
            for t in range(count)
        ]

    def paired(a, b):
        return jnp.concatenate(
            [a[..., :head_width], b[..., :head_width], a[..., head_width:], b[..., head_width:]], axis=-1
        )

    def attn_fetch(first, second):
        packed = outer_gather(jnp.concatenate([first, second], axis=1))
        groups = [[across(packed, head_pairs(side, which)) for which in range(2)] for side in range(2)]
        return jnp.stack([paired(*pair) for pair in groups])

    def attn_pair(first, second, extra):
        packed = jnp.concatenate([outer_gather(jnp.concatenate([first, second], axis=1)), extra])
        return jnp.stack([packed, swap(packed, 1)])

    def attn_fetch_packed(packed, rows):
        groups = [across(packed, head_pairs(0, which)) for which in range(2)]
        sides = [
            paired(*(group[:, :rows, at : at + head_width] for group in groups))
            for at in range(0, packed.shape[2], head_width)
        ]
        return *sides, [group[0, rows:] for group in groups]

    def attn_first(sides):
        return sides, swap(sides, 2), swap(sides, 4)

    def attn_second(first):
        sides, along_x, along_y = first
        return sides, along_x, along_y, swap(along_y[0], 2), swap(along_x[1], 4)

    def attn_lay(blocks):
        return full_rows(place(blocks, [2 * (chip ^ (i // 2)) + (core ^ (i % 2)) for i in range(8)]))

    def attn_pack(packed, extra):
        grad = plane_rows(packed).reshape(CHIPS, 2, -1, packed.shape[1])
        return spread_pack(grad, extra, chip)

    def attn_send(messages):
        first, second, keep = messages
        return swap(first, 2), swap(second, 4), keep

    def attn_turn(messages):
        to_y, to_x = messages
        return swap(to_y, 4), swap(to_x, 2)

    def attn_scatter(sent, turned):
        pieces = spread_finish(*sent, *turned, head_width, core)
        return [
            across(pieces[2 * side + which], [(b, a) for a, b in head_pairs(side, which)])
            for side in range(2)
            for which in range(2)
        ]

    def attn_join(got, extra_rows):
        got = [piece.astype(wide) for piece in got]
        rows = got[0].shape[0] - extra_rows
        small = jnp.stack([piece[rows:] for piece in got])
        extra = jnp.zeros(small.shape[1:], wide)
        for t in range(count):
            back = (z - t) % count
            index = 2 * ((back >> 1) ^ core) + (back & 1)
            extra = extra + lax.dynamic_index_in_dim(small, index, 0, keepdims=False)
        return attn_own(sum(piece[:rows] for piece in got), extra)

    def attn_own(grads, extra):
        grads = outer_scatter(grads)
        bit = 8
        while bit < plane:
            extra = extra + swap(extra, bit)
            bit *= 2
        return grads[:, :head_width], grads[:, head_width:], extra

    def unit_join(n, mine):
        return [full_rows(w) for w in unit_lay(n, mine, swap(mine, 1), core)]

    def unit_collect(grads):
        keep, send = unit_unlay([plane_rows(g) for g in grads], core)
        return add_low(keep, swap(send, 1))

    def unit_return(n, total):
        return [outer_scatter(g) for g in unit_unpack(n, lax.all_to_all(total, "chip", 0, 0, tiled=True))]

    tie = lax.optimization_barrier

    def halved(value):
        upper_part = lax.reduce_precision(value, 8, 7)
        return jnp.stack([upper_part, value - upper_part]).astype(low)

    qk_sides = attn_fetch(w_query, w_key)
    unit_blocks = unit_pack([[outer_gather(w_up), outer_gather(w_gate)]])
    mains = lax.dynamic_slice_in_dim(jnp.stack([up_gain, gate_gain]), chip * main, main, 1)
    rests = lax.dynamic_slice_in_dim(jnp.stack([up_gain, gate_gain]), CHIPS * main + chip * rest, rest, 1)
    unit_gains = halved(jnp.concatenate([mains, rests], axis=1).reshape(-1))
    gain_rows = jnp.concatenate(
        [unit_gains, halved(qk_gain).reshape(1, -1), jnp.zeros((13, 2 * head_width), low)]
    )
    vo_packed = attn_pair(w_value, w_out, gain_rows)
    places_here = global_pos[:, 0]
    places_there = swap(places_here, 1)
    qk_sides, vo_packed, places_there, unit_blocks, block_in = tie(
        (qk_sides, vo_packed, places_there, unit_blocks, block_in)
    )
    qk_first = attn_first(qk_sides)
    value_sides, out_sides, gain_groups = attn_fetch_packed(vo_packed, qk_sides.shape[1])
    near = seq_near(block_in[:, 0])
    qk_first, value_sides, out_sides, gain_groups, near, block_in, unit_blocks = tie(
        (qk_first, value_sides, out_sides, gain_groups, near, block_in, unit_blocks)
    )
    ug_laid = lax.all_to_all(unit_blocks, "chip", 0, 0, tiled=True)
    lower, upper_rows = block_in[:, 0, : local_rows // 2], block_in[:, 0, local_rows // 2 :]
    far_first, upper_rows = tie((seq_far(lower), upper_rows))
    far = jnp.concatenate([far_first, seq_far(upper_rows)])
    qk_w = attn_lay(attn_second(qk_first))
    value_w = attn_lay(attn_second(attn_first(value_sides)))
    qk_w, value_w, out_sides, gain_groups, far, near, ug_laid, w_down = tie(
        (qk_w, value_w, out_sides, gain_groups, far, near, ug_laid, w_down)
    )
    down_laid = lax.all_to_all(unit_pack([[outer_gather(w_down)]]), "chip", 0, 0, tiled=True)
    gain_here = jnp.stack(gain_groups)[:, :2].astype(wide).sum(axis=1)
    gain_there = swap(gain_here, 1)
    out_across = [out_sides] + [swap(out_sides, 2 * k) for k in range(1, CHIPS)]
    tokens = seq_join(near, far)
    sequence = both_cores(tokens)
    ug_shifted = lax.all_gather(ug_laid, "tensor")
    unit_gains = pick(
        core == 0, jnp.concatenate([gain_here, gain_there]), jnp.concatenate([gain_there, gain_here])
    )
    unit_gains = lax.dynamic_slice_in_dim(jnp.concatenate([unit_gains, unit_gains]), count - z, count, 0)
    unit_gains = unit_gains.reshape(count, 2, plane_unit).transpose(1, 0, 2)
    scales = jnp.concatenate(
        [unit_gains[..., :main].reshape(2, -1), unit_gains[..., main:].reshape(2, -1)], axis=1
    )
    head_gain = jnp.stack(gain_groups)[:, 2].astype(wide).reshape(2, 2, head_width).sum(axis=1)
    head_gain = head_gain.reshape(core_heads)
    places = lax.dynamic_index_in_dim(
        pick((z & 1) == core, places_here, places_there), z >> 1, 0, keepdims=False
    )
    flags = jnp.any(places[:, None] == jnp.arange(seq_len, dtype=jnp.int32)[None, :], axis=0).astype(wide)
    flag_row, flag_col = flags[None], flags[:, None]

    heads, raw = project_heads(sequence, qk_w, jnp.concatenate([head_gain, head_gain]))
    value_rows = product(sequence, value_w)
    mixed, lse = attend_forward(heads, value_rows, flag_row, flag_col)
    mixed, out_across, down_laid = tie((mixed, out_across, down_laid))
    down_shifted = lax.all_gather(down_laid, "tensor")
    out_w = attn_lay(out_across)
    partial = sum_back([(mixed, 0, core_heads)], [(out_w, 0, core_heads)])
    partial = partial.reshape(2, 2, local_rows, model_width)
    got = swap(lax.dynamic_index_in_dim(partial, 1 - core, 1, keepdims=False), 1)
    hidden, hidden_low, att_branch = settle_attention(partial, got, tokens, att_rate, core)

    own_rows = 2 * local_rows
    all_rows = CHIPS * own_rows
    hidden_low, ug_shifted = tie((hidden_low, ug_shifted))
    first = plane_first(hidden_low)
    up_w, gate_w = unit_join(2, ug_shifted)
    earlier, saved, acts = (), [], []

    def forward(blocks, at):
        nonlocal earlier
        *earlier, act, up_raw, gate_raw = mlp_forward(blocks, up_w, gate_w, scales, all_rows, at, earlier)
        saved.append((up_raw, gate_raw))
        return act

    def back(act):
        return sum_back([(act, 0, act.shape[1])], [(down_w, 0, act.shape[1])])

    def by_chip(own, both, diagonal):
        return [own, both[:own_rows], both[own_rows:], diagonal]

    act_own = forward([hidden_low], 2)
    out_grad_low = out_grad[:, 0].astype(low)
    first, act_own, out_grad_low = tie((first, act_own, out_grad_low))
    _, along_x, along_y, *diagonal = plane_second(first)
    act_both = forward([along_x, along_y], 0)
    diagonal, act_both, down_shifted = tie((diagonal, act_both, down_shifted))
    (down_w,) = unit_join(1, down_shifted)
    act_diagonal = forward(diagonal, 3)
    mid, activated = earlier
    parts = [back(act) for act in (act_own, act_both, act_diagonal)]
    parts, out_grad_low = tie((parts, out_grad_low))
    sent, _ = scatter_first(by_chip(*parts))
    cotangent = seq_near(out_grad_low), seq_far(out_grad_low)
    sent, cotangent = tie((sent, cotangent))
    block_rows, direct, branch_grad, mlp_rate_term = settle_units(
        scatter_last(sent), hidden, *cotangent, early, mlp_rate
    )

    first = plane_first(branch_grad)
    returned = from_sequence(block_rows)
    earlier, unit_terms = (), []

    def backward(blocks, at, raws):
        nonlocal earlier
        *earlier, part, unit_term = mlp_backward(
            blocks, up_w, gate_w, down_w, scales, *raws, all_rows, at, earlier
        )
        unit_terms.append(unit_term[:2])
        return part

    part_own = backward([branch_grad], 2, saved[0])
    first, part_own = tie((first, part_own))
    _, along_x, along_y, *diagonal = plane_second(first)
    part_both = backward([along_x, along_y], 0, saved[1])
    diagonal, part_both, returned = tie((diagonal, part_both, returned))
    part_diagonal = backward(diagonal, 3, saved[2])
    branch, up_low, gate_low = earlier
    sent, (branch, mid) = scatter_first(by_chip(part_own, part_both, part_diagonal), (branch, mid))
    down_blocks = unit_unlay(plane_rows(rows_product([(branch, [activated])], 2 * LANES)), 1, core)
    ug_grad = rows_product([(mid, [up_low, gate_low])], 2 * LANES)
    small = jnp.concatenate([sum(unit_terms), mlp_rate_term[:1]])
    small = small + swap(small, 1)
    sent, down_blocks, ug_grad, small = tie((sent, down_blocks, ug_grad, small))
    arrived = scatter_last(sent)
    down_blocks = add_low(down_blocks[0], swap(down_blocks[1], 1))
    ug_blocks = unit_unlay(plane_rows(ug_grad), 2, core)
    def rate_rows_of(term):
        rows = jnp.broadcast_to(term.reshape(2, 2, 1, head_width), (2, 2, 2, head_width))
        return jnp.where(own_chip[..., None], rows.reshape(1, 2, 4 * head_width), 0.0).reshape(2 * CHIPS, -1)

    own_chip = jnp.arange(CHIPS)[:, None] == chip
    empty_rows = jnp.zeros((EXTRA - 3 * CHIPS, 4 * head_width), wide)
    unit_rows = jnp.concatenate(
        [small[:2, : count * main].reshape(2, count, main), small[:2, count * main :].reshape(2, count, rest)],
        axis=2,
    )
    unit_rows = lax.dynamic_slice_in_dim(
        jnp.concatenate([unit_rows, unit_rows], axis=1), z + 2 * core, 2, 1
    ).reshape(1, 4 * plane_unit)
    vo_extra = jnp.concatenate([jnp.where(own_chip, unit_rows, 0.0), rate_rows_of(small[2:]), empty_rows])
    vo_extra = vo_extra.astype(low)
    arrived, ug_blocks, down_blocks, vo_extra = tie((arrived, ug_blocks, down_blocks, vo_extra))
    down_back = lax.psum_scatter(down_blocks, "tensor", scatter_dimension=0)
    ug_there = swap(ug_blocks[1], 1)
    input_direct, att_grad, att_rate_term = settle_attention_back(
        arrived, direct, hidden, tokens, att_branch, att_rate
    )
    att_low = both_cores(att_grad)
    ug_blocks = add_low(ug_blocks[0], ug_there)
    att_low, ug_blocks = tie((att_low, ug_blocks))
    ug_back = lax.psum_scatter(ug_blocks, "tensor", scatter_dimension=0)
    mixed_grad = product(att_low, out_w)
    heads_low, vraw_low, head_terms = attend_backward(
        heads, raw, value_rows, mixed, mixed_grad, lse, head_gain, flag_row, flag_col
    )
    block_out = by_micro(*returned)

    heads_low, vraw_low, down_back = tie((heads_low, vraw_low, down_back))
    vo_grad = rows_product([(sequence, [vraw_low]), (att_low, [mixed])], core_heads)
    vo_messages, vraw_low = tie((attn_pack(vo_grad, vo_extra), vraw_low))
    vo_sent = attn_send(vo_messages)
    in_part = sum_back(
        [(heads_low, 0, 2 * core_heads), (vraw_low, 0, core_heads)],
        [(qk_w, 0, 2 * core_heads), (value_w, 0, core_heads)],
    )
    (grad_down,) = unit_return(1, down_back)
    vo_sent, heads_low, in_part, ug_back, block_out, grad_down = tie(
        (vo_sent, heads_low, in_part, ug_back, block_out, grad_down)
    )
    att_term = att_rate_term[:1] + swap(att_rate_term[:1], 1)
    vo_messages, heads_low, in_part, att_term = tie((spread_turn(*vo_sent), heads_low, in_part, att_term))
    qk_extra = jnp.concatenate(
        [
            jnp.where(own_chip, head_terms[:2].reshape(1, 4 * head_width), 0.0),
            rate_rows_of(att_term),
            empty_rows,
        ]
    )
    vo_turned = attn_turn(vo_messages)
    in_rows = (input_direct + core_scatter(in_part)).astype(low)
    qk_messages = attn_pack(rows_product([(sequence, [heads_low])], 2 * LANES), qk_extra)
    vo_turned, in_rows, qk_messages = tie((vo_turned, in_rows, qk_messages))
    qk_sent = attn_send(qk_messages)
    returned_in = from_sequence(in_rows)
    qk_sent, vo_turned = tie((qk_sent, vo_turned))
    vo_got = attn_scatter(vo_sent, vo_turned)
    qk_turned = attn_turn(spread_turn(*qk_sent))
    qk_turned, returned_in, ug_back = tie((qk_turned, returned_in, ug_back))
    qk_got = attn_scatter(qk_sent, qk_turned)
    grad_up, grad_gate = unit_return(2, ug_back)
    in_grad = by_micro(*returned_in)
    vo_got, qk_got = tie((vo_got, qk_got))
    grad_value, grad_out, vo_small = attn_join(vo_got, EXTRA)
    grad_query, grad_key, qk_small = attn_join(qk_got, EXTRA)

    units = vo_small[:CHIPS].reshape(CHIPS, 2, plane_unit).transpose(1, 0, 2)
    units = jnp.concatenate([units[..., :main].reshape(2, -1), units[..., main:].reshape(2, -1)], axis=1)
    mlp_total, att_total = (
        jnp.sum(member[CHIPS : 3 * CHIPS].reshape(CHIPS, model_width), axis=0) for member in (vo_small, qk_small)
    )
    head_sums = jnp.sum(qk_small[:CHIPS], axis=0)
    grad_qk_gain = head_sums[:head_width] + head_sums[head_width:]
    return (
        block_out[:, None], in_grad[:, None],
        grad_query, grad_key, grad_value, grad_out, grad_up, grad_gate, grad_down,
        grad_qk_gain, units[0], units[1], att_total, mlp_total,
    )


def solution(mesh):
    shape = dict(mesh.shape)
    plane, count = shape["dp"], shape["tensor"]
    split = Mesh(mesh.devices.reshape(plane // 8, CHIPS, 2, count), ALL)
    tokens = P(None, DP, "tensor", None)
    matrix = P(DP, "tensor")
    in_specs = (tokens, tokens, P(None, DP, None)) + (matrix,) * 7 + (P("tensor"),) * 3 + (P(), P())
    out_specs = (tokens, tokens) + (matrix,) * 7 + (P("tensor"),) * 3 + (P(), P())
    return jax.shard_map(
        per_device, mesh=split, in_specs=in_specs, out_specs=out_specs, check_vma=False
    )
```

```python
import math

import jax
import jax.numpy as jnp
from jax import lax
from jax.experimental import pallas as pl
from jax.experimental.pallas import tpu as pltpu
from jax.sharding import Mesh, PartitionSpec as P

HD = 64
WINDOW = 512
CHIPS = 4
LANES = 128
HALF = 64
EXTRA = 16
BLOCK = 256
VMEM_LIMIT = 48 * 2**20

DP = ("outer", "chip", "core")
ALL = DP + ("tensor",)

epsilon = 1e-06
blocked = -1e30
low = jnp.bfloat16
wide = jnp.float32


def swap(value, bit):
    count = lax.axis_size(DP)
    return lax.ppermute(value, DP, [(i, i ^ bit) for i in range(count)])


def pick(flag, when_true, when_false):
    return jnp.where(flag, when_true, when_false)


def outer_gather(value):
    me = lax.axis_index(DP)
    bit = 8
    while bit < lax.axis_size(DP):
        other = swap(value, bit)
        upper = (me & bit) != 0
        value = pick(
            upper, jnp.concatenate([other, value]), jnp.concatenate([value, other])
        )
        bit *= 2
    return value


def outer_scatter(value):
    me = lax.axis_index(DP)
    bit = lax.axis_size(DP) // 2
    while bit >= 8:
        rows = value.shape[0] // 2
        upper = (me & bit) != 0
        keep = pick(upper, value[rows:], value[:rows])
        send = pick(upper, value[:rows], value[rows:])
        value = (keep.astype(wide) + swap(send, bit).astype(wide)).astype(value.dtype)
        bit //= 2
    return value


def full_rows(value):
    outer = lax.axis_size(DP) // 8
    count, rows, columns = value.shape
    if outer > 1:
        value = value.reshape(count, outer, rows // outer, columns).transpose(1, 0, 2, 3)
    return value.reshape(count * rows, columns)


def plane_rows(value):
    outer = lax.axis_size(DP) // 8
    total, columns = value.shape
    if outer > 1:
        value = value.reshape(outer, 8, total // 8 // outer, columns).transpose(1, 0, 2, 3)
    return value.reshape(8, total // 8, columns)


def plane_first(value):
    return value, swap(value, 2), swap(value, 4)


def plane_second(first):
    value, along_x, along_y = first
    half = value.shape[0] // 2
    return value, along_x, along_y, swap(along_y[:half], 2), swap(along_x[half:], 4)


def scatter_first(blocks, then=()):
    own, along_x, along_y, diagonal = blocks
    half = own.shape[0] // 2
    first, second, then = lax.optimization_barrier(
        (
            jnp.concatenate([along_x[:half], diagonal[:half]]),
            jnp.concatenate([along_y[half:], diagonal[half:]]),
            then,
        )
    )
    return (blocks, swap(first, 2), swap(second, 4)), then


def scatter_last(sent):
    (own, along_x, along_y, _), first, second = sent
    half = own.shape[0] // 2
    next_y = (along_y[:half].astype(wide) + first[half:].astype(wide)).astype(low)
    next_x = (along_x[half:].astype(wide) + second[half:].astype(wide)).astype(low)
    return own, first, second, swap(next_y, 4), swap(next_x, 2)


def scatter_second(sent):
    own, first, second, last_y, last_x = scatter_last(sent)
    half = own.shape[0] // 2
    top = own[:half].astype(wide) + first[:half].astype(wide) + last_y.astype(wide)
    bottom = own[half:].astype(wide) + second[:half].astype(wide) + last_x.astype(wide)
    return jnp.concatenate([top, bottom])


def nt(left, right):
    return lax.dot_general(left, right, (((1,), (1,)), ((), ())), preferred_element_type=wide)


def nn(left, right):
    return lax.dot_general(left, right, (((1,), (0,)), ((), ())), preferred_element_type=wide)


def tn(left, right):
    return lax.dot_general(left, right, (((0,), (0,)), ((), ())), preferred_element_type=wide)


def params():
    return pltpu.CompilerParams(vmem_limit_bytes=VMEM_LIMIT)


def cost(flops, moved):
    return pl.CostEstimate(flops=1, bytes_accessed=1, transcendentals=0)


def head_means(width):
    rows = lax.broadcasted_iota(jnp.int32, (width, width), 0) // HD
    columns = lax.broadcasted_iota(jnp.int32, (width, width), 1) // HD
    return jnp.where(rows == columns, 1.0 / HD, 0.0).astype(low)


def head_scale(raw, means):
    return lax.rsqrt(nn((raw * raw).astype(low), means) + epsilon)


def project_heads(rows, weight, gain):
    n, depth = rows.shape
    width = weight.shape[1]
    tile = 2 * LANES
    block = n

    def kernel(rows_ref, weight_ref, gain_ref, out_ref, raw_ref):
        means = head_means(tile)
        for start in range(0, n, block):
            span = slice(start, start + block)
            raw = nn(rows_ref[span, :], weight_ref[...])
            raw_ref[span, :] = raw.astype(low)
            out_ref[span, :] = (raw * head_scale(raw, means) * gain_ref[...]).astype(low)

    out = pl.BlockSpec((n, tile), lambda j: (0, j))
    return pl.pallas_call(
        kernel,
        grid=(width // tile,),
        in_specs=[
            pl.BlockSpec((n, depth), lambda j: (0, 0)),
            pl.BlockSpec((depth, tile), lambda j: (0, j)),
            pl.BlockSpec((1, tile), lambda j: (0, j)),
        ],
        out_specs=[out, out],
        out_shape=[jax.ShapeDtypeStruct((n, width), low)] * 2,
        compiler_params=params(),
        cost_estimate=cost(2 * n * depth * width, 2 * (n * depth + depth * width + 2 * n * width)),
    )(rows, weight, gain[None])


def fill_bias(bias, flag_row, flag_col):
    @pl.when(pl.program_id(0) == 0)
    def _():
        for i in range(bias.shape[0] // BLOCK):
            for j in range(i + 1):
                keys = slice(j * BLOCK, (j + 1) * BLOCK)
                rows = slice(i * BLOCK, (i + 1) * BLOCK)
                key_ids = j * BLOCK + lax.broadcasted_iota(jnp.int32, (BLOCK, BLOCK), 0)
                row_ids = i * BLOCK + lax.broadcasted_iota(jnp.int32, (BLOCK, BLOCK), 1)
                flagged = jnp.maximum(flag_row[:, rows], flag_col[keys, :]) > 0.5
                allow = (key_ids <= row_ids) & ((row_ids - key_ids < WINDOW) | flagged)
                bias[keys, rows] = jnp.where(allow, 0.0, blocked)


def head_lanes(value, head):
    lane = lax.broadcasted_iota(jnp.int32, value.shape, 1)
    mine = (lane < HD) if head == 0 else (lane >= HD)
    return jnp.where(mine, value, jnp.zeros_like(value))


def flag_specs(seq_len):
    return [pl.BlockSpec((1, seq_len), lambda h: (0, 0)), pl.BlockSpec((seq_len, 1), lambda h: (0, 0))]


def attend_forward(heads, value_rows, flag_row, flag_col):
    seq_len, width = value_rows.shape
    pairs = width // LANES

    def kernel(q_ref, k_ref, v_ref, row_ref, col_ref, out_ref, lse_ref, bias, turned):
        fill_bias(bias, row_ref, col_ref)
        turned[...] = v_ref[...].astype(wide).T.astype(low)
        for i in range(seq_len // BLOCK):
            rows = slice(i * BLOCK, (i + 1) * BLOCK)
            reach = (i + 1) * BLOCK
            block = q_ref[rows, :] * jnp.asarray(1.0 / math.sqrt(HD), low)
            halves = []
            for head in range(2):
                scores = nt(k_ref[:reach, :], head_lanes(block, head)) + bias[:reach, rows]
                raised = jnp.exp(scores)
                total = jnp.sum(raised, axis=0, keepdims=True)
                mixed = nn(turned[head * HD : (head + 1) * HD, :reach], raised.astype(low))
                halves.append(mixed / total)
                lse_ref[0, head : head + 1, rows] = jnp.log(total)
            out_ref[rows, :] = jnp.concatenate(halves, axis=0).T.astype(low)

    block = pl.BlockSpec((seq_len, LANES), lambda h: (0, h))
    keys = pl.BlockSpec((seq_len, LANES), lambda h: (0, pairs + h))
    return pl.pallas_call(
        kernel,
        grid=(pairs,),
        in_specs=[block, keys, block] + flag_specs(seq_len),
        out_specs=[block, pl.BlockSpec((1, 8, seq_len), lambda h: (h, 0, 0))],
        out_shape=[
            jax.ShapeDtypeStruct((seq_len, width), low),
            jax.ShapeDtypeStruct((pairs, 8, seq_len), wide),
        ],
        scratch_shapes=[pltpu.VMEM((seq_len, seq_len), wide), pltpu.VMEM((LANES, seq_len), low)],
        compiler_params=params(),
        cost_estimate=cost(16 * seq_len * seq_len * width, 10 * seq_len * width),
    )(heads, heads, value_rows, flag_row, flag_col)


def attend_backward(heads, raw, value_rows, mixed, mixed_grad, lse, gain, flag_row, flag_col):
    seq_len, width = value_rows.shape
    pairs = width // LANES
    scale = 1.0 / math.sqrt(HD)

    def unnorm(grad, raw_block, gain_row, means):
        raw_block = raw_block.astype(wide)
        factor = head_scale(raw_block, means)
        normed = raw_block * factor
        term = jnp.sum(grad * normed, axis=0, keepdims=True)
        grad = grad * gain_row
        inner = nn((grad * normed).astype(low), means)
        return (factor * (grad - normed * inner)).astype(low), term

    def kernel(
        q_ref, k_ref, v_ref, qraw_ref, kraw_ref, m_ref, g_ref, lse_ref, gain_ref, row_ref, col_ref,
        heads_ref, dv_ref, term_ref, bias, turned, key_total, value_total, dq_ref, dk_ref, sems,
    ):
        step = pl.program_id(0)

        def stores(pair):
            return [
                pltpu.make_async_copy(
                    ref, heads_ref.at[:, pl.ds(pl.multiple_of((side * pairs + pair) * LANES, LANES), LANES)], sems.at[side]
                )
                for side, ref in enumerate((dq_ref, dk_ref))
            ]

        @pl.when(step > 0)
        def _():
            for store in stores(step - 1):
                store.wait()

        fill_bias(bias, row_ref, col_ref)
        turned[...] = k_ref[...].astype(wide).T.astype(low)
        means = head_means(LANES)
        gain_row = gain_ref[...]
        query_term = key_term = jnp.zeros((1, LANES), wide)
        count = seq_len // BLOCK
        for i in reversed(range(count)):
            rows = slice(i * BLOCK, (i + 1) * BLOCK)
            reach = (i + 1) * BLOCK
            block = q_ref[rows, :] * jnp.asarray(scale, low)
            grads = g_ref[rows, :]
            products = (grads.astype(wide) * m_ref[rows, :].astype(wide)).T
            halves = []
            key_parts = value_parts = None
            for head in range(2):
                inner = jnp.sum(products[head * HD : (head + 1) * HD], axis=0, keepdims=True)
                query = head_lanes(block, head)
                grad = head_lanes(grads, head)
                scores = nt(k_ref[:reach, :], query) + bias[:reach, rows]
                probs = jnp.exp(scores - lse_ref[0, head : head + 1, rows])
                prob_grad = nt(v_ref[:reach, :], grad)
                score_grad = (probs * (prob_grad - inner)).astype(low)
                halves.append(nn(turned[head * HD : (head + 1) * HD, :reach], score_grad))
                key_part = nn(score_grad, query)
                value_part = nn(probs.astype(low), grad)
                key_parts = key_part if key_parts is None else key_parts + key_part
                value_parts = value_part if value_parts is None else value_parts + value_part
            if i == count - 1:
                key_total[...] = key_parts
                value_total[...] = value_parts
            else:
                key_total[:reach, :] += key_parts
                value_total[:reach, :] += value_parts
            query_grad = jnp.concatenate(halves, axis=0).T * scale
            dq_ref[rows, :], term = unnorm(query_grad, qraw_ref[rows, :], gain_row, means)
            query_term = query_term + term
        dv_ref[...] = value_total[...].astype(low)
        for i in range(count):
            rows = slice(i * BLOCK, (i + 1) * BLOCK)
            dk_ref[rows, :], term = unnorm(key_total[rows, :], kraw_ref[rows, :], gain_row, means)
            key_term = key_term + term
        term_ref[...] = jnp.concatenate([query_term, key_term, jnp.zeros((6, LANES), wide)], axis=0)
        for store in stores(step):
            store.start()

        @pl.when(step == pairs - 1)
        def _():
            for store in stores(step):
                store.wait()

    block = pl.BlockSpec((seq_len, LANES), lambda h: (0, h))
    keys = pl.BlockSpec((seq_len, LANES), lambda h: (0, pairs + h))
    return pl.pallas_call(
        kernel,
        grid=(pairs,),
        in_specs=[block, keys, block, block, keys, block, block]
        + [pl.BlockSpec((1, 8, seq_len), lambda h: (h, 0, 0)), pl.BlockSpec((1, LANES), lambda h: (0, h))]
        + flag_specs(seq_len),
        out_specs=[pl.BlockSpec(memory_space=pl.ANY), block, pl.BlockSpec((8, LANES), lambda h: (0, h))],
        out_shape=[
            jax.ShapeDtypeStruct((seq_len, 2 * width), low),
            jax.ShapeDtypeStruct((seq_len, width), low),
            jax.ShapeDtypeStruct((8, width), wide),
        ],
        scratch_shapes=[
            pltpu.VMEM((seq_len, seq_len), wide),
            pltpu.VMEM((LANES, seq_len), low),
            pltpu.VMEM((seq_len, LANES), wide),
            pltpu.VMEM((seq_len, LANES), wide),
            pltpu.VMEM((seq_len, LANES), low),
            pltpu.VMEM((seq_len, LANES), low),
            pltpu.SemaphoreType.DMA((2,)),
        ],
        compiler_params=params(),
        cost_estimate=cost(32 * seq_len * seq_len * width, 20 * seq_len * width),
    )(heads, heads, value_rows, raw, raw, mixed, mixed_grad, lse, gain[None], flag_row, flag_col)


def sum_back(lefts, rights, n=None, first=0):
    n = n or lefts[0][0].shape[0]
    out_width = rights[0][0].shape[0]
    tile = 2 * LANES
    count = len(lefts)

    def kernel(*refs):
        total = nt(refs[0][...], refs[count][...])
        for i in range(1, count):
            total = total + nt(refs[i][...], refs[count + i][...])
        refs[2 * count][...] = total.astype(low)

    depth = sum(columns for _, _, columns in lefts)
    return pl.pallas_call(
        kernel,
        grid=(out_width // tile,),
        in_specs=[pl.BlockSpec((n, columns), lambda j, at=at: (first, at)) for _, at, columns in lefts]
        + [pl.BlockSpec((tile, columns), lambda j, at=at: (j, at)) for _, at, columns in rights],
        out_specs=pl.BlockSpec((n, tile), lambda j: (0, j)),
        out_shape=jax.ShapeDtypeStruct((n, out_width), low),
        compiler_params=params(),
        cost_estimate=cost(2 * n * out_width * depth, 2 * (n + out_width) * depth + 2 * n * out_width),
    )(*(matrix for matrix, _, _ in lefts + rights))


def add_low(first, second):
    columns = first.shape[-1]
    flat = (first.size // columns, columns)
    block = flat[0] // 8

    def kernel(a_ref, b_ref, out_ref):
        out_ref[...] = (a_ref[...].astype(wide) + b_ref[...].astype(wide)).astype(low)

    spec = pl.BlockSpec((block, columns), lambda r: (r, 0))
    out = pl.pallas_call(
        kernel,
        grid=(8,),
        in_specs=[spec, spec],
        out_specs=spec,
        out_shape=jax.ShapeDtypeStruct(flat, low),
        compiler_params=params(),
        cost_estimate=cost(first.size, 6 * first.size),
    )(first.reshape(flat), second.reshape(flat))
    return out.reshape(first.shape)


def rows_product(pairs, tile):
    n, depth = pairs[0][0].shape
    lefts = [left for left, _ in pairs]
    rights = [right for _, group in pairs for right in group]
    owner = [k for k, (_, group) in enumerate(pairs) for _ in group]
    steps = [right.shape[1] // tile for right in rights]
    starts = [sum(steps[:i]) for i in range(len(steps))]
    chunk = 256

    def kernel(*refs):
        left_refs, right_refs = refs[: len(lefts)], refs[len(lefts) : len(lefts) + len(rights)]
        out, turned = refs[-2:]
        step = pl.program_id(0)
        for i, right in enumerate(right_refs):
            if i == 0 or owner[i] != owner[i - 1]:

                @pl.when(step == starts[i])
                def _(left=left_refs[owner[i]]):
                    for at in range(0, n, chunk):
                        turned[:, at : at + chunk] = left[at : at + chunk, :].T

            @pl.when((step >= starts[i]) & (step < starts[i] + steps[i]))
            def _(right=right):
                out[...] = nn(turned[...], right[...]).astype(low)

    def tile_of(i):
        return lambda j: (0, jnp.clip(j - starts[i], 0, steps[i] - 1))

    width = sum(right.shape[1] for right in rights)
    return pl.pallas_call(
        kernel,
        grid=(sum(steps),),
        in_specs=[pl.BlockSpec((n, depth), lambda j: (0, 0))] * len(lefts)
        + [pl.BlockSpec((n, tile), tile_of(i)) for i in range(len(rights))],
        out_specs=pl.BlockSpec((depth, tile), lambda j: (0, j)),
        out_shape=jax.ShapeDtypeStruct((depth, width), low),
        scratch_shapes=[pltpu.VMEM((depth, n), low)],
        compiler_params=params(),
        cost_estimate=cost(2 * n * depth * width, 2 * (n * (depth + width) + depth * width)),
    )(*lefts, *rights)


def product(left, right):
    n, depth = left.shape
    width = right.shape[1]

    def kernel(left_ref, right_ref, out_ref):
        out_ref[...] = nn(left_ref[...], right_ref[...]).astype(low)

    return pl.pallas_call(
        kernel,
        grid=(1,),
        in_specs=[pl.BlockSpec((n, depth), lambda j: (0, 0)), pl.BlockSpec((depth, width), lambda j: (0, 0))],
        out_specs=pl.BlockSpec((n, width), lambda j: (0, 0)),
        out_shape=jax.ShapeDtypeStruct((n, width), low),
        compiler_params=params(),
        cost_estimate=cost(2 * n * depth * width, 2 * (n * depth + depth * width + n * width)),
    )(left, right)


def chunk_specs(blocks, width):
    return [pl.BlockSpec(block.shape, lambda j: (0, 0)) for block in blocks]


def row_scale(values):
    return lax.rsqrt(jnp.mean(values * values, axis=-1, keepdims=True) + epsilon)


def unscale(grad, normed, scale):
    return scale * (grad - normed * jnp.mean(grad * normed, axis=-1, keepdims=True))


def settle_step(base, branch, rate):
    branch_scale = row_scale(branch)
    normed = branch * branch_scale
    moved = base + rate * (normed - base)
    scale = row_scale(moved)
    return moved * scale, (normed, branch_scale, scale)


def settle_back(grad, result, base, rate, saved):
    normed, branch_scale, scale = saved
    grad = unscale(grad, result, scale)
    return grad * (1.0 - rate), unscale(grad * rate, normed, branch_scale), grad * (normed - base)


def rate_rows(terms):
    return jnp.concatenate([jnp.sum(terms, axis=0, keepdims=True), jnp.zeros((7, terms.shape[1]), wide)])


def settle_attention(partial, got, tokens, rate, core):
    _, _, n, depth = partial.shape
    block = n // 2

    def kernel(core_ref, part_ref, got_ref, token_ref, rate_ref, hidden_ref, low_ref, branch_ref):
        branch = part_ref[0, 0].astype(wide) + got_ref[0].astype(wide)
        hidden, _ = settle_step(token_ref[...].astype(wide), branch, rate_ref[...])
        hidden_ref[...] = hidden
        low_ref[...] = hidden.astype(low)
        branch_ref[...] = branch

    rows = pl.BlockSpec((block, depth), lambda j, r, core_ref: (2 * j + r, 0))
    return pl.pallas_call(
        kernel,
        grid_spec=pltpu.PrefetchScalarGridSpec(
            num_scalar_prefetch=1,
            grid=(2, 2),
            in_specs=[
                pl.BlockSpec((1, 1, block, depth), lambda j, r, core_ref: (j, core_ref[0], r, 0)),
                pl.BlockSpec((1, block, depth), lambda j, r, core_ref: (j, r, 0)),
                rows,
                pl.BlockSpec((1, depth), lambda j, r, core_ref: (0, 0)),
            ],
            out_specs=[rows] * 3,
        ),
        out_shape=[
            jax.ShapeDtypeStruct((2 * n, depth), wide),
            jax.ShapeDtypeStruct((2 * n, depth), low),
            jax.ShapeDtypeStruct((2 * n, depth), wide),
        ],
        compiler_params=params(),
        cost_estimate=cost(0, 0),
    )(core.reshape(1), partial, got, tokens, rate[None])


def arrived_specs(n, depth):
    block = n // 4
    piece = pl.BlockSpec((block, depth), lambda h, r, *_: (r, 0))
    return [pl.BlockSpec((block, depth), lambda h, r, *_: (2 * h + r, 0))] + [piece] * 4


def arrived_sum(h, own, first, second, last_y, last_x):
    top, bottom = (a[...].astype(wide) + b[...].astype(wide) for a, b in ((first, last_y), (second, last_x)))
    return own[...].astype(wide) + jnp.where(h == 0, top, bottom)


def settle_units(arrived, hidden, near, far, early, rate):
    n, depth = hidden.shape
    block = n // 4

    def kernel(early_ref, *refs):
        h = pl.program_id(0)
        branch = arrived_sum(h, *refs[:5])
        hidden_ref, near_ref, far_ref, rate_ref, out_ref, direct_ref, grad_ref, term_ref = refs[5:]
        base, rates = hidden_ref[...], rate_ref[...]
        result, saved = settle_step(base, branch, rates)
        cotangent = jnp.where((h == 0) == (early_ref[0] == 1), near_ref[...], far_ref[...])
        direct, grad, terms = settle_back(cotangent.astype(wide), result, base, rates, saved)
        out_ref[...] = result.astype(low)
        direct_ref[...] = direct
        grad_ref[...] = grad.astype(low)

        start = (h == 0) & (pl.program_id(1) == 0)

        @pl.when(start)
        def _():
            term_ref[...] = rate_rows(terms)

        @pl.when(jnp.logical_not(start))
        def _():
            term_ref[...] += rate_rows(terms)

    rows = pl.BlockSpec((block, depth), lambda h, r, *_: (2 * h + r, 0))
    piece = pl.BlockSpec((block, depth), lambda h, r, *_: (r, 0))
    return pl.pallas_call(
        kernel,
        grid_spec=pltpu.PrefetchScalarGridSpec(
            num_scalar_prefetch=1,
            grid=(2, 2),
            in_specs=arrived_specs(n, depth)
            + [rows, piece, piece, pl.BlockSpec((1, depth), lambda h, r, *_: (0, 0))],
            out_specs=[rows, rows, rows, pl.BlockSpec((8, depth), lambda h, r, *_: (0, 0))],
        ),
        out_shape=[
            jax.ShapeDtypeStruct((n, depth), low),
            jax.ShapeDtypeStruct((n, depth), wide),
            jax.ShapeDtypeStruct((n, depth), low),
            jax.ShapeDtypeStruct((8, depth), wide),
        ],
        compiler_params=params(),
        cost_estimate=cost(0, 0),
    )(early.astype(jnp.int32).reshape(1), *arrived, hidden, near, far, rate[None])


def settle_attention_back(arrived, direct, hidden, tokens, branch, rate):
    n, depth = hidden.shape
    block = n // 4

    def kernel(*refs):
        h = pl.program_id(0)
        direct_ref, token_ref, branch_ref, rate_ref, out_ref, grad_ref, term_ref = refs[5:]
        grad = direct_ref[...] + arrived_sum(h, *refs[:5])
        base, rates = token_ref[...].astype(wide), rate_ref[...]
        result, saved = settle_step(base, branch_ref[...], rates)
        back, branch_grad, terms = settle_back(grad, result, base, rates, saved)
        out_ref[...] = back
        grad_ref[...] = branch_grad.astype(low)

        start = (h == 0) & (pl.program_id(1) == 0)

        @pl.when(start)
        def _():
            term_ref[...] = rate_rows(terms)

        @pl.when(jnp.logical_not(start))
        def _():
            term_ref[...] += rate_rows(terms)

    rows = pl.BlockSpec((block, depth), lambda h, r: (2 * h + r, 0))
    return pl.pallas_call(
        kernel,
        grid=(2, 2),
        in_specs=arrived_specs(n, depth) + [rows] * 3 + [pl.BlockSpec((1, depth), lambda h, r: (0, 0))],
        out_specs=[rows, rows, pl.BlockSpec((8, depth), lambda h, r: (0, 0))],
        out_shape=[
            jax.ShapeDtypeStruct((n, depth), wide),
            jax.ShapeDtypeStruct((n, depth), low),
            jax.ShapeDtypeStruct((8, depth), wide),
        ],
        compiler_params=params(),
        cost_estimate=cost(0, 0),
    )(*arrived, direct, tokens, branch, rate[None])


def lay_rows(refs, out):
    @pl.when(pl.program_id(0) == 0)
    def _():
        at = 0
        for ref in refs:
            out[at : at + ref.shape[0], :] = ref[...]
            at += ref.shape[0]


def mlp_forward(blocks, up_w, gate_w, scales, total, first, earlier):
    n = sum(block.shape[0] for block in blocks)
    depth, units = up_w.shape
    tile = 2 * LANES
    count = len(blocks)

    def kernel(*refs):
        ins, rest = refs[:count], refs[count:]
        up_ref, gate_ref, scale_ref = rest[:3]
        mid_ref, act_all, act_out, up_out, gate_out = rest[-5:]
        lay_rows(ins, mid_ref)
        left = mid_ref[...]
        up = nn(left, up_ref[...])
        gate = nn(left, gate_ref[...])
        lifted = scale_ref[1:2, :] * gate
        up_out[...] = up.astype(low)
        gate_out[...] = gate.astype(low)
        act = (scale_ref[0:1, :] * up * (lifted * jax.nn.sigmoid(lifted))).astype(low)
        act_out[...] = act
        act_all[...] = act

    weight = pl.BlockSpec((depth, tile), lambda j: (0, j))
    alone = pl.BlockSpec((n, tile), lambda j: (0, j))
    return pl.pallas_call(
        kernel,
        grid=(units // tile,),
        in_specs=chunk_specs(blocks, depth)
        + [weight] * 2
        + [pl.BlockSpec((2, tile), lambda j: (0, j))]
        + [pl.BlockSpec(memory_space=pl.ANY)] * len(earlier),
        out_specs=[
            pl.BlockSpec((n, depth), lambda j: (first, 0)), pl.BlockSpec((n, tile), lambda j: (first, j)),
            alone, alone, alone,
        ],
        out_shape=[jax.ShapeDtypeStruct((total, depth), low), jax.ShapeDtypeStruct((total, units), low)]
        + [jax.ShapeDtypeStruct((n, units), low)] * 3,
        input_output_aliases={count + 3 + i: i for i in range(len(earlier))},
        compiler_params=params(),
        cost_estimate=cost(4 * n * depth * units, 2 * (2 * n * depth + 2 * depth * units + 3 * n * units)),
    )(*blocks, up_w, gate_w, scales, *earlier)


def mlp_backward(blocks, up_w, gate_w, down_w, scales, up_raw, gate_raw, total, first, earlier):
    n = sum(block.shape[0] for block in blocks)
    depth, units = up_w.shape
    tile = 2 * LANES
    count = len(blocks)
    steps = units // tile

    def kernel(*refs):
        ins, rest = refs[:count], refs[count:]
        down_ref, scale_ref, up_raw_ref, gate_raw_ref, up_ref, gate_ref = rest[:6]
        branch_ref, up_out, gate_out, part_ref, gain_ref, kept, weights, sems = rest[-8:]
        step = pl.program_id(0)
        fetches = [
            pltpu.make_async_copy(ref, weights.at[i], sems.at[i]) for i, ref in enumerate((up_ref, gate_ref))
        ]

        @pl.when(step == 0)
        def _():
            for fetch in fetches:
                fetch.start()

        lay_rows(ins, branch_ref)
        up_gain, gate_gain = scale_ref[0:1, :], scale_ref[1:2, :]
        grad = nn(branch_ref[...], down_ref[...])
        up = up_raw_ref[...].astype(wide)
        gate = gate_raw_ref[...].astype(wide)
        lifted = gate_gain * gate
        slope = jax.nn.sigmoid(lifted)
        swished = lifted * slope
        up_part = grad * swished
        lifted_grad = grad * up * (up_gain * (slope + swished * (1.0 - slope)))
        up_term = jnp.sum(up_part * up, axis=0, keepdims=True)
        gate_term = jnp.sum(lifted_grad * gate, axis=0, keepdims=True)
        up_low = (up_part * up_gain).astype(low)
        gate_low = (lifted_grad * gate_gain).astype(low)
        up_out[...] = up_low
        gate_out[...] = gate_low
        kept[0, step] = up_low
        kept[1, step] = gate_low
        gain_ref[...] = jnp.concatenate([up_term, gate_term, jnp.zeros((6, tile), wide)], axis=0)

        @pl.when(step == steps - 1)
        def _():
            for fetch in fetches:
                fetch.wait()
            ups, gates = (jnp.concatenate([kept[i, k] for k in range(steps)], axis=1) for i in range(2))
            for at in range(0, depth, tile):
                part = nt(ups, weights[0, at : at + tile, :]) + nt(gates, weights[1, at : at + tile, :])
                part_ref[:, at : at + tile] = part.astype(low)

    anywhere = pl.BlockSpec(memory_space=pl.ANY)
    tiles = pl.BlockSpec((n, tile), lambda j: (first, j))
    alone = pl.BlockSpec((n, tile), lambda j: (0, j))
    all_units = jax.ShapeDtypeStruct((total, units), low)
    return pl.pallas_call(
        kernel,
        grid=(steps,),
        in_specs=chunk_specs(blocks, depth)
        + [
            pl.BlockSpec((depth, tile), lambda j: (0, j)), pl.BlockSpec((2, tile), lambda j: (0, j)),
            alone, alone, anywhere, anywhere,
        ]
        + [anywhere] * len(earlier),
        out_specs=[
            pl.BlockSpec((n, depth), lambda j: (first, 0)), tiles, tiles,
            pl.BlockSpec((n, depth), lambda j: (0, 0)), pl.BlockSpec((8, tile), lambda j: (0, j)),
        ],
        out_shape=[
            jax.ShapeDtypeStruct((total, depth), low), all_units, all_units,
            jax.ShapeDtypeStruct((n, depth), low), jax.ShapeDtypeStruct((8, units), wide),
        ],
        scratch_shapes=[
            pltpu.VMEM((2, steps, n, tile), low), pltpu.VMEM((2, depth, units), low),
            pltpu.SemaphoreType.DMA((2,)),
        ],
        input_output_aliases={count + 6 + i: i for i in range(len(earlier))},
        compiler_params=params(),
        cost_estimate=cost(6 * n * depth * units, 2 * (2 * n * depth + 3 * depth * units + 4 * n * units)),
    )(*blocks, down_w, scales, up_raw, gate_raw, up_w, gate_w, *earlier)


def place(blocks, indices):
    ndim = 2
    n = len(indices)
    count = len(blocks)
    pieces = [
        (i, at) for i, block in enumerate(blocks) for at in ([None] if block.ndim == ndim else range(block.shape[0]))
    ]
    shape = blocks[0].shape[-ndim:]
    where_to = jnp.stack([jnp.asarray(i, jnp.int32) for i in indices])

    def kernel(index_ref, *refs):
        out, sems = refs[count], refs[count + 1]
        copies = []
        for k, (i, at) in enumerate(pieces):
            source = refs[i] if at is None else refs[i].at[at]
            copies.append(pltpu.make_async_copy(source, out.at[index_ref[k]], sems.at[k]))
        for copy in copies:
            copy.start()
        for copy in copies:
            copy.wait()

    anywhere = pl.BlockSpec(memory_space=pl.ANY)
    out = jax.ShapeDtypeStruct((n,) + shape, blocks[0].dtype)
    return pl.pallas_call(
        kernel,
        in_specs=[pl.BlockSpec(memory_space=pltpu.SMEM)] + [anywhere] * count,
        out_specs=pl.BlockSpec(memory_space=pltpu.VMEM),
        out_shape=out,
        scratch_shapes=[pltpu.SemaphoreType.DMA((n,))],
        compiler_params=params(),
        cost_estimate=cost(0, 2 * out.size * out.dtype.itemsize),
    )(where_to, *blocks)


def spread_pack(grad, extra, chip):
    _, _, rows, columns = grad.shape
    total = rows + extra.shape[0]
    tile = 2 * LANES

    def kernel(chip_ref, grad_ref, extra_ref, first, second, keep):
        plan = [(first, 1, 0), (first, 3, 0), (second, 2, 1), (second, 3, 1)]
        plan += [(keep, 0, 0), (keep, 0, 1), (keep, 2, 0), (keep, 1, 1)]
        used = {}
        for out, k, half in plan:
            slot = used.get(id(out), 0)
            used[id(out)] = slot + 1
            out[slot, :rows, :] = grad_ref[chip_ref[0] ^ k, half]
            out[slot, rows:, :] = extra_ref[...]

    def out(n):
        return pl.BlockSpec((n, total, tile), lambda j, *_: (0, 0, j))

    return pl.pallas_call(
        kernel,
        grid_spec=pltpu.PrefetchScalarGridSpec(
            num_scalar_prefetch=1,
            grid=(columns // tile,),
            in_specs=[
                pl.BlockSpec((CHIPS, 2, rows, tile), lambda j, *_: (0, 0, 0, j)),
                pl.BlockSpec((extra.shape[0], tile), lambda j, *_: (0, j)),
            ],
            out_specs=[out(2), out(2), out(4)],
        ),
        out_shape=[jax.ShapeDtypeStruct((n, total, columns), low) for n in (2, 2, 4)],
        compiler_params=params(),
        cost_estimate=cost(0, 0),
    )(chip.reshape(1), grad, extra.astype(low))


def spread_turn(first, second, keep):
    _, total, columns = first.shape
    tile = 2 * LANES

    def kernel(first_ref, second_ref, keep_ref, y_ref, x_ref):
        y_ref[...] = (keep_ref[2].astype(wide) + first_ref[1].astype(wide)).astype(low)
        x_ref[...] = (keep_ref[3].astype(wide) + second_ref[1].astype(wide)).astype(low)

    def spec(n):
        return pl.BlockSpec((n, total, tile), lambda j: (0, 0, j))

    out = pl.BlockSpec((total, tile), lambda j: (0, j))
    return pl.pallas_call(
        kernel,
        grid=(columns // tile,),
        in_specs=[spec(2), spec(2), spec(4)],
        out_specs=[out] * 2,
        out_shape=[jax.ShapeDtypeStruct((total, columns), low)] * 2,
        compiler_params=params(),
        cost_estimate=cost(0, 0),
    )(first, second, keep)


def spread_finish(first, second, keep, last_y, last_x, width, core):
    _, total, columns = first.shape
    out_width = columns // 2

    def kernel(core_ref, first_ref, second_ref, keep_ref, y_ref, x_ref, *outs):
        for half in range(2):
            got, last = ((first_ref, y_ref), (second_ref, x_ref))[half]
            value = keep_ref[half].astype(wide) + got[0].astype(wide) + last[...].astype(wide)
            for which in range(2):
                piece = jnp.concatenate(
                    [
                        value[:, at + which * width : at + (which + 1) * width]
                        for at in range(0, columns, 2 * width)
                    ],
                    axis=1,
                ).astype(low)
                for side in range(2):

                    @pl.when((core_ref[0] ^ side) == half)
                    def _(side=side, which=which, piece=piece):
                        outs[2 * side + which][...] = piece

    whole = pl.BlockSpec(memory_space=pltpu.VMEM)
    return pl.pallas_call(
        kernel,
        in_specs=[pl.BlockSpec(memory_space=pltpu.SMEM)] + [whole] * 5,
        out_specs=[whole] * 4,
        out_shape=[jax.ShapeDtypeStruct((total, out_width), low)] * 4,
        compiler_params=params(),
        cost_estimate=cost(0, 0),
    )(core.reshape(1), first, second, keep, last_y, last_x)


def half_tiles(first, second, first_upper, second_upper):
    first, second = first.astype(wide), second.astype(wide)
    axis = first.ndim - 1
    first = jnp.where(first_upper, pltpu.roll(first, HALF, axis), first)
    second = jnp.where(second_upper, second, pltpu.roll(second, HALF, axis))
    lane = lax.broadcasted_iota(jnp.int32, first.shape, axis)
    return jnp.where(lane < HALF, first, second).astype(low)


def unit_pack(groups):
    weights = [weight for group in groups for weight in group]
    rows, units = weights[0].shape
    main = units // CHIPS // LANES * LANES
    width = len(weights) * main + len(groups) * LANES

    def kernel(*refs):
        out, at, first = refs[-1], 0, 0
        target = pl.program_id(0)
        start = pl.multiple_of(target * main, LANES)
        tile = pl.multiple_of(CHIPS * main + (target // 2) * LANES, LANES)
        upper = (target & 1) == 1
        for group in groups:
            members = refs[first : first + len(group)]
            first += len(group)
            for ref in members:
                out[0, :, at : at + main] = ref[:, pl.ds(start, main)]
                at += main
            rests = [ref[:, pl.ds(tile, LANES)] for ref in members]
            out[0, :, at : at + LANES] = half_tiles(rests[0], rests[-1], upper, upper)
            at += LANES

    whole = pl.BlockSpec((rows, units), lambda k: (0, 0))
    return pl.pallas_call(
        kernel,
        grid=(CHIPS,),
        in_specs=[whole] * len(weights),
        out_specs=pl.BlockSpec((1, rows, width), lambda k: (k, 0, 0)),
        out_shape=jax.ShapeDtypeStruct((CHIPS, rows, width), weights[0].dtype),
        cost_estimate=cost(0, 0),
    )(*weights)


def unit_lay(n, mine, theirs, core):
    count, _, rows, columns = mine.shape
    main = (columns - LANES) // n
    units = count * main + count // 2 * LANES

    def kernel(core_ref, *refs):
        outs = refs[2:]
        for side in range(2):
            slot = core_ref[0] ^ side
            blocks = refs[side]
            for i in range(n):
                for k in range(count):
                    outs[i][slot, :, k * main : (k + 1) * main] = blocks[k, 0, :, i * main : (i + 1) * main]
                tile = n * main
                upper = i == 1
                for k in range(0, count, 2):
                    at = count * main + k // 2 * LANES
                    outs[i][slot, :, at : at + LANES] = half_tiles(
                        blocks[k, 0, :, tile : tile + LANES],
                        blocks[k + 1, 0, :, tile : tile + LANES],
                        upper,
                        upper,
                    )

    block = pl.BlockSpec((count, 1, rows, columns), lambda q: (0, q, 0, 0))
    out = pl.BlockSpec((2, rows, units), lambda q: (q, 0, 0))
    return pl.pallas_call(
        kernel,
        grid=(CHIPS,),
        in_specs=[pl.BlockSpec(memory_space=pltpu.SMEM)] + [block] * 2,
        out_specs=[out] * n,
        out_shape=[jax.ShapeDtypeStruct((2 * CHIPS, rows, units), low)] * n,
        compiler_params=params(),
        cost_estimate=cost(0, 14 * n * 8 * rows * units // 4),
    )(core.reshape(1), mine, theirs)


def unit_unlay(grads, n, core):
    count = lax.axis_size("tensor")
    _, rows, units = grads.shape
    units = units // n
    main = units // count // LANES * LANES
    columns = n * main + (n + 1) // 2 * LANES

    def kernel(core_ref, *refs):
        for side in range(2):
            slot = core_ref[0] ^ side
            out = refs[1 + side]
            for k in range(count):
                for i in range(n):
                    out[k, 0, :, i * main : (i + 1) * main] = refs[0][slot, :, i * units + k * main : i * units + (k + 1) * main]
                at = count * main + k // 2 * LANES
                upper = k % 2 == 1
                rests = [refs[0][slot, :, i * units + at : i * units + at + LANES] for i in range(n)]
                for i in range(0, n, 2):
                    to = n * main + i // 2 * LANES
                    out[k, 0, :, to : to + LANES] = half_tiles(
                        rests[i], rests[min(i + 1, n - 1)], upper, upper
                    )

    block = pl.BlockSpec((2, rows, n * units), lambda q: (q, 0, 0))
    return pl.pallas_call(
        kernel,
        grid=(CHIPS,),
        in_specs=[pl.BlockSpec(memory_space=pltpu.SMEM)] + [block],
        out_specs=[pl.BlockSpec((count, 1, rows, columns), lambda q: (0, q, 0, 0))] * 2,
        out_shape=[jax.ShapeDtypeStruct((count, CHIPS, rows, columns), low)] * 2,
        compiler_params=params(),
        cost_estimate=cost(0, 14 * n * 8 * rows * units // 4),
    )(core.reshape(1), grads)


def unit_unpack(n, blocks):
    _, rows, columns = blocks.shape
    main = (columns - (n + 1) // 2 * LANES) // n
    units = CHIPS * main + CHIPS // 2 * LANES

    def kernel(block_ref, *outs):
        for i in range(n):
            for j in range(CHIPS):
                outs[i][:, j * main : (j + 1) * main] = block_ref[j, :, i * main : (i + 1) * main].astype(wide)
            tile = n * main + i // 2 * LANES
            upper = i % 2 == 1
            for j in range(0, CHIPS, 2):
                at = CHIPS * main + j // 2 * LANES
                outs[i][:, at : at + LANES] = half_tiles(
                    block_ref[j, :, tile : tile + LANES], block_ref[j + 1, :, tile : tile + LANES], upper, upper
                ).astype(wide)

    return pl.pallas_call(
        kernel,
        out_shape=[jax.ShapeDtypeStruct((rows, units), wide)] * n,
        compiler_params=params(),
    )(blocks)


def per_device(
    block_in, out_grad, global_pos,
    w_query, w_key, w_value, w_out, w_up, w_gate, w_down,
    qk_gain, up_gain, gate_gain, att_rate, mlp_rate,
):
    count = lax.axis_size("tensor")
    plane = lax.axis_size(DP)
    micro_count, _, local_rows, model_width = block_in.shape
    assert micro_count == 2 and count == 4
    seq_len = local_rows * count
    head_width = w_query.shape[1]
    core_heads = head_width * 2
    unit_width = w_up.shape[1]
    plane_unit = unit_width // CHIPS
    main = plane_unit // LANES * LANES
    rest = plane_unit - main
    me = lax.axis_index(DP)
    z = lax.axis_index("tensor")
    core = me & 1
    chip = (me >> 1) & 3
    early = z < 2

    def across(value, pairs):
        return lax.ppermute(
            value, ALL, [(a * count + b, c * count + d) for (a, b), (c, d) in pairs]
        )

    def home(far):
        return [
            ((p, t), ((p & ~1) | (t & 1), ((t & 2) ^ (2 if far else 0)) | (p & 1)))
            for p in range(plane)
            for t in range(count)
        ]

    def seq_near(value):
        return across(lax.dynamic_index_in_dim(value, z >> 1, 0, keepdims=False), home(False))

    def seq_far(value):
        return across(lax.dynamic_index_in_dim(value, 1 - (z >> 1), 0, keepdims=False), home(True))

    def seq_join(near, far):
        return pick(early, jnp.concatenate([near, far]), jnp.concatenate([far, near]))

    def from_sequence(value):
        first, second = value[:local_rows], value[local_rows:]
        near = across(pick(early, first, second), [(b, a) for a, b in home(False)])
        far = across(pick(early, second, first), [(b, a) for a, b in home(True)])
        return near, far

    def by_micro(near, far):
        return pick(early, jnp.stack([near, far]), jnp.stack([far, near])).astype(wide)

    def both_cores(value):
        value = value.reshape(2, local_rows, model_width)
        return place([value, swap(value, 1)], [core, core + 2, 1 - core, 3 - core]).reshape(
            seq_len, model_width
        )

    def core_scatter(partial):
        split = partial.reshape(2, 2, local_rows, model_width)
        got = swap(lax.dynamic_index_in_dim(split, 1 - core, 1, keepdims=False), 1)
        mine = lax.dynamic_index_in_dim(split, core, 1, keepdims=False)
        return (mine.astype(wide) + got.astype(wide)).reshape(2 * local_rows, model_width)

    def head_pairs(other_core, second):
        return [
            ((p ^ other_core, (t + 2 * (p & 1) + second) % count), (p, t))
            for p in range(plane)
            for t in range(count)
        ]

    def paired(a, b):
        return jnp.concatenate(
            [a[..., :head_width], b[..., :head_width], a[..., head_width:], b[..., head_width:]], axis=-1
        )

    def attn_fetch(first, second):
        packed = outer_gather(jnp.concatenate([first, second], axis=1))
        groups = [[across(packed, head_pairs(side, which)) for which in range(2)] for side in range(2)]
        return jnp.stack([paired(*pair) for pair in groups])

    def attn_pair(first, second, extra):
        packed = jnp.concatenate([outer_gather(jnp.concatenate([first, second], axis=1)), extra])
        return jnp.stack([packed, swap(packed, 1)])

    def attn_fetch_packed(packed, rows):
        groups = [across(packed, head_pairs(0, which)) for which in range(2)]
        sides = [
            paired(*(group[:, :rows, at : at + head_width] for group in groups))
            for at in range(0, packed.shape[2], head_width)
        ]
        return *sides, [group[0, rows:] for group in groups]

    def attn_first(sides):
        return sides, swap(sides, 2), swap(sides, 4)

    def attn_second(first):
        sides, along_x, along_y = first
        return sides, along_x, along_y, swap(along_y[0], 2), swap(along_x[1], 4)

    def attn_lay(blocks):
        return full_rows(place(blocks, [2 * (chip ^ (i // 2)) + (core ^ (i % 2)) for i in range(8)]))

    def attn_pack(packed, extra):
        grad = plane_rows(packed).reshape(CHIPS, 2, -1, packed.shape[1])
        return spread_pack(grad, extra, chip)

    def attn_send(messages):
        first, second, keep = messages
        return swap(first, 2), swap(second, 4), keep

    def attn_turn(messages):
        to_y, to_x = messages
        return swap(to_y, 4), swap(to_x, 2)

    def attn_scatter(sent, turned):
        pieces = spread_finish(*sent, *turned, head_width, core)
        return [
            across(pieces[2 * side + which], [(b, a) for a, b in head_pairs(side, which)])
            for side in range(2)
            for which in range(2)
        ]

    def attn_join(got, extra_rows):
        got = [piece.astype(wide) for piece in got]
        rows = got[0].shape[0] - extra_rows
        small = jnp.stack([piece[rows:] for piece in got])
        extra = jnp.zeros(small.shape[1:], wide)
        for t in range(count):
            back = (z - t) % count
            index = 2 * ((back >> 1) ^ core) + (back & 1)
            extra = extra + lax.dynamic_index_in_dim(small, index, 0, keepdims=False)
        return attn_own(sum(piece[:rows] for piece in got), extra)

    def attn_own(grads, extra):
        grads = outer_scatter(grads)
        bit = 8
        while bit < plane:
            extra = extra + swap(extra, bit)
            bit *= 2
        return grads[:, :head_width], grads[:, head_width:], extra

    def unit_join(n, mine):
        return [full_rows(w) for w in unit_lay(n, mine, swap(mine, 1), core)]

    def unit_collect(grads):
        keep, send = unit_unlay([plane_rows(g) for g in grads], core)
        return add_low(keep, swap(send, 1))

    def unit_return(n, total):
        return [outer_scatter(g) for g in unit_unpack(n, lax.all_to_all(total, "chip", 0, 0, tiled=True))]

    tie = lax.optimization_barrier

    def halved(value):
        upper_part = lax.reduce_precision(value, 8, 7)
        return jnp.stack([upper_part, value - upper_part]).astype(low)

    qk_sides = attn_fetch(w_query, w_key)
    unit_blocks = unit_pack([[outer_gather(w_up), outer_gather(w_gate)]])
    mains = lax.dynamic_slice_in_dim(jnp.stack([up_gain, gate_gain]), chip * main, main, 1)
    rests = lax.dynamic_slice_in_dim(jnp.stack([up_gain, gate_gain]), CHIPS * main + chip * rest, rest, 1)
    unit_gains = halved(jnp.concatenate([mains, rests], axis=1).reshape(-1))
    gain_rows = jnp.concatenate(
        [unit_gains, halved(qk_gain).reshape(1, -1), jnp.zeros((13, 2 * head_width), low)]
    )
    vo_packed = attn_pair(w_value, w_out, gain_rows)
    places_here = global_pos[:, 0]
    places_there = swap(places_here, 1)
    qk_sides, vo_packed, places_there, unit_blocks, block_in = tie(
        (qk_sides, vo_packed, places_there, unit_blocks, block_in)
    )
    qk_first = attn_first(qk_sides)
    value_sides, out_sides, gain_groups = attn_fetch_packed(vo_packed, qk_sides.shape[1])
    near = seq_near(block_in[:, 0])
    qk_first, value_sides, out_sides, gain_groups, near, block_in, unit_blocks = tie(
        (qk_first, value_sides, out_sides, gain_groups, near, block_in, unit_blocks)
    )
    ug_laid = lax.all_to_all(unit_blocks, "chip", 0, 0, tiled=True)
    lower, upper_rows = block_in[:, 0, : local_rows // 2], block_in[:, 0, local_rows // 2 :]
    far_first, upper_rows = tie((seq_far(lower), upper_rows))
    far = jnp.concatenate([far_first, seq_far(upper_rows)])
    qk_w = attn_lay(attn_second(qk_first))
    value_w = attn_lay(attn_second(attn_first(value_sides)))
    qk_w, value_w, out_sides, gain_groups, far, near, ug_laid, w_down = tie(
        (qk_w, value_w, out_sides, gain_groups, far, near, ug_laid, w_down)
    )
    down_laid = lax.all_to_all(unit_pack([[outer_gather(w_down)]]), "chip", 0, 0, tiled=True)
    gain_here = jnp.stack(gain_groups)[:, :2].astype(wide).sum(axis=1)
    gain_there = swap(gain_here, 1)
    out_across = [out_sides] + [swap(out_sides, 2 * k) for k in range(1, CHIPS)]
    tokens = seq_join(near, far)
    sequence = both_cores(tokens)
    ug_shifted = lax.all_gather(ug_laid, "tensor")
    unit_gains = pick(
        core == 0, jnp.concatenate([gain_here, gain_there]), jnp.concatenate([gain_there, gain_here])
    )
    unit_gains = lax.dynamic_slice_in_dim(jnp.concatenate([unit_gains, unit_gains]), count - z, count, 0)
    unit_gains = unit_gains.reshape(count, 2, plane_unit).transpose(1, 0, 2)
    scales = jnp.concatenate(
        [unit_gains[..., :main].reshape(2, -1), unit_gains[..., main:].reshape(2, -1)], axis=1
    )
    head_gain = jnp.stack(gain_groups)[:, 2].astype(wide).reshape(2, 2, head_width).sum(axis=1)
    head_gain = head_gain.reshape(core_heads)
    places = lax.dynamic_index_in_dim(
        pick((z & 1) == core, places_here, places_there), z >> 1, 0, keepdims=False
    )
    flags = jnp.any(places[:, None] == jnp.arange(seq_len, dtype=jnp.int32)[None, :], axis=0).astype(wide)
    flag_row, flag_col = flags[None], flags[:, None]

    heads, raw = project_heads(sequence, qk_w, jnp.concatenate([head_gain, head_gain]))
    value_rows = product(sequence, value_w)
    mixed, lse = attend_forward(heads, value_rows, flag_row, flag_col)
    mixed, out_across, down_laid = tie((mixed, out_across, down_laid))
    down_shifted = lax.all_gather(down_laid, "tensor")
    out_w = attn_lay(out_across)
    partial = sum_back([(mixed, 0, core_heads)], [(out_w, 0, core_heads)])
    partial = partial.reshape(2, 2, local_rows, model_width)
    got = swap(lax.dynamic_index_in_dim(partial, 1 - core, 1, keepdims=False), 1)
    hidden, hidden_low, att_branch = settle_attention(partial, got, tokens, att_rate, core)

    own_rows = 2 * local_rows
    all_rows = CHIPS * own_rows
    hidden_low, ug_shifted = tie((hidden_low, ug_shifted))
    first = plane_first(hidden_low)
    up_w, gate_w = unit_join(2, ug_shifted)
    earlier, saved, acts = (), [], []

    def forward(blocks, at):
        nonlocal earlier
        *earlier, act, up_raw, gate_raw = mlp_forward(blocks, up_w, gate_w, scales, all_rows, at, earlier)
        saved.append((up_raw, gate_raw))
        return act

    def back(act):
        return sum_back([(act, 0, act.shape[1])], [(down_w, 0, act.shape[1])])

    def by_chip(own, both, diagonal):
        return [own, both[:own_rows], both[own_rows:], diagonal]

    act_own = forward([hidden_low], 2)
    out_grad_low = out_grad[:, 0].astype(low)
    first, act_own, out_grad_low = tie((first, act_own, out_grad_low))
    _, along_x, along_y, *diagonal = plane_second(first)
    act_both = forward([along_x, along_y], 0)
    diagonal, act_both, down_shifted = tie((diagonal, act_both, down_shifted))
    (down_w,) = unit_join(1, down_shifted)
    act_diagonal = forward(diagonal, 3)
    mid, activated = earlier
    parts = [back(act) for act in (act_own, act_both, act_diagonal)]
    parts, out_grad_low = tie((parts, out_grad_low))
    sent, _ = scatter_first(by_chip(*parts))
    cotangent = seq_near(out_grad_low), seq_far(out_grad_low)
    sent, cotangent = tie((sent, cotangent))
    block_rows, direct, branch_grad, mlp_rate_term = settle_units(
        scatter_last(sent), hidden, *cotangent, early, mlp_rate
    )

    first = plane_first(branch_grad)
    returned = from_sequence(block_rows)
    earlier, unit_terms = (), []

    def backward(blocks, at, raws):
        nonlocal earlier
        *earlier, part, unit_term = mlp_backward(
            blocks, up_w, gate_w, down_w, scales, *raws, all_rows, at, earlier
        )
        unit_terms.append(unit_term[:2])
        return part

    part_own = backward([branch_grad], 2, saved[0])
    first, part_own = tie((first, part_own))
    _, along_x, along_y, *diagonal = plane_second(first)
    part_both = backward([along_x, along_y], 0, saved[1])
    diagonal, part_both, returned = tie((diagonal, part_both, returned))
    part_diagonal = backward(diagonal, 3, saved[2])
    branch, up_low, gate_low = earlier
    sent, (branch, mid) = scatter_first(by_chip(part_own, part_both, part_diagonal), (branch, mid))
    down_blocks = unit_unlay(plane_rows(rows_product([(branch, [activated])], 2 * LANES)), 1, core)
    ug_grad = rows_product([(mid, [up_low, gate_low])], 2 * LANES)
    small = jnp.concatenate([sum(unit_terms), mlp_rate_term[:1]])
    small = small + swap(small, 1)
    sent, down_blocks, ug_grad, small = tie((sent, down_blocks, ug_grad, small))
    arrived = scatter_last(sent)
    down_blocks = add_low(down_blocks[0], swap(down_blocks[1], 1))
    ug_blocks = unit_unlay(plane_rows(ug_grad), 2, core)
    def rate_rows_of(term):
        rows = jnp.broadcast_to(term.reshape(2, 2, 1, head_width), (2, 2, 2, head_width))
        return jnp.where(own_chip[..., None], rows.reshape(1, 2, 4 * head_width), 0.0).reshape(2 * CHIPS, -1)

    own_chip = jnp.arange(CHIPS)[:, None] == chip
    empty_rows = jnp.zeros((EXTRA - 3 * CHIPS, 4 * head_width), wide)
    unit_rows = jnp.concatenate(
        [small[:2, : count * main].reshape(2, count, main), small[:2, count * main :].reshape(2, count, rest)],
        axis=2,
    )
    unit_rows = lax.dynamic_slice_in_dim(
        jnp.concatenate([unit_rows, unit_rows], axis=1), z + 2 * core, 2, 1
    ).reshape(1, 4 * plane_unit)
    vo_extra = jnp.concatenate([jnp.where(own_chip, unit_rows, 0.0), rate_rows_of(small[2:]), empty_rows])
    vo_extra = vo_extra.astype(low)
    arrived, ug_blocks, down_blocks, vo_extra = tie((arrived, ug_blocks, down_blocks, vo_extra))
    down_back = lax.psum_scatter(down_blocks, "tensor", scatter_dimension=0)
    ug_there = swap(ug_blocks[1], 1)
    input_direct, att_grad, att_rate_term = settle_attention_back(
        arrived, direct, hidden, tokens, att_branch, att_rate
    )
    att_low = both_cores(att_grad)
    ug_blocks = add_low(ug_blocks[0], ug_there)
    att_low, ug_blocks = tie((att_low, ug_blocks))
    ug_back = lax.psum_scatter(ug_blocks, "tensor", scatter_dimension=0)
    mixed_grad = product(att_low, out_w)
    heads_low, vraw_low, head_terms = attend_backward(
        heads, raw, value_rows, mixed, mixed_grad, lse, head_gain, flag_row, flag_col
    )
    block_out = by_micro(*returned)

    heads_low, vraw_low, down_back = tie((heads_low, vraw_low, down_back))
    vo_grad = rows_product([(sequence, [vraw_low]), (att_low, [mixed])], core_heads)
    vo_messages, vraw_low = tie((attn_pack(vo_grad, vo_extra), vraw_low))
    vo_sent = attn_send(vo_messages)
    in_part = sum_back(
        [(heads_low, 0, 2 * core_heads), (vraw_low, 0, core_heads)],
        [(qk_w, 0, 2 * core_heads), (value_w, 0, core_heads)],
    )
    (grad_down,) = unit_return(1, down_back)
    vo_sent, heads_low, in_part, ug_back, block_out, grad_down = tie(
        (vo_sent, heads_low, in_part, ug_back, block_out, grad_down)
    )
    att_term = att_rate_term[:1] + swap(att_rate_term[:1], 1)
    vo_messages, heads_low, in_part, att_term = tie((spread_turn(*vo_sent), heads_low, in_part, att_term))
    qk_extra = jnp.concatenate(
        [
            jnp.where(own_chip, head_terms[:2].reshape(1, 4 * head_width), 0.0),
            rate_rows_of(att_term),
            empty_rows,
        ]
    )
    vo_turned = attn_turn(vo_messages)
    in_rows = (input_direct + core_scatter(in_part)).astype(low)
    qk_messages = attn_pack(rows_product([(sequence, [heads_low])], 2 * LANES), qk_extra)
    vo_turned, in_rows, qk_messages = tie((vo_turned, in_rows, qk_messages))
    qk_sent = attn_send(qk_messages)
    returned_in = from_sequence(in_rows)
    qk_sent, vo_turned = tie((qk_sent, vo_turned))
    vo_got = attn_scatter(vo_sent, vo_turned)
    qk_turned = attn_turn(spread_turn(*qk_sent))
    qk_turned, returned_in, ug_back = tie((qk_turned, returned_in, ug_back))
    qk_got = attn_scatter(qk_sent, qk_turned)
    grad_up, grad_gate = unit_return(2, ug_back)
    in_grad = by_micro(*returned_in)
    vo_got, qk_got = tie((vo_got, qk_got))
    grad_value, grad_out, vo_small = attn_join(vo_got, EXTRA)
    grad_query, grad_key, qk_small = attn_join(qk_got, EXTRA)

    units = vo_small[:CHIPS].reshape(CHIPS, 2, plane_unit).transpose(1, 0, 2)
    units = jnp.concatenate([units[..., :main].reshape(2, -1), units[..., main:].reshape(2, -1)], axis=1)
    mlp_total, att_total = (
        jnp.sum(member[CHIPS : 3 * CHIPS].reshape(CHIPS, model_width), axis=0) for member in (vo_small, qk_small)
    )
    head_sums = jnp.sum(qk_small[:CHIPS], axis=0)
    grad_qk_gain = head_sums[:head_width] + head_sums[head_width:]
    return (
        block_out[:, None], in_grad[:, None],
        grad_query, grad_key, grad_value, grad_out, grad_up, grad_gate, grad_down,
        grad_qk_gain, units[0], units[1], att_total, mlp_total,
    )


def solution(mesh):
    shape = dict(mesh.shape)
    plane, count = shape["dp"], shape["tensor"]
    split = Mesh(mesh.devices.reshape(plane // 8, CHIPS, 2, count), ALL)
    tokens = P(None, DP, "tensor", None)
    matrix = P(DP, "tensor")
    in_specs = (tokens, tokens, P(None, DP, None)) + (matrix,) * 7 + (P("tensor"),) * 3 + (P(), P())
    out_specs = (tokens, tokens) + (matrix,) * 7 + (P("tensor"),) * 3 + (P(), P())
    return jax.shard_map(
        per_device, mesh=split, in_specs=in_specs, out_specs=out_specs, check_vma=False
    )
```
